32 devices in a mesh: dp: 4 (over y, x), seq: 4 (over z), col: 2 (over core).
Axes of the slice: x: 2, y: 2, z: 4, core: 2. Of those that a mesh axis runs over, the one named last changes fastest.
Arguments:
- latents: bfloat16 [4, 16, 32, 10240], P('dp', 'seq', None, 'col'), may hold values from -62 to 62
- spatial_kernel: bfloat16 [3, 3, 320, 320], replicated, may hold values from -0.109375 to 0.109375
- temporal_kernel: bfloat16 [3, 320, 320], replicated, may hold values from -0.1875 to 0.1875
- cotangent: bfloat16 [4, 16, 32, 10240], P('dp', 'seq', None, 'col'), may hold values from -6 to 6
Outputs:
- grad_latents: float32 [4, 16, 32, 10240], P('dp', 'seq', None, 'col')
- grad_spatial: float32 [3, 3, 320, 320], replicated
- grad_temporal: float32 [3, 320, 320], replicated
The draws below stay inside these ranges and needn't reach their ends.
All inputs are finite; a program needn't handle non-finite values.
Results may differ from the reference program's by a relative error of at most 0.0049.
Values may be sent and summed in bfloat16 or wider, within the bound.
No kernel may reach another device: no remote copies, remote signals or barrier semaphores. Data moves between devices by JAX's collectives and lax.ppermute only.
A program may use at most 128 MiB of HBM per device.

```python
import math
from functools import partial
import jax
import jax.numpy as jnp
from jax import lax

C = 320
GROUPS = 32
H = 32
W = 32
CLIPS = 4
FRAMES = 16


def draw_latents(key, part):
    key = jax.random.fold_in(key, 7)
    subkeys = jax.random.split(key, 4)
    full_shape = (CLIPS, FRAMES, H, W, C)
    channel_scale = jnp.exp(jax.random.uniform(subkeys[0], (CLIPS, 1, 1, 1, C), jnp.float32, jnp.log(0.3), jnp.log(3.0)))
    frame_scale = (3.0 ** (jnp.arange(FRAMES, dtype=jnp.float32) / (FRAMES - 1) - 0.5)).reshape(1, FRAMES, 1, 1, 1)
    column_scale = (9.0 ** (jnp.arange(W, dtype=jnp.float32) / (W - 1) - 0.5)).reshape(1, 1, 1, W, 1)
    rough_scale = jnp.exp(jax.random.uniform(subkeys[1], (CLIPS, FRAMES, H, W, 1), jnp.float32, jnp.log(0.8), jnp.log(1.25)))
    offset = jax.random.uniform(subkeys[2], (CLIPS, 1, 1, 1, C), jnp.float32, -1.0, 1.0)
    noise_part = jnp.clip(jax.random.normal(subkeys[3], full_shape, jnp.float32), -3.0, 3.0)
    drawn = channel_scale * (frame_scale * column_scale * rough_scale * noise_part + offset)
    return drawn.reshape(CLIPS, FRAMES, H, W * C).astype(jnp.bfloat16)


def level_of(key, dims, cuts, low, high):
    def one(position, shards_of):
        heights = jax.random.uniform(jax.random.fold_in(jax.random.fold_in(key, 6), position), (shards_of,), jnp.float32, low / len(cuts), high / len(cuts))
        return jnp.repeat(jnp.exp(heights), dims[position] // shards_of).reshape((-1,) + (1,) * (len(dims) - position - 1))

    level = one(*cuts[0])
    for cut in cuts[1:]:
        level = level * one(*cut)
    return level


def gaussian(own_key, shape, deviation, reach, cuts=(), kind=jnp.bfloat16):
    loudness = level_of(own_key, shape, cuts, -0.22, 0.18) if cuts else 1.0
    values = jax.random.normal(own_key, shape, jnp.float32) * deviation * loudness
    return jnp.minimum(jnp.maximum(values, -reach), reach).astype(kind)


def setup_inputs(seed: int = 0) -> dict:
    splits = jax.random.split(jax.random.key(seed), 5)
    latents = draw_latents(jax.random.fold_in(splits[4], 71), 0)
    spatial_kernel = gaussian(splits[1], (3, 3, C, C), (9 * C) ** -0.5, 0.109375)
    temporal_kernel = gaussian(splits[2], (3, C, C), (3 * C) ** -0.5, 0.1875)
    cotangent = gaussian(splits[3], (CLIPS, FRAMES, H, W * C), 1.0, 6.0, ((0, 4), (1, 4), (3, 2)))
    return {"latents": latents, "spatial_kernel": spatial_kernel, "temporal_kernel": temporal_kernel, "cotangent": cotangent}


epsilon = 1e-05

def silu_slope(values):
    sigmoid = jax.nn.sigmoid(values)
    return sigmoid * (1.0 + values * (1.0 - sigmoid))

def widen(values):
    return lax.optimization_barrier(values).astype(jnp.float32)

def group_means(plain, squared, entries):
    outputs = []
    for values in (plain, squared):
        totals = lax.optimization_barrier(jnp.sum(values, axis=-2))
        grouped = totals.reshape(totals.shape[:-1] + (GROUPS, C // GROUPS))
        means = lax.optimization_barrier(jnp.sum(grouped, axis=-1)) / entries
        outputs.append(jnp.repeat(means, C // GROUPS, axis=-1)[..., None, :])
    return (outputs[0], outputs[1])

def spatial_conv(values, kernel):
    return lax.conv_general_dilated(widen(values), kernel.astype(jnp.float32), (1, 1), ((1, 1), (1, 1)), dimension_numbers=('NHWC', 'HWIO', 'NHWC'), precision=lax.Precision.HIGHEST, preferred_element_type=jnp.float32)

def matmul(left, right):
    return jnp.dot(left, right, precision=lax.Precision.HIGHEST, preferred_element_type=jnp.float32)

def one_clip(clip_pair, spatial_kernel, temporal_kernel):
    clip_latents, clip_cotangent = clip_pair
    frame_entries = H * W * (C // GROUPS)
    clip_entries = FRAMES * H * W * (C // GROUPS)
    latent_view = clip_latents.astype(jnp.float32).reshape(FRAMES, H * W, C)
    frame_mean, frame_square = group_means(latent_view, latent_view * latent_view, frame_entries)
    frame_rate = lax.rsqrt(frame_square - frame_mean * frame_mean + epsilon)
    normed = (latent_view - frame_mean) * frame_rate
    activated = jax.nn.silu(normed).astype(jnp.bfloat16).reshape(FRAMES, H, W, C)
    spatial = spatial_conv(activated, spatial_kernel)
    hidden = (latent_view.reshape(FRAMES, H, W, C) + spatial).astype(jnp.bfloat16)
    hidden_view = widen(hidden).reshape(1, FRAMES * H * W, C)
    clip_mean, clip_square = group_means(hidden_view, hidden_view * hidden_view, clip_entries)
    clip_rate = lax.rsqrt(clip_square - clip_mean * clip_mean + epsilon)
    tnormed = (hidden_view - clip_mean) * clip_rate
    tactivated = widen(jax.nn.silu(tnormed).astype(jnp.bfloat16)).reshape(FRAMES, H * W, C)
    padded_act = jnp.pad(tactivated, ((1, 1), (0, 0), (0, 0)))
    cot_view = clip_cotangent.astype(jnp.float32).reshape(FRAMES, H * W, C)
    padded_cot = jnp.pad(cot_view, ((1, 1), (0, 0), (0, 0)))
    cot_flat = cot_view.reshape(-1, C)
    temporal_taps = []
    act_grad = jnp.zeros((FRAMES * H * W, C), jnp.float32)
    for frame_tap in range(3):
        shifted = padded_act[frame_tap:frame_tap + FRAMES].reshape(-1, C)
        temporal_taps.append(matmul(shifted.T, cot_flat))
        shifted_grad = padded_cot[2 - frame_tap:2 - frame_tap + FRAMES].reshape(-1, C)
        act_grad = act_grad + matmul(shifted_grad, temporal_kernel[frame_tap].astype(jnp.float32).T)
    tnorm_grad = act_grad.reshape(1, -1, C) * silu_slope(tnormed)
    grad_mean, cross_mean = group_means(tnorm_grad, tnorm_grad * tnormed, clip_entries)
    dtemporal = widen((clip_rate * (tnorm_grad - grad_mean - tnormed * cross_mean)).astype(jnp.bfloat16))
    dhidden = cot_view.reshape(FRAMES, H, W, C) + dtemporal.reshape(FRAMES, H, W, C)
    dspatial = dhidden.astype(jnp.bfloat16)
    flipped = jnp.flip(spatial_kernel, (0, 1)).transpose(0, 1, 3, 2)
    dactivated = spatial_conv(dspatial, flipped)
    act_padded = jnp.pad(widen(activated), ((0, 0), (1, 1), (1, 1), (0, 0)))
    grad_flat = widen(dspatial).reshape(-1, C)
    spatial_rows = []
    for row_tap in range(3):
        taps_row = []
        for col_tap in range(3):
            window = act_padded[:, row_tap:row_tap + H, col_tap:col_tap + W, :].reshape(-1, C)
            taps_row.append(matmul(window.T, grad_flat))
        spatial_rows.append(jnp.stack(taps_row))
    dnormed = dactivated.reshape(FRAMES, H * W, C) * silu_slope(normed)
    grad_mean, cross_mean = group_means(dnormed, dnormed * normed, frame_entries)
    grad_latents = dhidden.reshape(FRAMES, H * W, C) + frame_rate * (dnormed - grad_mean - normed * cross_mean)
    return (grad_latents.reshape(FRAMES, H, W * C), jnp.stack(spatial_rows), jnp.stack(temporal_taps))

def reference(latents, spatial_kernel, temporal_kernel, cotangent):
    clip_step = partial(one_clip, spatial_kernel=spatial_kernel, temporal_kernel=temporal_kernel)
    grad_latents, spatial_terms, temporal_terms = lax.map(clip_step, (latents, cotangent))
    grad_scale = 1.0 / math.sqrt(CLIPS * FRAMES * H * W)
    return (grad_latents, lax.optimization_barrier(jnp.sum(spatial_terms, axis=0)) * grad_scale, lax.optimization_barrier(jnp.sum(temporal_terms, axis=0)) * grad_scale)
```

```python
import functools
import math

import jax
import jax.numpy as jnp
from jax import lax
from jax.experimental import pallas as pl
from jax.experimental.pallas import tpu as pltpu
from jax.sharding import PartitionSpec as P

GROUPS = 32
EPSILON = 1e-05
F32 = jnp.float32
BF16 = jnp.bfloat16
VMEM_LIMIT = 56 * 1024 * 1024


def whole(count):
    return [pl.BlockSpec(memory_space=pltpu.VMEM)] * count


def call(body, outs, scratch=(), flops=0, moved=0):
    return pl.pallas_call(
        body,
        out_shape=outs,
        out_specs=jax.tree.map(lambda _: pl.BlockSpec(memory_space=pltpu.VMEM), outs),
        scratch_shapes=list(scratch),
        compiler_params=pltpu.CompilerParams(vmem_limit_bytes=VMEM_LIMIT),
        cost_estimate=pl.CostEstimate(flops=flops, bytes_accessed=moved, transcendentals=0),
    )


def struct(shape, kind):
    return jax.ShapeDtypeStruct(shape, kind)


class Sizes:
    def __init__(self, frames, rows, columns, channels):
        self.frames = frames
        self.rows = rows
        self.columns = columns
        self.channels = channels
        self.pixels = frames * rows
        self.width = columns * channels
        self.pair = 2 * channels
        self.pairs = columns // 2
        self.edge = -(-channels // 128) * 128
        self.slack = self.edge - channels
        self.window = 3 * channels + self.slack
        self.padded = self.width + 2 * self.edge


def group_totals(sums, sizes):
    size = sizes.channels // GROUPS

    def member(shape, lane_dim):
        lane = lax.broadcasted_iota(jnp.int32, shape, lane_dim)
        group = lax.broadcasted_iota(jnp.int32, shape, 1 - lane_dim)
        channel = jnp.where(lane >= sizes.channels, lane - sizes.channels, lane)
        return ((channel >= group * size) & (channel < group * size + size)).astype(F32)

    high = lax.Precision.HIGHEST
    by_group = jnp.dot(sums, member((sizes.pair, 128), 0), precision=high, preferred_element_type=F32)
    return jnp.dot(by_group, member((128, sizes.pair), 1), precision=high, preferred_element_type=F32)


def moments(sums, half, entries, sizes):
    totals = group_totals(sums, sizes) * (1.0 / entries)
    mean = totals[0:half]
    rate = lax.rsqrt(totals[half : 2 * half] - mean * mean + EPSILON)
    return mean, rate


def fold(values):
    return jnp.sum(values.reshape(values.shape[0] // 8, 8, values.shape[1]), axis=0)


def pair_lanes(p, sizes):
    return pl.ds(pl.multiple_of(p * sizes.pair, 128), sizes.pair)


def join(even, odd, sizes):
    cut = sizes.edge - 128
    middle = even[:, cut:] + odd[:, :128]
    return jnp.concatenate([even[:, :cut], middle, odd[:, 128:]], axis=1)


def latent_sums_body(sizes, x_ref, sums_ref, edge_ref):
    def frame(f):
        rows = pl.ds(f * sizes.rows, sizes.rows)

        def step(p, carry):
            plain, square = carry
            v = x_ref[rows, pair_lanes(p, sizes)].astype(F32)
            return plain + fold(v), square + fold(v * v)

        zero = jnp.zeros((8, sizes.pair), F32)
        plain, square = lax.fori_loop(0, sizes.pairs, step, (zero, zero))
        return jnp.sum(plain, axis=0, keepdims=True), jnp.sum(square, axis=0, keepdims=True)

    found = [frame(f) for f in range(sizes.frames)]
    for f, (plain, square) in enumerate(found):
        sums_ref[f : f + 1, :] = plain
        sums_ref[sizes.frames + f : sizes.frames + f + 1, :] = square
    store_edge(sizes, x_ref, edge_ref)


def store_edge(sizes, source, target, at=0):
    left = lax.axis_index("col") == 0
    rows = pl.ds(at, sizes.pixels)

    @pl.when(left)
    def _():
        target[rows, :] = source[:, sizes.width - sizes.edge : sizes.width].astype(target.dtype)

    @pl.when(jnp.logical_not(left))
    def _():
        target[rows, :] = source[:, 0 : sizes.edge].astype(target.dtype)


def row_shifts(values, sizes):
    row = lax.broadcasted_iota(jnp.int32, values.shape, 0)
    down = jnp.where(row == 0, 0.0, pltpu.roll(values, 1, 0))
    up = jnp.where(row == sizes.rows - 1, 0.0, pltpu.roll(values, sizes.rows - 1, 0))
    return down, values, up


def put_shifts(values, frame, lanes, target, sizes):
    rows = pl.ds(frame * sizes.rows, sizes.rows)
    for i, moved in enumerate(row_shifts(values, sizes)):
        target[i, rows, lanes] = moved.astype(BF16)


def put_halo(of_frame, target, sizes):
    left = lax.axis_index("col") == 0
    for f in range(sizes.frames):
        rows = pl.ds(f * sizes.rows, sizes.rows)
        before, after = of_frame(rows, f, True), of_frame(rows, f, False)
        put_shifts(jnp.where(left, 0.0, before), f, pl.ds(0, sizes.edge), target, sizes)
        put_shifts(
            jnp.where(left, after, 0.0), f, pl.ds(sizes.edge + sizes.width, sizes.edge), target, sizes
        )


def windows(padded_ref, p, count, odd, sizes):
    found = []
    for q in range(count):
        start = pl.multiple_of((p + q) * sizes.pair, 128) + (sizes.edge if odd else 0)
        lanes = pl.ds(pl.multiple_of(start, 128), sizes.window)
        found.append(jnp.concatenate([padded_ref[i, :, lanes] for i in range(3)], axis=1))
    return jnp.concatenate(found, axis=0)


def silu_parts(v):
    s = 1.0 / (1.0 + jnp.exp(-v))
    return v * s, s


def forward_body(
    sizes, frame_entries, block, x_ref, sums_ref, other_ref, rim_ref, even_ref, odd_ref,
    hidden_ref, act_ref, clip_ref, padded,
):
    mean, rate = moments(sums_ref[...] + other_ref[...], sizes.frames, frame_entries, sizes)

    def rim(rows, f, before):
        lanes = slice(sizes.pair - sizes.edge, sizes.pair) if before else slice(0, sizes.edge)
        v = rim_ref[rows, :].astype(F32)
        return silu_parts((v - mean[f : f + 1, lanes]) * rate[f : f + 1, lanes])[0]

    put_halo(rim, padded, sizes)

    def activate(p, _):
        for f in range(sizes.frames):
            v = x_ref[pl.ds(f * sizes.rows, sizes.rows), pair_lanes(p, sizes)].astype(F32)
            act = silu_parts((v - mean[f : f + 1]) * rate[f : f + 1])[0]
            lanes = pl.ds(pl.multiple_of(p * sizes.pair + sizes.edge, 128), sizes.pair)
            put_shifts(act, f, lanes, padded, sizes)
        return 0

    lax.fori_loop(0, sizes.pairs, activate, 0)
    act_ref[...] = padded[1]

    def step(b, carry):
        plain, square = carry
        p = b * block
        even = jnp.dot(windows(padded, p, block, False, sizes), even_ref[...], preferred_element_type=F32)
        odd = jnp.dot(windows(padded, p, block, True, sizes), odd_ref[...], preferred_element_type=F32)
        for q in range(block):
            rows = slice(q * sizes.pixels, (q + 1) * sizes.pixels)
            spatial = join(even[rows], odd[rows], sizes)
            lanes = pair_lanes(p + q, sizes)
            hidden = (x_ref[:, lanes].astype(F32) + spatial).astype(BF16)
            hidden_ref[:, lanes] = hidden
            wide = hidden.astype(F32)
            plain = plain + fold(wide)
            square = square + fold(wide * wide)
        return plain, square

    zero = jnp.zeros((8, sizes.pair), F32)
    plain, square = lax.fori_loop(0, sizes.pairs // block, step, (zero, zero))
    put_sums(clip_ref, plain, square)


def put_sums(target, plain, square):
    target[...] = jnp.zeros(target.shape, F32)
    target[0:1, :] = jnp.sum(plain, axis=0, keepdims=True)
    target[1:2, :] = jnp.sum(square, axis=0, keepdims=True)


def frame_taps(cot_ref, before_ref, after_ref, lanes, sizes):
    own = cot_ref[:, lanes]
    later = jnp.concatenate([own[sizes.rows :], after_ref[:, lanes]], axis=0)
    earlier = jnp.concatenate([before_ref[:, lanes], own[: sizes.pixels - sizes.rows]], axis=0)
    return later, own, earlier


def temporal_body(
    sizes, clip_entries, block, hidden_ref, cot_ref, before_ref, after_ref, clip_ref, even_ref, odd_ref,
    act_ref, grad_ref, sums_ref, rim_ref, normed,
):
    mean, rate = moments(clip_ref[...], 1, clip_entries, sizes)

    def step(b, carry):
        plain, cross = carry
        p = b * block
        found = []
        for odd, weights in ((False, even_ref), (True, odd_ref)):
            rows = []
            for q in range(block):
                start = (p + q) * sizes.pair + (sizes.pair - sizes.edge if odd else 0)
                lanes = pl.ds(pl.multiple_of(start, 128), sizes.edge)
                rows.append(
                    jnp.concatenate(frame_taps(cot_ref, before_ref, after_ref, lanes, sizes), axis=1)
                )
            found.append(
                lax.dot_general(
                    jnp.concatenate(rows, axis=0), weights[...], (((1,), (1,)), ((), ())),
                    preferred_element_type=F32,
                )
            )
        for q in range(block):
            rows = slice(q * sizes.pixels, (q + 1) * sizes.pixels)
            dact = join(found[0][rows], found[1][rows], sizes)
            lanes = pair_lanes(p + q, sizes)
            tnormed = (hidden_ref[:, lanes].astype(F32) - mean) * rate
            act, s = silu_parts(tnormed)
            act_ref[:, lanes] = act.astype(BF16)
            normed[:, lanes] = tnormed
            grad = dact * (s * (1.0 + tnormed * (1.0 - s)))
            grad_ref[:, lanes] = grad
            plain = plain + fold(grad)
            cross = cross + fold(grad * tnormed)
        return plain, cross

    zero = jnp.zeros((8, sizes.pair), F32)
    plain, cross = lax.fori_loop(0, sizes.pairs // block, step, (zero, zero))
    put_sums(sums_ref, plain, cross)
    for k, source in enumerate((grad_ref, normed, cot_ref)):
        store_edge(sizes, source, rim_ref, k * sizes.pixels)


def temporal_grad_body(sizes, act_ref, cot_ref, before_ref, after_ref, out_ref, total):
    total[...] = jnp.zeros(total.shape, F32)
    channels = sizes.channels
    zeros = jnp.zeros((sizes.pixels, sizes.slack), BF16)

    def step(p, _):
        lanes = pair_lanes(p, sizes)
        act = act_ref[:, lanes]
        act = jnp.concatenate([act[:, :channels], act[:, channels:]], axis=0)
        taps = frame_taps(cot_ref, before_ref, after_ref, lanes, sizes)
        even = jnp.concatenate([jnp.concatenate([t[:, :channels], zeros], axis=1) for t in taps], axis=1)
        odd = jnp.concatenate([jnp.concatenate([t[:, channels:], zeros], axis=1) for t in taps], axis=1)
        total[...] += lax.dot_general(
            act, jnp.concatenate([even, odd], axis=0), (((0,), (0,)), ((), ())),
            preferred_element_type=F32,
        )
        return 0

    lax.fori_loop(0, sizes.pairs, step, 0)
    for i in range(3):
        out_ref[i] = total[:, i * sizes.edge : i * sizes.edge + channels]


def spatial_grad_body(
    sizes, clip_entries, hidden_ref, cot_ref, grad_ref, clip_ref, mean_ref, rim_ref, act_ref,
    dtemp_ref, dspat_ref, out_ref, padded, total,
):
    mean, rate = moments(clip_ref[...], 1, clip_entries, sizes)
    means = group_totals(mean_ref[...], sizes) * (1.0 / clip_entries)
    plain, cross = means[0:1], means[1:2]

    def rim(rows, f, before):
        lanes = slice(sizes.pair - sizes.edge, sizes.pair) if before else slice(0, sizes.edge)
        at = [pl.ds(k * sizes.pixels + f * sizes.rows, sizes.rows) for k in range(3)]
        grad, tnormed, cot = (rim_ref[r, :] for r in at)
        dtemp = rate[:, lanes] * (grad - plain[:, lanes] - tnormed * cross[:, lanes])
        return (cot + dtemp.astype(BF16).astype(F32)).astype(BF16).astype(F32)

    put_halo(rim, padded, sizes)

    def combine(p, _):
        lanes = pair_lanes(p, sizes)
        for f in range(sizes.frames):
            rows = pl.ds(f * sizes.rows, sizes.rows)
            tnormed = (hidden_ref[rows, lanes].astype(F32) - mean) * rate
            dtemp = (rate * (grad_ref[rows, lanes] - plain - tnormed * cross)).astype(BF16)
            dtemp_ref[rows, lanes] = dtemp
            dspat = cot_ref[rows, lanes].astype(F32) + dtemp.astype(F32)
            put_shifts(
                dspat, f, pl.ds(pl.multiple_of(p * sizes.pair + sizes.edge, 128), sizes.pair), padded, sizes
            )
        return 0

    lax.fori_loop(0, sizes.pairs, combine, 0)
    dspat_ref[...] = padded[1]

    channels = sizes.channels
    zeros = jnp.zeros((sizes.pixels, sizes.slack), BF16)
    total[...] = jnp.zeros(total.shape, F32)

    def step(b, _):
        for odd in (False, True):
            left, right = [], []
            for q in range(2):
                p = 2 * b + q
                start = p * sizes.pair + (sizes.edge if odd else 0)
                left.append(act_ref[:, pl.ds(pl.multiple_of(start, 128), sizes.window)])
                both = pl.ds(pl.multiple_of(p * sizes.pair + sizes.edge, 128), sizes.pair)
                taps = []
                for i in range(3):
                    d = padded[2 - i, :, both]
                    d = d[:, channels:] if odd else d[:, :channels]
                    taps.append(jnp.concatenate([d, zeros], axis=1))
                right.append(jnp.concatenate(taps, axis=1))
            part = lax.dot_general(
                jnp.concatenate(left, axis=0), jnp.concatenate(right, axis=0), (((0,), (0,)), ((), ())),
                preferred_element_type=F32,
            )
            total[...] += part[: 3 * channels] if odd else part[sizes.slack :]
        return 0

    lax.fori_loop(0, sizes.pairs // 2, step, 0)
    for i in range(3):
        out_ref[i] = total[:, i * sizes.edge : i * sizes.edge + channels]


def backward_body(
    sizes, frame_entries, block, x_ref, sums_ref, other_ref, dspat_ref, even_ref, odd_ref,
    grad_ref, out_ref, padded, plains,
):
    mean, rate = moments(sums_ref[...] + other_ref[...], sizes.frames, frame_entries, sizes)

    def spread(k, _):
        lanes = pl.ds(pl.multiple_of(k * 128, 128), 128)
        for f in range(sizes.frames):
            rows = pl.ds(f * sizes.rows, sizes.rows)
            put_shifts(dspat_ref[rows, lanes].astype(F32), f, lanes, padded, sizes)
        return 0

    lax.fori_loop(0, sizes.padded // 128, spread, 0)
    plains[...] = jnp.zeros(plains.shape, F32)
    contract = (((1,), (1,)), ((), ()))

    def step(b, _):
        p = b * block
        even = lax.dot_general(
            windows(padded, p, block, False, sizes), even_ref[...], contract, preferred_element_type=F32
        )
        odd = lax.dot_general(
            windows(padded, p, block, True, sizes), odd_ref[...], contract, preferred_element_type=F32
        )
        for q in range(block):
            base = q * sizes.pixels
            for f in range(sizes.frames):
                at = slice(base + f * sizes.rows, base + (f + 1) * sizes.rows)
                dact = join(even[at], odd[at], sizes)
                rows, lanes = pl.ds(f * sizes.rows, sizes.rows), pair_lanes(p + q, sizes)
                normed = (x_ref[rows, lanes].astype(F32) - mean[f : f + 1]) * rate[f : f + 1]
                _, s = silu_parts(normed)
                grad = dact * (s * (1.0 + normed * (1.0 - s)))
                grad_ref[rows, lanes] = grad
                plains[f] += fold(grad)
                plains[sizes.frames + f] += fold(grad * normed)
        return 0

    lax.fori_loop(0, sizes.pairs // block, step, 0)
    for k in range(2 * sizes.frames):
        out_ref[k : k + 1, :] = jnp.sum(plains[k], axis=0, keepdims=True)


def finish_body(
    sizes, frame_entries, x_ref, sums_ref, other_ref, cot_ref, dtemp_ref, grad_ref, mine_ref, theirs_ref, out_ref
):
    mean, rate = moments(sums_ref[...] + other_ref[...], sizes.frames, frame_entries, sizes)
    means = group_totals(mine_ref[...] + theirs_ref[...], sizes) * (1.0 / frame_entries)

    def step(p, _):
        lanes = pair_lanes(p, sizes)
        for f in range(sizes.frames):
            rows = pl.ds(f * sizes.rows, sizes.rows)
            normed = (x_ref[rows, lanes].astype(F32) - mean[f : f + 1]) * rate[f : f + 1]
            dhidden = cot_ref[rows, lanes].astype(F32) + dtemp_ref[rows, lanes].astype(F32)
            plain, cross = means[f : f + 1], means[sizes.frames + f : sizes.frames + f + 1]
            out_ref[rows, lanes] = dhidden + rate[f : f + 1] * (grad_ref[rows, lanes] - plain - normed * cross)
        return 0

    lax.fori_loop(0, sizes.pairs, step, 0)


def swap(values, axis, bit):
    count = lax.axis_size(axis)
    return lax.ppermute(values, axis, [(i, i ^ bit) for i in range(count)])


def sum_over(values, axes):
    for axis in axes:
        bit = 1
        while bit < lax.axis_size(axis):
            values = values + swap(values, axis, bit)
            bit *= 2
    return values


def shards(latents, spatial_kernel, temporal_kernel, cotangent):
    _, frames, rows, width = latents.shape
    channels = spatial_kernel.shape[2]
    sizes = Sizes(frames, rows, width // channels, channels)
    cols, seqs = lax.axis_size("col"), lax.axis_size("seq")
    frame_entries = float(rows * sizes.columns * cols * (channels // GROUPS))
    clip_entries = frame_entries * frames * seqs
    pixels = lax.axis_size("dp") * seqs * cols * sizes.pixels * sizes.columns
    grad_scale = 1.0 / math.sqrt(pixels)

    x = latents.reshape(sizes.pixels, width)
    cot = cotangent.reshape(sizes.pixels, width)
    sum_shape = struct((8, sizes.pair), F32)
    frame_shape = struct((2 * frames, sizes.pair), F32)
    padded_scratch = pltpu.VMEM((3, sizes.pixels, sizes.padded), BF16)
    slack = sizes.slack

    flat = spatial_kernel.reshape(3, 3 * channels, channels)
    fwd_even = jnp.pad(flat, ((0, 0), (slack, 0), (0, slack))).reshape(3 * sizes.window, sizes.edge)
    fwd_odd = jnp.pad(flat, ((0, 0), (0, slack), (slack, 0))).reshape(3 * sizes.window, sizes.edge)
    back = jnp.flip(spatial_kernel, (0, 1)).transpose(2, 0, 1, 3).reshape(channels, 3, 3 * channels)
    bwd_even = jnp.pad(back, ((0, slack), (0, 0), (slack, 0))).reshape(sizes.edge, 3 * sizes.window)
    bwd_odd = jnp.pad(back, ((slack, 0), (0, 0), (0, slack))).reshape(sizes.edge, 3 * sizes.window)
    times = temporal_kernel.transpose(1, 0, 2)
    time_even = jnp.pad(times, ((0, slack), (0, 0), (0, slack))).reshape(sizes.edge, 3 * sizes.edge)
    time_odd = jnp.pad(times, ((slack, 0), (0, 0), (slack, 0))).reshape(sizes.edge, 3 * sizes.edge)

    forth = [(i, i + 1) for i in range(seqs - 1)]
    before = lax.ppermute(cot[sizes.pixels - rows :], "seq", forth)
    after = lax.ppermute(cot[:rows], "seq", [(j, i) for i, j in forth])

    sums, edge = call(
        functools.partial(latent_sums_body, sizes),
        [frame_shape, struct((sizes.pixels, sizes.edge), BF16)],
    )(x)
    other = swap(sums, "col", 1)
    rim = swap(edge, "col", 1)
    hidden, act, clip = call(
        functools.partial(forward_body, sizes, frame_entries, min(4, sizes.pairs)),
        [struct((sizes.pixels, width), BF16), struct((sizes.pixels, sizes.padded), BF16), sum_shape],
        [padded_scratch],
    )(x, sums, other, rim, fwd_even, fwd_odd)
    clip = sum_over(clip, ("col", "seq"))
    tact, tgrad, means, pack = call(
        functools.partial(temporal_body, sizes, clip_entries, min(4, sizes.pairs)),
        [
            struct((sizes.pixels, width), BF16),
            struct((sizes.pixels, width), F32),
            sum_shape,
            struct((3 * sizes.pixels, sizes.edge), F32),
        ],
        [pltpu.VMEM((sizes.pixels, width), F32)],
    )(hidden, cot, before, after, clip, time_even, time_odd)
    means = sum_over(means, ("col", "seq"))
    pack = swap(pack, "col", 1)
    temporal_grad = call(
        functools.partial(temporal_grad_body, sizes),
        struct((3, channels, channels), F32),
        [pltpu.VMEM((channels, 3 * sizes.edge), F32)],
    )(tact, cot, before, after)
    dtemp, dspat, spatial_grad = call(
        functools.partial(spatial_grad_body, sizes, clip_entries),
        [
            struct((sizes.pixels, width), BF16),
            struct((sizes.pixels, sizes.padded), BF16),
            struct((3, 3 * channels, channels), F32),
        ],
        [padded_scratch, pltpu.VMEM((3 * channels, 3 * sizes.edge), F32)],
    )(hidden, cot, tgrad, clip, means, pack, act)
    dnormed, mine = call(
        functools.partial(backward_body, sizes, frame_entries, min(4, sizes.pairs)),
        [struct((sizes.pixels, width), F32), frame_shape],
        [padded_scratch, pltpu.VMEM((2 * frames, 8, sizes.pair), F32)],
    )(x, sums, other, dspat, bwd_even, bwd_odd)
    theirs = swap(mine, "col", 1)
    grad_latents = call(
        functools.partial(finish_body, sizes, frame_entries), struct((sizes.pixels, width), F32)
    )(x, sums, other, cot, dtemp, dnormed, mine, theirs)

    spatial_grad, temporal_grad = lax.psum((spatial_grad, temporal_grad), ("dp", "seq", "col"))
    spatial_grad = spatial_grad.reshape(spatial_kernel.shape)
    return (grad_latents.reshape(latents.shape), spatial_grad * grad_scale, temporal_grad * grad_scale)


def solution(mesh):
    in_specs = (P("dp", "seq", None, "col"), P(), P(), P("dp", "seq", None, "col"))
    out_specs = (P("dp", "seq", None, "col"), P(), P())
    return jax.shard_map(shards, mesh=mesh, in_specs=in_specs, out_specs=out_specs, check_vma=False)
```

```python
import functools
import math

import jax
import jax.numpy as jnp
from jax import lax
from jax.experimental import pallas as pl
from jax.experimental.pallas import tpu as pltpu
from jax.sharding import PartitionSpec as P

GROUPS = 32
EPSILON = 1e-05
F32 = jnp.float32
BF16 = jnp.bfloat16
VMEM_LIMIT = 56 * 1024 * 1024
CONV_COST = 12_000_000_000


def whole(count):
    return [pl.BlockSpec(memory_space=pltpu.VMEM)] * count


def call(body, outs, scratch=(), flops=0, moved=0):
    return pl.pallas_call(
        body,
        out_shape=outs,
        out_specs=jax.tree.map(lambda _: pl.BlockSpec(memory_space=pltpu.VMEM), outs),
        scratch_shapes=list(scratch),
        compiler_params=pltpu.CompilerParams(vmem_limit_bytes=VMEM_LIMIT),
        cost_estimate=pl.CostEstimate(flops=flops, bytes_accessed=moved, transcendentals=0),
    )


def struct(shape, kind):
    return jax.ShapeDtypeStruct(shape, kind)


class Sizes:
    def __init__(self, frames, rows, columns, channels):
        self.frames = frames
        self.rows = rows
        self.columns = columns
        self.channels = channels
        self.pixels = frames * rows
        self.width = columns * channels
        self.pair = 2 * channels
        self.pairs = columns // 2
        self.edge = -(-channels // 128) * 128
        self.slack = self.edge - channels
        self.window = 3 * channels + self.slack
        self.padded = self.width + 2 * self.edge


def group_totals(sums, sizes):
    size = sizes.channels // GROUPS

    def member(shape, lane_dim):
        lane = lax.broadcasted_iota(jnp.int32, shape, lane_dim)
        group = lax.broadcasted_iota(jnp.int32, shape, 1 - lane_dim)
        channel = jnp.where(lane >= sizes.channels, lane - sizes.channels, lane)
        return ((channel >= group * size) & (channel < group * size + size)).astype(F32)

    high = lax.Precision.HIGHEST
    by_group = jnp.dot(sums, member((sizes.pair, 128), 0), precision=high, preferred_element_type=F32)
    return jnp.dot(by_group, member((128, sizes.pair), 1), precision=high, preferred_element_type=F32)


def moments(sums, half, entries, sizes):
    totals = group_totals(sums, sizes) * (1.0 / entries)
    mean = totals[0:half]
    rate = lax.rsqrt(totals[half : 2 * half] - mean * mean + EPSILON)
    return mean, rate


def fold(values):
    return jnp.sum(values.reshape(values.shape[0] // 8, 8, values.shape[1]), axis=0)


def pair_lanes(p, sizes):
    return pl.ds(pl.multiple_of(p * sizes.pair, 128), sizes.pair)


def join(even, odd, sizes):
    cut = sizes.edge - 128
    middle = even[:, cut:] + odd[:, :128]
    return jnp.concatenate([even[:, :cut], middle, odd[:, 128:]], axis=1)


def latent_sums_body(sizes, x_ref, sums_ref, edge_ref):
    def frame(f):
        rows = pl.ds(f * sizes.rows, sizes.rows)

        def step(p, carry):
            plain, square = carry
            v = x_ref[rows, pair_lanes(p, sizes)].astype(F32)
            return plain + fold(v), square + fold(v * v)

        zero = jnp.zeros((8, sizes.pair), F32)
        plain, square = lax.fori_loop(0, sizes.pairs, step, (zero, zero))
        return jnp.sum(plain, axis=0, keepdims=True), jnp.sum(square, axis=0, keepdims=True)

    found = [frame(f) for f in range(sizes.frames)]
    for f, (plain, square) in enumerate(found):
        sums_ref[f : f + 1, :] = plain
        sums_ref[sizes.frames + f : sizes.frames + f + 1, :] = square
    store_edge(sizes, x_ref, edge_ref)


def store_edge(sizes, source, target, at=0):
    left = lax.axis_index("col") == 0
    rows = pl.ds(at, sizes.pixels)

    @pl.when(left)
    def _():
        target[rows, :] = source[:, sizes.width - sizes.edge : sizes.width].astype(target.dtype)

    @pl.when(jnp.logical_not(left))
    def _():
        target[rows, :] = source[:, 0 : sizes.edge].astype(target.dtype)


def row_shifts(values, sizes):
    row = lax.broadcasted_iota(jnp.int32, values.shape, 0)
    down = jnp.where(row == 0, 0.0, pltpu.roll(values, 1, 0))
    up = jnp.where(row == sizes.rows - 1, 0.0, pltpu.roll(values, sizes.rows - 1, 0))
    return down, values, up


def put_shifts(values, frame, lanes, target, sizes):
    rows = pl.ds(frame * sizes.rows, sizes.rows)
    for i, moved in enumerate(row_shifts(values, sizes)):
        target[i, rows, lanes] = moved.astype(BF16)


def put_halo(of_frame, target, sizes):
    left = lax.axis_index("col") == 0
    for f in range(sizes.frames):
        rows = pl.ds(f * sizes.rows, sizes.rows)
        before, after = of_frame(rows, f, True), of_frame(rows, f, False)
        put_shifts(jnp.where(left, 0.0, before), f, pl.ds(0, sizes.edge), target, sizes)
        put_shifts(
            jnp.where(left, after, 0.0), f, pl.ds(sizes.edge + sizes.width, sizes.edge), target, sizes
        )


def forward_weights(kernel_ref, even_ref, odd_ref, sizes):
    channels, slack, window = sizes.channels, sizes.slack, sizes.window
    for weights in (even_ref, odd_ref):
        weights[...] = jnp.zeros(weights.shape, BF16)
    for i in range(3):
        for j in range(3):
            taps = kernel_ref[i, j]
            zeros = jnp.zeros((channels, slack), BF16)
            at = i * window + j * channels
            even_ref[at + slack : at + slack + channels, :] = jnp.concatenate([taps, zeros], axis=1)
            odd_ref[at : at + channels, :] = jnp.concatenate([zeros, taps], axis=1)


def backward_weights(kernel_ref, even_ref, odd_ref, sizes):
    channels, slack, window = sizes.channels, sizes.slack, sizes.window
    for weights in (even_ref, odd_ref):
        weights[...] = jnp.zeros(weights.shape, BF16)
    zeros = jnp.zeros((channels, slack), BF16)
    for i in range(3):
        taps = [kernel_ref[2 - i, 2 - j] for j in range(3)]
        lanes = slice(i * window, (i + 1) * window)
        even_ref[0:channels, lanes] = jnp.concatenate([zeros] + taps, axis=1)
        odd_ref[slack : slack + channels, lanes] = jnp.concatenate(taps + [zeros], axis=1)


def temporal_weights(kernel_ref, even_ref, odd_ref, sizes):
    channels, slack, edge = sizes.channels, sizes.slack, sizes.edge
    for weights in (even_ref, odd_ref):
        weights[...] = jnp.zeros(weights.shape, BF16)
    zeros = jnp.zeros((channels, slack), BF16)
    for i in range(3):
        lanes = slice(i * edge, (i + 1) * edge)
        even_ref[0:channels, lanes] = jnp.concatenate([kernel_ref[i], zeros], axis=1)
        odd_ref[slack : slack + channels, lanes] = jnp.concatenate([zeros, kernel_ref[i]], axis=1)


def windows(padded_ref, p, count, odd, sizes):
    found = []
    for q in range(count):
        start = pl.multiple_of((p + q) * sizes.pair, 128) + (sizes.edge if odd else 0)
        lanes = pl.ds(pl.multiple_of(start, 128), sizes.window)
        found.append(jnp.concatenate([padded_ref[i, :, lanes] for i in range(3)], axis=1))
    return jnp.concatenate(found, axis=0)


def silu_parts(v):
    s = 1.0 / (1.0 + jnp.exp(-v))
    return v * s, s


def forward_body(
    sizes, frame_entries, block, x_ref, sums_ref, other_ref, rim_ref, kernel_ref,
    hidden_ref, act_ref, clip_ref, padded, even_ref, odd_ref,
):
    forward_weights(kernel_ref, even_ref, odd_ref, sizes)
    mean, rate = moments(sums_ref[...] + other_ref[...], sizes.frames, frame_entries, sizes)

    def rim(rows, f, before):
        lanes = slice(sizes.pair - sizes.edge, sizes.pair) if before else slice(0, sizes.edge)
        v = rim_ref[rows, :].astype(F32)
        return silu_parts((v - mean[f : f + 1, lanes]) * rate[f : f + 1, lanes])[0]

    put_halo(rim, padded, sizes)

    def activate(p, _):
        for f in range(sizes.frames):
            v = x_ref[pl.ds(f * sizes.rows, sizes.rows), pair_lanes(p, sizes)].astype(F32)
            act = silu_parts((v - mean[f : f + 1]) * rate[f : f + 1])[0]
            lanes = pl.ds(pl.multiple_of(p * sizes.pair + sizes.edge, 128), sizes.pair)
            put_shifts(act, f, lanes, padded, sizes)
        return 0

    lax.fori_loop(0, sizes.pairs, activate, 0)
    act_ref[...] = padded[1]

    def step(b, carry):
        plain, square = carry
        p = b * block
        even = jnp.dot(windows(padded, p, block, False, sizes), even_ref[...], preferred_element_type=F32)
        odd = jnp.dot(windows(padded, p, block, True, sizes), odd_ref[...], preferred_element_type=F32)
        for q in range(block):
            rows = slice(q * sizes.pixels, (q + 1) * sizes.pixels)
            spatial = join(even[rows], odd[rows], sizes)
            lanes = pair_lanes(p + q, sizes)
            hidden = (x_ref[:, lanes].astype(F32) + spatial).astype(BF16)
            hidden_ref[:, lanes] = hidden
            wide = hidden.astype(F32)
            plain = plain + fold(wide)
            square = square + fold(wide * wide)
        return plain, square

    zero = jnp.zeros((8, sizes.pair), F32)
    plain, square = lax.fori_loop(0, sizes.pairs // block, step, (zero, zero))
    put_sums(clip_ref, plain, square)


def add_up(refs):
    total = refs[0][...]
    for ref in refs[1:]:
        total = total + ref[...]
    return total


def put_sums(target, plain, square):
    target[...] = jnp.zeros(target.shape, F32)
    target[0:1, :] = jnp.sum(plain, axis=0, keepdims=True)
    target[1:2, :] = jnp.sum(square, axis=0, keepdims=True)


def frame_taps(cot_ref, before_ref, after_ref, lanes, sizes):
    own = cot_ref[:, lanes]
    later = jnp.concatenate([own[sizes.rows :], after_ref[:, lanes]], axis=0)
    earlier = jnp.concatenate([before_ref[:, lanes], own[: sizes.pixels - sizes.rows]], axis=0)
    return later, own, earlier


def activation_grad_body(sizes, block, cot_ref, before_ref, after_ref, kernel_ref, dact_ref, even_ref, odd_ref):
    temporal_weights(kernel_ref, even_ref, odd_ref, sizes)

    def step(b, _):
        p = b * block
        found = []
        for odd, weights in ((False, even_ref), (True, odd_ref)):
            rows = []
            for q in range(block):
                start = (p + q) * sizes.pair + (sizes.pair - sizes.edge if odd else 0)
                lanes = pl.ds(pl.multiple_of(start, 128), sizes.edge)
                rows.append(
                    jnp.concatenate(frame_taps(cot_ref, before_ref, after_ref, lanes, sizes), axis=1)
                )
            found.append(
                lax.dot_general(
                    jnp.concatenate(rows, axis=0), weights[...], (((1,), (1,)), ((), ())),
                    preferred_element_type=F32,
                )
            )
        for q in range(block):
            rows = slice(q * sizes.pixels, (q + 1) * sizes.pixels)
            dact_ref[:, pair_lanes(p + q, sizes)] = join(found[0][rows], found[1][rows], sizes)
        return 0

    lax.fori_loop(0, sizes.pairs // block, step, 0)


def temporal_body(
    sizes, clip_entries, terms, hidden_ref, cot_ref, dact_ref, *refs
):
    clips, (act_ref, grad_ref, sums_ref, rim_ref, normed) = refs[:terms], refs[terms:]
    mean, rate = moments(add_up(clips), 1, clip_entries, sizes)

    def step(p, carry):
        plain, cross = carry
        lanes = pair_lanes(p, sizes)
        for f in range(sizes.frames):
            rows = pl.ds(f * sizes.rows, sizes.rows)
            tnormed = (hidden_ref[rows, lanes].astype(F32) - mean) * rate
            act, s = silu_parts(tnormed)
            act_ref[rows, lanes] = act.astype(BF16)
            normed[rows, lanes] = tnormed
            grad = dact_ref[rows, lanes] * (s * (1.0 + tnormed * (1.0 - s)))
            grad_ref[rows, lanes] = grad
            plain = plain + fold(grad)
            cross = cross + fold(grad * tnormed)
        return plain, cross

    zero = jnp.zeros((8, sizes.pair), F32)
    plain, cross = lax.fori_loop(0, sizes.pairs, step, (zero, zero))
    put_sums(sums_ref, plain, cross)
    for k, source in enumerate((grad_ref, normed, cot_ref)):
        store_edge(sizes, source, rim_ref, k * sizes.pixels)


def pack(total, target, at, sizes):
    rows, channels = total.shape[0], sizes.channels
    full = channels // 128
    count = 3 * rows
    for i in range(3):
        for k in range(full):
            lanes = slice(i * sizes.edge + k * 128, i * sizes.edge + (k + 1) * 128)
            target[at + k * count + i * rows : at + k * count + (i + 1) * rows, :] = total[:, lanes]
    ends = jnp.concatenate([total[:, i * sizes.edge + full * 128 : (i + 1) * sizes.edge] for i in range(3)], axis=0)
    half = count // 2
    target[at + full * count : at + full * count + half, :] = jnp.concatenate(
        [ends[:half, : 128 - sizes.slack], ends[half:, : 128 - sizes.slack]], axis=1
    )


def packed_rows(rows, sizes):
    return 3 * rows * sizes.channels // 128


def temporal_grad_body(sizes, block, act_ref, cot_ref, before_ref, after_ref, out_ref, total):
    total[...] = jnp.zeros(total.shape, F32)
    channels = sizes.channels
    zeros = jnp.zeros((sizes.pixels, sizes.slack), BF16)

    def step(b, _):
        acts, cots = [], []
        for q in range(block):
            lanes = pair_lanes(b * block + q, sizes)
            act = act_ref[:, lanes]
            acts += [act[:, :channels], act[:, channels:]]
            taps = frame_taps(cot_ref, before_ref, after_ref, lanes, sizes)
            for part in (slice(0, channels), slice(channels, 2 * channels)):
                cots.append(
                    jnp.concatenate([jnp.concatenate([t[:, part], zeros], axis=1) for t in taps], axis=1)
                )
        total[...] += lax.dot_general(
            jnp.concatenate(acts, axis=0), jnp.concatenate(cots, axis=0), (((0,), (0,)), ((), ())),
            preferred_element_type=F32,
        )
        return 0

    lax.fori_loop(0, sizes.pairs // block, step, 0)
    pack(total, out_ref, 0, sizes)


def spatial_grad_body(
    sizes, clip_entries, terms, hidden_ref, cot_ref, grad_ref, rim_ref, act_ref, time_ref, *refs
):
    clips, sums = refs[:terms], refs[terms : 2 * terms]
    dtemp_ref, dspat_ref, keep_ref, send_ref, padded, total, packed = refs[2 * terms :]
    mean, rate = moments(add_up(clips), 1, clip_entries, sizes)
    means = group_totals(add_up(sums), sizes) * (1.0 / clip_entries)
    plain, cross = means[0:1], means[1:2]

    def rim(rows, f, before):
        lanes = slice(sizes.pair - sizes.edge, sizes.pair) if before else slice(0, sizes.edge)
        at = [pl.ds(k * sizes.pixels + f * sizes.rows, sizes.rows) for k in range(3)]
        grad, tnormed, cot = (rim_ref[r, :] for r in at)
        dtemp = rate[:, lanes] * (grad - plain[:, lanes] - tnormed * cross[:, lanes])
        return (cot + dtemp.astype(BF16).astype(F32)).astype(BF16).astype(F32)

    put_halo(rim, padded, sizes)

    def combine(p, _):
        lanes = pair_lanes(p, sizes)
        for f in range(sizes.frames):
            rows = pl.ds(f * sizes.rows, sizes.rows)
            tnormed = (hidden_ref[rows, lanes].astype(F32) - mean) * rate
            dtemp = (rate * (grad_ref[rows, lanes] - plain - tnormed * cross)).astype(BF16)
            dtemp_ref[rows, lanes] = dtemp
            dspat = cot_ref[rows, lanes].astype(F32) + dtemp.astype(F32)
            put_shifts(
                dspat, f, pl.ds(pl.multiple_of(p * sizes.pair + sizes.edge, 128), sizes.pair), padded, sizes
            )
        return 0

    lax.fori_loop(0, sizes.pairs, combine, 0)
    dspat_ref[...] = padded[1]

    channels = sizes.channels
    zeros = jnp.zeros((sizes.pixels, sizes.slack), BF16)
    total[...] = jnp.zeros(total.shape, F32)

    block = min(4, sizes.pairs)

    def step(b, _):
        for odd in (False, True):
            left, right = [], []
            for q in range(block):
                p = block * b + q
                start = p * sizes.pair + (sizes.edge if odd else 0)
                left.append(act_ref[:, pl.ds(pl.multiple_of(start, 128), sizes.window)])
                both = pl.ds(pl.multiple_of(p * sizes.pair + sizes.edge, 128), sizes.pair)
                taps = []
                for i in range(3):
                    d = padded[2 - i, :, both]
                    d = d[:, channels:] if odd else d[:, :channels]
                    taps.append(jnp.concatenate([d, zeros], axis=1))
                right.append(jnp.concatenate(taps, axis=1))
            part = lax.dot_general(
                jnp.concatenate(left, axis=0), jnp.concatenate(right, axis=0), (((0,), (0,)), ((), ())),
                preferred_element_type=F32,
            )
            total[...] += part[: 3 * channels] if odd else part[sizes.slack :]
        return 0

    lax.fori_loop(0, sizes.pairs // block, step, 0)
    pack(total, packed, 0, sizes)
    own, half = packed_rows(3 * channels, sizes), packed.shape[0] // 2
    packed[own : own + time_ref.shape[0], :] = time_ref[...]
    used = own + time_ref.shape[0]
    packed[used:, :] = jnp.zeros((packed.shape[0] - used, 128), F32)
    core = lax.axis_index("col")
    keep_ref[...] = packed[pl.ds(pl.multiple_of(core * half, 16), half), :]
    send_ref[...] = packed[pl.ds(pl.multiple_of((1 - core) * half, 16), half), :].astype(BF16)


def backward_body(
    sizes, frame_entries, block, x_ref, sums_ref, other_ref, dspat_ref, kernel_ref,
    grad_ref, out_ref, padded, plains, even_ref, odd_ref,
):
    backward_weights(kernel_ref, even_ref, odd_ref, sizes)
    mean, rate = moments(sums_ref[...] + other_ref[...], sizes.frames, frame_entries, sizes)

    def spread(k, _):
        lanes = pl.ds(pl.multiple_of(k * 128, 128), 128)
        for f in range(sizes.frames):
            rows = pl.ds(f * sizes.rows, sizes.rows)
            put_shifts(dspat_ref[rows, lanes].astype(F32), f, lanes, padded, sizes)
        return 0

    lax.fori_loop(0, sizes.padded // 128, spread, 0)
    plains[...] = jnp.zeros(plains.shape, F32)
    contract = (((1,), (1,)), ((), ()))

    def step(b, _):
        p = b * block
        even = lax.dot_general(
            windows(padded, p, block, False, sizes), even_ref[...], contract, preferred_element_type=F32
        )
        odd = lax.dot_general(
            windows(padded, p, block, True, sizes), odd_ref[...], contract, preferred_element_type=F32
        )
        for q in range(block):
            base = q * sizes.pixels
            for f in range(sizes.frames):
                at = slice(base + f * sizes.rows, base + (f + 1) * sizes.rows)
                dact = join(even[at], odd[at], sizes)
                rows, lanes = pl.ds(f * sizes.rows, sizes.rows), pair_lanes(p + q, sizes)
                normed = (x_ref[rows, lanes].astype(F32) - mean[f : f + 1]) * rate[f : f + 1]
                _, s = silu_parts(normed)
                grad = dact * (s * (1.0 + normed * (1.0 - s)))
                grad_ref[rows, lanes] = grad
                plains[f] += fold(grad)
                plains[sizes.frames + f] += fold(grad * normed)
        return 0

    lax.fori_loop(0, sizes.pairs // block, step, 0)
    for k in range(2 * sizes.frames):
        out_ref[k : k + 1, :] = jnp.sum(plains[k], axis=0, keepdims=True)


def finish_body(
    sizes, frame_entries, x_ref, sums_ref, other_ref, cot_ref, dtemp_ref, grad_ref, mine_ref, theirs_ref, out_ref
):
    mean, rate = moments(sums_ref[...] + other_ref[...], sizes.frames, frame_entries, sizes)
    means = group_totals(mine_ref[...] + theirs_ref[...], sizes) * (1.0 / frame_entries)

    def step(p, _):
        lanes = pair_lanes(p, sizes)
        for f in range(sizes.frames):
            rows = pl.ds(f * sizes.rows, sizes.rows)
            normed = (x_ref[rows, lanes].astype(F32) - mean[f : f + 1]) * rate[f : f + 1]
            dhidden = cot_ref[rows, lanes].astype(F32) + dtemp_ref[rows, lanes].astype(F32)
            plain, cross = means[f : f + 1], means[sizes.frames + f : sizes.frames + f + 1]
            out_ref[rows, lanes] = dhidden + rate[f : f + 1] * (grad_ref[rows, lanes] - plain - normed * cross)
        return 0

    lax.fori_loop(0, sizes.pairs, step, 0)


def unpack_body(sizes, scale, parts, *refs):
    mine, theirs = refs[:parts], refs[parts : 2 * parts]
    spatial_ref, temporal_ref, packed = refs[2 * parts :]
    rows = mine[0].shape[0]
    half = packed.shape[0] // 2
    core, me = lax.axis_index("col"), lax.axis_index("dp")
    for s in range(parts):
        place = (me ^ s) * rows
        packed[pl.ds(pl.multiple_of(core * half + place, 16), rows), :] = mine[s][...]
        packed[pl.ds(pl.multiple_of((1 - core) * half + place, 16), rows), :] = theirs[s][...]
    full = sizes.channels // 128
    at = 0
    for target in (spatial_ref, temporal_ref):
        count = target.shape[0]
        tile = math.gcd(count // 2, 240)

        def step(k, _, at=at, target=target, count=count, tile=tile):
            for second in range(2):
                row = pl.multiple_of(k * tile, 16) + second * (count // 2)
                found = [
                    packed[pl.ds(pl.multiple_of(at + b * count + row, 16), tile), :].astype(F32) for b in range(full)
                ]
                ends = packed[pl.ds(pl.multiple_of(at + full * count + k * tile, 16), tile), :].astype(F32)
                cut = 128 - sizes.slack
                found.append(ends[:, cut:] if second else ends[:, :cut])
                target[pl.ds(pl.multiple_of(row, 16), tile), :] = jnp.concatenate(found, axis=1) * scale
            return 0

        lax.fori_loop(0, count // 2 // tile, step, 0)
        at += count * sizes.channels // 128


def swap(values, axis, bit):
    count = lax.axis_size(axis)
    return lax.ppermute(values, axis, [(i, i ^ bit) for i in range(count)])


def from_all(values, axis):
    return [values] + [swap(values, axis, s) for s in range(1, lax.axis_size(axis))]


def scattered(total, axis, beside=None):
    count = lax.axis_size(axis)
    rows = total.shape[0] // count
    me = lax.axis_index(axis)
    chunks = [lax.dynamic_slice_in_dim(total, (me ^ s) * rows, rows, 0) for s in range(count)]
    found = [swap(chunks[s].astype(BF16), axis, s) for s in range(1, count)]
    if beside is not None:
        found, beside = lax.optimization_barrier((found, beside))
    total = chunks[0]
    for chunk in found:
        total = total + chunk.astype(F32)
    return total, beside


def gathered(chunk, axis):
    parts = from_all(chunk, axis)
    me = lax.axis_index(axis)
    rows = chunk.shape[0]
    out = jnp.zeros((rows * len(parts), chunk.shape[1]), chunk.dtype)
    for s, part in enumerate(parts):
        out = lax.dynamic_update_slice_in_dim(out, part, (me ^ s) * rows, 0)
    return out


def shards(latents, spatial_kernel, temporal_kernel, cotangent):
    _, frames, rows, width = latents.shape
    channels = spatial_kernel.shape[2]
    sizes = Sizes(frames, rows, width // channels, channels)
    cols, seqs = lax.axis_size("col"), lax.axis_size("seq")
    frame_entries = float(rows * sizes.columns * cols * (channels // GROUPS))
    clip_entries = frame_entries * frames * seqs
    pixels = lax.axis_size("dp") * seqs * cols * sizes.pixels * sizes.columns
    grad_scale = 1.0 / math.sqrt(pixels)

    x = latents.reshape(sizes.pixels, width)
    cot = cotangent.reshape(sizes.pixels, width)
    sum_shape = struct((8, sizes.pair), F32)
    frame_shape = struct((2 * frames, sizes.pair), F32)
    padded_scratch = pltpu.VMEM((3, sizes.pixels, sizes.padded), BF16)
    slack = sizes.slack

    forth = [(i, i + 1) for i in range(seqs - 1)]
    before = lax.ppermute(cot[sizes.pixels - rows :], "seq", forth)
    after = lax.ppermute(cot[:rows], "seq", [(j, i) for i, j in forth])

    sums, edge = call(
        functools.partial(latent_sums_body, sizes),
        [frame_shape, struct((sizes.pixels, sizes.edge), BF16)],
    )(x)
    other = swap(sums, "col", 1)
    rim = swap(edge, "col", 1)
    window_weights = [pltpu.VMEM((3 * sizes.window, sizes.edge), BF16)] * 2
    hidden, act, clip = call(
        functools.partial(forward_body, sizes, frame_entries, min(4, sizes.pairs)),
        [struct((sizes.pixels, width), BF16), struct((sizes.pixels, sizes.padded), BF16), sum_shape],
        [padded_scratch] + window_weights,
        flops=CONV_COST,
    )(x, sums, other, rim, spatial_kernel)
    clips = from_all(clip + swap(clip, "col", 1), "seq")
    dact = call(
        functools.partial(activation_grad_body, sizes, min(4, sizes.pairs)),
        struct((sizes.pixels, width), F32),
        [pltpu.VMEM((sizes.edge, 3 * sizes.edge), BF16)] * 2,
        flops=CONV_COST // 3,
    )(cot, before, after, temporal_kernel)
    tact, tgrad, means, rims = call(
        functools.partial(temporal_body, sizes, clip_entries, seqs),
        [
            struct((sizes.pixels, width), BF16),
            struct((sizes.pixels, width), F32),
            sum_shape,
            struct((3 * sizes.pixels, sizes.edge), F32),
        ],
        [pltpu.VMEM((sizes.pixels, width), F32)],
        flops=CONV_COST // 3,
    )(hidden, cot, dact, *clips)
    means = from_all(means + swap(means, "col", 1), "seq")
    rims = swap(rims, "col", 1)
    temporal_grad = call(
        functools.partial(temporal_grad_body, sizes, min(4, sizes.pairs)),
        struct((packed_rows(channels, sizes), 128), F32),
        [pltpu.VMEM((channels, 3 * sizes.edge), F32)],
        flops=CONV_COST // 3,
    )(tact, cot, before, after)

    devices = lax.axis_size("dp") * seqs * cols
    used = packed_rows(3 * channels, sizes) + packed_rows(channels, sizes)
    all_rows = -(-used // (16 * devices)) * 16 * devices
    half = all_rows // 2
    dtemp, dspat, keep, send = call(
        functools.partial(spatial_grad_body, sizes, clip_entries, seqs),
        [
            struct((sizes.pixels, width), BF16),
            struct((sizes.pixels, sizes.padded), BF16),
            struct((half, 128), F32),
            struct((half, 128), BF16),
        ],
        [
            padded_scratch,
            pltpu.VMEM((3 * channels, 3 * sizes.edge), F32),
            pltpu.VMEM((all_rows, 128), F32),
        ],
        flops=CONV_COST,
    )(hidden, cot, tgrad, rims, act, temporal_grad, *clips, *means)
    dnormed, mine = call(
        functools.partial(backward_body, sizes, frame_entries, min(4, sizes.pairs)),
        [struct((sizes.pixels, width), F32), frame_shape],
        [padded_scratch, pltpu.VMEM((2 * frames, 8, sizes.pair), F32)]
        + [pltpu.VMEM((sizes.edge, 3 * sizes.window), BF16)] * 2,
        flops=CONV_COST,
    )(x, sums, other, dspat, spatial_kernel)
    total = keep + swap(send, "col", 1).astype(F32)
    total, (dnormed, mine) = scattered(total, "dp", (dnormed, mine))
    total, _ = scattered(total, "seq")
    theirs = swap(mine, "col", 1)
    grad_latents = call(
        functools.partial(finish_body, sizes, frame_entries), struct((sizes.pixels, width), F32),
        flops=CONV_COST // 3,
    )(x, sums, other, cot, dtemp, dnormed, mine, theirs)
    parts = from_all(gathered(total.astype(BF16), "seq"), "dp")
    parts[1], grad_latents = lax.optimization_barrier((parts[1], grad_latents))
    others = [swap(part, "col", 1) for part in parts]
    spatial_grad, temporal_grad = call(
        functools.partial(unpack_body, sizes, grad_scale, len(parts)),
        [struct((9 * channels, channels), F32), struct((3 * channels, channels), F32)],
        [pltpu.VMEM((all_rows, 128), BF16)],
        flops=CONV_COST // 4,
    )(*parts, *others)

    return (
        grad_latents.reshape(latents.shape),
        spatial_grad.reshape(spatial_kernel.shape),
        temporal_grad.reshape(temporal_kernel.shape),
    )


def solution(mesh):
    in_specs = (P("dp", "seq", None, "col"), P(), P(), P("dp", "seq", None, "col"))
    out_specs = (P("dp", "seq", None, "col"), P(), P())
    return jax.shard_map(shards, mesh=mesh, in_specs=in_specs, out_specs=out_specs, check_vma=False)
```

```python
import functools
import math

import jax
import jax.numpy as jnp
from jax import lax
from jax.experimental import pallas as pl
from jax.experimental.pallas import tpu as pltpu
from jax.sharding import PartitionSpec as P

GROUPS = 32
EPSILON = 1e-05
F32 = jnp.float32
BF16 = jnp.bfloat16
VMEM_LIMIT = 28 * 1024 * 1024
CONV_COST = 12_000_000_000


def whole(count):
    return [pl.BlockSpec(memory_space=pltpu.VMEM)] * count


def call(body, outs, scratch=(), flops=0, moved=0):
    return pl.pallas_call(
        body,
        out_shape=outs,
        out_specs=jax.tree.map(lambda _: pl.BlockSpec(memory_space=pltpu.VMEM), outs),
        scratch_shapes=list(scratch),
        compiler_params=pltpu.CompilerParams(vmem_limit_bytes=VMEM_LIMIT),
        cost_estimate=pl.CostEstimate(flops=flops, bytes_accessed=moved, transcendentals=0),
    )


def struct(shape, kind):
    return jax.ShapeDtypeStruct(shape, kind)


class Sizes:
    def __init__(self, frames, rows, columns, channels):
        self.frames = frames
        self.rows = rows
        self.columns = columns
        self.channels = channels
        self.pixels = frames * rows
        self.width = columns * channels
        self.pair = 2 * channels
        self.pairs = columns // 2
        self.edge = -(-channels // 128) * 128
        self.slack = self.edge - channels
        self.window = 3 * channels + self.slack
        self.padded = self.width + 2 * self.edge


def group_totals(sums, sizes):
    size = sizes.channels // GROUPS

    def member(shape, lane_dim):
        lane = lax.broadcasted_iota(jnp.int32, shape, lane_dim)
        group = lax.broadcasted_iota(jnp.int32, shape, 1 - lane_dim)
        channel = jnp.where(lane >= sizes.channels, lane - sizes.channels, lane)
        return ((channel >= group * size) & (channel < group * size + size)).astype(F32)

    high = lax.Precision.HIGHEST
    by_group = jnp.dot(sums, member((sizes.pair, 128), 0), precision=high, preferred_element_type=F32)
    return jnp.dot(by_group, member((128, sizes.pair), 1), precision=high, preferred_element_type=F32)


def moments(sums, half, entries, sizes):
    totals = group_totals(sums, sizes) * (1.0 / entries)
    mean = totals[0:half]
    rate = lax.rsqrt(totals[half : 2 * half] - mean * mean + EPSILON)
    return mean, rate


def fold(values):
    return jnp.sum(values.reshape(values.shape[0] // 8, 8, values.shape[1]), axis=0)


def pair_lanes(p, sizes):
    return pl.ds(pl.multiple_of(p * sizes.pair, 128), sizes.pair)


def join(even, odd, sizes):
    cut = sizes.edge - 128
    middle = even[:, cut:] + odd[:, :128]
    return jnp.concatenate([even[:, :cut], middle, odd[:, 128:]], axis=1)


def latent_sums_body(sizes, x_ref, sums_ref, edge_ref):
    def frame(f):
        rows = pl.ds(f * sizes.rows, sizes.rows)

        def step(p, carry):
            plain, square = carry
            v = x_ref[rows, pair_lanes(p, sizes)].astype(F32)
            return plain + fold(v), square + fold(v * v)

        zero = jnp.zeros((8, sizes.pair), F32)
        plain, square = lax.fori_loop(0, sizes.pairs, step, (zero, zero))
        return jnp.sum(plain, axis=0, keepdims=True), jnp.sum(square, axis=0, keepdims=True)

    found = [frame(f) for f in range(sizes.frames)]
    for f, (plain, square) in enumerate(found):
        sums_ref[f : f + 1, :] = plain
        sums_ref[sizes.frames + f : sizes.frames + f + 1, :] = square
    store_edge(sizes, x_ref, edge_ref)


def store_edge(sizes, source, target, at=0):
    left = lax.axis_index("col") == 0
    rows = pl.ds(at, sizes.pixels)

    @pl.when(left)
    def _():
        target[rows, :] = source[:, sizes.width - sizes.edge : sizes.width].astype(target.dtype)

    @pl.when(jnp.logical_not(left))
    def _():
        target[rows, :] = source[:, 0 : sizes.edge].astype(target.dtype)


def row_shifts(values, sizes):
    row = lax.broadcasted_iota(jnp.int32, values.shape, 0)
    down = jnp.where(row == 0, 0.0, pltpu.roll(values, 1, 0))
    up = jnp.where(row == sizes.rows - 1, 0.0, pltpu.roll(values, sizes.rows - 1, 0))
    return down, values, up


def put_shifts(values, frame, lanes, target, sizes):
    rows = pl.ds(frame * sizes.rows, sizes.rows)
    for i, moved in enumerate(row_shifts(values, sizes)):
        target[i, rows, lanes] = moved.astype(BF16)


def put_halo(of_frame, target, sizes):
    left = lax.axis_index("col") == 0
    for f in range(sizes.frames):
        rows = pl.ds(f * sizes.rows, sizes.rows)
        before, after = of_frame(rows, f, True), of_frame(rows, f, False)
        put_shifts(jnp.where(left, 0.0, before), f, pl.ds(0, sizes.edge), target, sizes)
        put_shifts(
            jnp.where(left, after, 0.0), f, pl.ds(sizes.edge + sizes.width, sizes.edge), target, sizes
        )


def forward_weights(kernel_ref, even_ref, odd_ref, sizes):
    channels, slack, window = sizes.channels, sizes.slack, sizes.window
    for weights in (even_ref, odd_ref):
        weights[...] = jnp.zeros(weights.shape, BF16)
    for i in range(3):
        for j in range(3):
            taps = kernel_ref[i, j]
            zeros = jnp.zeros((channels, slack), BF16)
            at = i * window + j * channels
            even_ref[at + slack : at + slack + channels, :] = jnp.concatenate([taps, zeros], axis=1)
            odd_ref[at : at + channels, :] = jnp.concatenate([zeros, taps], axis=1)


def backward_weights(kernel_ref, even_ref, odd_ref, sizes):
    channels, slack, window = sizes.channels, sizes.slack, sizes.window
    for weights in (even_ref, odd_ref):
        weights[...] = jnp.zeros(weights.shape, BF16)
    zeros = jnp.zeros((channels, slack), BF16)
    for i in range(3):
        taps = [kernel_ref[2 - i, 2 - j] for j in range(3)]
        lanes = slice(i * window, (i + 1) * window)
        even_ref[0:channels, lanes] = jnp.concatenate([zeros] + taps, axis=1)
        odd_ref[slack : slack + channels, lanes] = jnp.concatenate(taps + [zeros], axis=1)


def temporal_weights(kernel_ref, even_ref, odd_ref, sizes):
    channels, slack, edge = sizes.channels, sizes.slack, sizes.edge
    for weights in (even_ref, odd_ref):
        weights[...] = jnp.zeros(weights.shape, BF16)
    zeros = jnp.zeros((channels, slack), BF16)
    for i in range(3):
        lanes = slice(i * edge, (i + 1) * edge)
        even_ref[0:channels, lanes] = jnp.concatenate([kernel_ref[i], zeros], axis=1)
        odd_ref[slack : slack + channels, lanes] = jnp.concatenate([zeros, kernel_ref[i]], axis=1)


def windows(padded_ref, p, count, odd, sizes):
    found = []
    for q in range(count):
        start = pl.multiple_of((p + q) * sizes.pair, 128) + (sizes.edge if odd else 0)
        lanes = pl.ds(pl.multiple_of(start, 128), sizes.window)
        found.append(jnp.concatenate([padded_ref[i, :, lanes] for i in range(3)], axis=1))
    return jnp.concatenate(found, axis=0)


def silu_parts(v):
    s = 1.0 / (1.0 + jnp.exp(-v))
    return v * s, s


def forward_body(
    sizes, frame_entries, block, x_ref, sums_ref, other_ref, rim_ref, kernel_ref,
    hidden_ref, act_ref, clip_ref, padded, even_ref, odd_ref,
):
    forward_weights(kernel_ref, even_ref, odd_ref, sizes)
    mean, rate = moments(sums_ref[...] + other_ref[...], sizes.frames, frame_entries, sizes)

    def rim(rows, f, before):
        lanes = slice(sizes.pair - sizes.edge, sizes.pair) if before else slice(0, sizes.edge)
        v = rim_ref[rows, :].astype(F32)
        return silu_parts((v - mean[f : f + 1, lanes]) * rate[f : f + 1, lanes])[0]

    put_halo(rim, padded, sizes)

    def activate(p, _):
        for f in range(sizes.frames):
            v = x_ref[pl.ds(f * sizes.rows, sizes.rows), pair_lanes(p, sizes)].astype(F32)
            act = silu_parts((v - mean[f : f + 1]) * rate[f : f + 1])[0]
            lanes = pl.ds(pl.multiple_of(p * sizes.pair + sizes.edge, 128), sizes.pair)
            put_shifts(act, f, lanes, padded, sizes)
        return 0

    lax.fori_loop(0, sizes.pairs, activate, 0)
    act_ref[...] = padded[1]

    def step(b, carry):
        plain, square = carry
        p = b * block
        even = jnp.dot(windows(padded, p, block, False, sizes), even_ref[...], preferred_element_type=F32)
        odd = jnp.dot(windows(padded, p, block, True, sizes), odd_ref[...], preferred_element_type=F32)
        for q in range(block):
            rows = slice(q * sizes.pixels, (q + 1) * sizes.pixels)
            spatial = join(even[rows], odd[rows], sizes)
            lanes = pair_lanes(p + q, sizes)
            hidden = (x_ref[:, lanes].astype(F32) + spatial).astype(BF16)
            hidden_ref[:, lanes] = hidden
            wide = hidden.astype(F32)
            plain = plain + fold(wide)
            square = square + fold(wide * wide)
        return plain, square

    zero = jnp.zeros((8, sizes.pair), F32)
    plain, square = lax.fori_loop(0, sizes.pairs // block, step, (zero, zero))
    put_sums(clip_ref, plain, square)


def add_up(refs):
    total = refs[0][...]
    for ref in refs[1:]:
        total = total + ref[...]
    return total


def put_sums(target, plain, square):
    target[...] = jnp.zeros(target.shape, F32)
    target[0:1, :] = jnp.sum(plain, axis=0, keepdims=True)
    target[1:2, :] = jnp.sum(square, axis=0, keepdims=True)


def frame_taps(cot_ref, before_ref, after_ref, lanes, sizes):
    own = cot_ref[:, lanes]
    later = jnp.concatenate([own[sizes.rows :], after_ref[:, lanes]], axis=0)
    earlier = jnp.concatenate([before_ref[:, lanes], own[: sizes.pixels - sizes.rows]], axis=0)
    return later, own, earlier


def activation_grad_body(sizes, block, cot_ref, before_ref, after_ref, kernel_ref, dact_ref, even_ref, odd_ref):
    temporal_weights(kernel_ref, even_ref, odd_ref, sizes)

    def step(b, _):
        p = b * block
        found = []
        for odd, weights in ((False, even_ref), (True, odd_ref)):
            rows = []
            for q in range(block):
                start = (p + q) * sizes.pair + (sizes.pair - sizes.edge if odd else 0)
                lanes = pl.ds(pl.multiple_of(start, 128), sizes.edge)
                rows.append(
                    jnp.concatenate(frame_taps(cot_ref, before_ref, after_ref, lanes, sizes), axis=1)
                )
            found.append(
                lax.dot_general(
                    jnp.concatenate(rows, axis=0), weights[...], (((1,), (1,)), ((), ())),
                    preferred_element_type=F32,
                )
            )
        for q in range(block):
            rows = slice(q * sizes.pixels, (q + 1) * sizes.pixels)
            dact_ref[:, pair_lanes(p + q, sizes)] = join(found[0][rows], found[1][rows], sizes)
        return 0

    lax.fori_loop(0, sizes.pairs // block, step, 0)


def temporal_body(
    sizes, clip_entries, terms, hidden_ref, cot_ref, dact_ref, *refs
):
    clips, (act_ref, grad_ref, sums_ref, rim_ref, normed) = refs[:terms], refs[terms:]
    mean, rate = moments(add_up(clips), 1, clip_entries, sizes)

    def step(p, carry):
        plain, cross = carry
        lanes = pair_lanes(p, sizes)
        for f in range(sizes.frames):
            rows = pl.ds(f * sizes.rows, sizes.rows)
            tnormed = (hidden_ref[rows, lanes].astype(F32) - mean) * rate
            act, s = silu_parts(tnormed)
            act_ref[rows, lanes] = act.astype(BF16)
            normed[rows, lanes] = tnormed
            grad = dact_ref[rows, lanes] * (s * (1.0 + tnormed * (1.0 - s)))
            grad_ref[rows, lanes] = grad
            plain = plain + fold(grad)
            cross = cross + fold(grad * tnormed)
        return plain, cross

    zero = jnp.zeros((8, sizes.pair), F32)
    plain, cross = lax.fori_loop(0, sizes.pairs, step, (zero, zero))
    put_sums(sums_ref, plain, cross)
    for k, source in enumerate((grad_ref, normed, cot_ref)):
        store_edge(sizes, source, rim_ref, k * sizes.pixels)


def pack(total, target, at, sizes):
    rows, channels = total.shape[0], sizes.channels
    full = channels // 128
    count = 3 * rows
    for i in range(3):
        for k in range(full):
            lanes = slice(i * sizes.edge + k * 128, i * sizes.edge + (k + 1) * 128)
            target[at + k * count + i * rows : at + k * count + (i + 1) * rows, :] = total[:, lanes]
    ends = jnp.concatenate([total[:, i * sizes.edge + full * 128 : (i + 1) * sizes.edge] for i in range(3)], axis=0)
    half = count // 2
    target[at + full * count : at + full * count + half, :] = jnp.concatenate(
        [ends[:half, : 128 - sizes.slack], ends[half:, : 128 - sizes.slack]], axis=1
    )


def packed_rows(rows, sizes):
    return 3 * rows * sizes.channels // 128


def temporal_grad_body(sizes, block, act_ref, cot_ref, before_ref, after_ref, out_ref, total):
    total[...] = jnp.zeros(total.shape, F32)
    channels = sizes.channels
    zeros = jnp.zeros((sizes.pixels, sizes.slack), BF16)

    def step(b, _):
        acts, cots = [], []
        for q in range(block):
            lanes = pair_lanes(b * block + q, sizes)
            act = act_ref[:, lanes]
            acts += [act[:, :channels], act[:, channels:]]
            taps = frame_taps(cot_ref, before_ref, after_ref, lanes, sizes)
            for part in (slice(0, channels), slice(channels, 2 * channels)):
                cots.append(
                    jnp.concatenate([jnp.concatenate([t[:, part], zeros], axis=1) for t in taps], axis=1)
                )
        total[...] += lax.dot_general(
            jnp.concatenate(acts, axis=0), jnp.concatenate(cots, axis=0), (((0,), (0,)), ((), ())),
            preferred_element_type=F32,
        )
        return 0

    lax.fori_loop(0, sizes.pairs // block, step, 0)
    pack(total, out_ref, 0, sizes)


def spatial_grad_body(
    sizes, clip_entries, terms, hidden_ref, cot_ref, grad_ref, rim_ref, act_ref, time_ref, *refs
):
    clips, sums = refs[:terms], refs[terms : 2 * terms]
    dtemp_ref, dspat_ref, keep_ref, send_ref, padded, total, packed = refs[2 * terms :]
    mean, rate = moments(add_up(clips), 1, clip_entries, sizes)
    means = group_totals(add_up(sums), sizes) * (1.0 / clip_entries)
    plain, cross = means[0:1], means[1:2]

    def rim(rows, f, before):
        lanes = slice(sizes.pair - sizes.edge, sizes.pair) if before else slice(0, sizes.edge)
        at = [pl.ds(k * sizes.pixels + f * sizes.rows, sizes.rows) for k in range(3)]
        grad, tnormed, cot = (rim_ref[r, :] for r in at)
        dtemp = rate[:, lanes] * (grad - plain[:, lanes] - tnormed * cross[:, lanes])
        return (cot + dtemp.astype(BF16).astype(F32)).astype(BF16).astype(F32)

    put_halo(rim, padded, sizes)

    def combine(p, _):
        lanes = pair_lanes(p, sizes)
        for f in range(sizes.frames):
            rows = pl.ds(f * sizes.rows, sizes.rows)
            tnormed = (hidden_ref[rows, lanes].astype(F32) - mean) * rate
            dtemp = (rate * (grad_ref[rows, lanes] - plain - tnormed * cross)).astype(BF16)
            dtemp_ref[rows, lanes] = dtemp
            dspat = cot_ref[rows, lanes].astype(F32) + dtemp.astype(F32)
            put_shifts(
                dspat, f, pl.ds(pl.multiple_of(p * sizes.pair + sizes.edge, 128), sizes.pair), padded, sizes
            )
        return 0

    lax.fori_loop(0, sizes.pairs, combine, 0)
    dspat_ref[...] = padded[1]

    channels = sizes.channels
    zeros = jnp.zeros((sizes.pixels, sizes.slack), BF16)
    total[...] = jnp.zeros(total.shape, F32)

    block = min(4, sizes.pairs)

    def step(b, _):
        for odd in (False, True):
            left, right = [], []
            for q in range(block):
                p = block * b + q
                start = p * sizes.pair + (sizes.edge if odd else 0)
                left.append(act_ref[:, pl.ds(pl.multiple_of(start, 128), sizes.window)])
                both = pl.ds(pl.multiple_of(p * sizes.pair + sizes.edge, 128), sizes.pair)
                taps = []
                for i in range(3):
                    d = padded[2 - i, :, both]
                    d = d[:, channels:] if odd else d[:, :channels]
                    taps.append(jnp.concatenate([d, zeros], axis=1))
                right.append(jnp.concatenate(taps, axis=1))
            part = lax.dot_general(
                jnp.concatenate(left, axis=0), jnp.concatenate(right, axis=0), (((0,), (0,)), ((), ())),
                preferred_element_type=F32,
            )
            total[...] += part[: 3 * channels] if odd else part[sizes.slack :]
        return 0

    lax.fori_loop(0, sizes.pairs // block, step, 0)
    pack(total, packed, 0, sizes)
    own, half = packed_rows(3 * channels, sizes), packed.shape[0] // 2
    packed[own : own + time_ref.shape[0], :] = time_ref[...]
    used = own + time_ref.shape[0]
    packed[used:, :] = jnp.zeros((packed.shape[0] - used, 128), F32)
    core = lax.axis_index("col")
    keep_ref[...] = packed[pl.ds(pl.multiple_of(core * half, 16), half), :]
    send_ref[...] = packed[pl.ds(pl.multiple_of((1 - core) * half, 16), half), :].astype(BF16)


def backward_body(
    sizes, frame_entries, block, x_ref, sums_ref, other_ref, dspat_ref, kernel_ref,
    grad_ref, out_ref, padded, plains, even_ref, odd_ref,
):
    backward_weights(kernel_ref, even_ref, odd_ref, sizes)
    mean, rate = moments(sums_ref[...] + other_ref[...], sizes.frames, frame_entries, sizes)

    def spread(k, _):
        lanes = pl.ds(pl.multiple_of(k * 128, 128), 128)
        for f in range(sizes.frames):
            rows = pl.ds(f * sizes.rows, sizes.rows)
            put_shifts(dspat_ref[rows, lanes].astype(F32), f, lanes, padded, sizes)
        return 0

    lax.fori_loop(0, sizes.padded // 128, spread, 0)
    plains[...] = jnp.zeros(plains.shape, F32)
    contract = (((1,), (1,)), ((), ()))

    def step(b, _):
        p = b * block
        even = lax.dot_general(
            windows(padded, p, block, False, sizes), even_ref[...], contract, preferred_element_type=F32
        )
        odd = lax.dot_general(
            windows(padded, p, block, True, sizes), odd_ref[...], contract, preferred_element_type=F32
        )
        for q in range(block):
            base = q * sizes.pixels
            for f in range(sizes.frames):
                at = slice(base + f * sizes.rows, base + (f + 1) * sizes.rows)
                dact = join(even[at], odd[at], sizes)
                rows, lanes = pl.ds(f * sizes.rows, sizes.rows), pair_lanes(p + q, sizes)
                normed = (x_ref[rows, lanes].astype(F32) - mean[f : f + 1]) * rate[f : f + 1]
                _, s = silu_parts(normed)
                grad = dact * (s * (1.0 + normed * (1.0 - s)))
                grad_ref[rows, lanes] = grad
                plains[f] += fold(grad)
                plains[sizes.frames + f] += fold(grad * normed)
        return 0

    lax.fori_loop(0, sizes.pairs // block, step, 0)
    for k in range(2 * sizes.frames):
        out_ref[k : k + 1, :] = jnp.sum(plains[k], axis=0, keepdims=True)


def finish_body(
    sizes, frame_entries, x_ref, sums_ref, other_ref, cot_ref, dtemp_ref, grad_ref, mine_ref, theirs_ref, out_ref
):
    mean, rate = moments(sums_ref[...] + other_ref[...], sizes.frames, frame_entries, sizes)
    means = group_totals(mine_ref[...] + theirs_ref[...], sizes) * (1.0 / frame_entries)

    def step(p, _):
        lanes = pair_lanes(p, sizes)
        for f in range(sizes.frames):
            rows = pl.ds(f * sizes.rows, sizes.rows)
            normed = (x_ref[rows, lanes].astype(F32) - mean[f : f + 1]) * rate[f : f + 1]
            dhidden = cot_ref[rows, lanes].astype(F32) + dtemp_ref[rows, lanes].astype(F32)
            plain, cross = means[f : f + 1], means[sizes.frames + f : sizes.frames + f + 1]
            out_ref[rows, lanes] = dhidden + rate[f : f + 1] * (grad_ref[rows, lanes] - plain - normed * cross)
        return 0

    lax.fori_loop(0, sizes.pairs, step, 0)


def unpack_body(sizes, scale, parts, *refs):
    mine, theirs = refs[:parts], refs[parts : 2 * parts]
    spatial_ref, temporal_ref, packed = refs[2 * parts :]
    rows = mine[0].shape[0]
    half = packed.shape[0] // 2
    core, me = lax.axis_index("col"), lax.axis_index("dp")
    for s in range(parts):
        place = (me ^ s) * rows
        packed[pl.ds(pl.multiple_of(core * half + place, 16), rows), :] = mine[s][...]
        packed[pl.ds(pl.multiple_of((1 - core) * half + place, 16), rows), :] = theirs[s][...]
    full = sizes.channels // 128
    at = 0
    for target in (spatial_ref, temporal_ref):
        count = target.shape[0]
        tile = math.gcd(count // 2, 240)

        def step(k, _, at=at, target=target, count=count, tile=tile):
            for second in range(2):
                row = pl.multiple_of(k * tile, 16) + second * (count // 2)
                found = [
                    packed[pl.ds(pl.multiple_of(at + b * count + row, 16), tile), :].astype(F32) for b in range(full)
                ]
                ends = packed[pl.ds(pl.multiple_of(at + full * count + k * tile, 16), tile), :].astype(F32)
                cut = 128 - sizes.slack
                found.append(ends[:, cut:] if second else ends[:, :cut])
                target[pl.ds(pl.multiple_of(row, 16), tile), :] = jnp.concatenate(found, axis=1) * scale
            return 0

        lax.fori_loop(0, count // 2 // tile, step, 0)
        at += count * sizes.channels // 128


def swap(values, axis, bit):
    count = lax.axis_size(axis)
    return lax.ppermute(values, axis, [(i, i ^ bit) for i in range(count)])


def from_all(values, axis):
    return [values] + [swap(values, axis, s) for s in range(1, lax.axis_size(axis))]


def scattered(total, axis, beside=None):
    count = lax.axis_size(axis)
    rows = total.shape[0] // count
    me = lax.axis_index(axis)
    chunks = [lax.dynamic_slice_in_dim(total, (me ^ s) * rows, rows, 0) for s in range(count)]
    found = [swap(chunks[s].astype(BF16), axis, s) for s in range(1, count)]
    if beside is not None:
        found, beside = lax.optimization_barrier((found, beside))
    total = chunks[0]
    for chunk in found:
        total = total + chunk.astype(F32)
    return total, beside


def gathered(chunk, axis):
    parts = from_all(chunk, axis)
    me = lax.axis_index(axis)
    rows = chunk.shape[0]
    out = jnp.zeros((rows * len(parts), chunk.shape[1]), chunk.dtype)
    for s, part in enumerate(parts):
        out = lax.dynamic_update_slice_in_dim(out, part, (me ^ s) * rows, 0)
    return out


def shards(latents, spatial_kernel, temporal_kernel, cotangent):
    _, frames, rows, width = latents.shape
    channels = spatial_kernel.shape[2]
    sizes = Sizes(frames, rows, width // channels, channels)
    cols, seqs = lax.axis_size("col"), lax.axis_size("seq")
    frame_entries = float(rows * sizes.columns * cols * (channels // GROUPS))
    clip_entries = frame_entries * frames * seqs
    pixels = lax.axis_size("dp") * seqs * cols * sizes.pixels * sizes.columns
    grad_scale = 1.0 / math.sqrt(pixels)

    x = latents.reshape(sizes.pixels, width)
    cot = cotangent.reshape(sizes.pixels, width)
    sum_shape = struct((8, sizes.pair), F32)
    frame_shape = struct((2 * frames, sizes.pair), F32)
    padded_scratch = pltpu.VMEM((3, sizes.pixels, sizes.padded), BF16)
    slack = sizes.slack

    forth = [(i, i + 1) for i in range(seqs - 1)]
    before = lax.ppermute(cot[sizes.pixels - rows :], "seq", forth)
    after = lax.ppermute(cot[:rows], "seq", [(j, i) for i, j in forth])

    sums, edge = call(
        functools.partial(latent_sums_body, sizes),
        [frame_shape, struct((sizes.pixels, sizes.edge), BF16)],
    )(x)
    other = swap(sums, "col", 1)
    rim = swap(edge, "col", 1)
    window_weights = [pltpu.VMEM((3 * sizes.window, sizes.edge), BF16)] * 2
    hidden, act, clip = call(
        functools.partial(forward_body, sizes, frame_entries, min(4, sizes.pairs)),
        [struct((sizes.pixels, width), BF16), struct((sizes.pixels, sizes.padded), BF16), sum_shape],
        [padded_scratch] + window_weights,
        flops=CONV_COST,
    )(x, sums, other, rim, spatial_kernel)
    clips = from_all(clip + swap(clip, "col", 1), "seq")
    dact = call(
        functools.partial(activation_grad_body, sizes, min(4, sizes.pairs)),
        struct((sizes.pixels, width), F32),
        [pltpu.VMEM((sizes.edge, 3 * sizes.edge), BF16)] * 2,
        flops=CONV_COST // 3,
    )(cot, before, after, temporal_kernel)
    tact, tgrad, means, rims = call(
        functools.partial(temporal_body, sizes, clip_entries, seqs),
        [
            struct((sizes.pixels, width), BF16),
            struct((sizes.pixels, width), F32),
            sum_shape,
            struct((3 * sizes.pixels, sizes.edge), F32),
        ],
        [pltpu.VMEM((sizes.pixels, width), F32)],
        flops=CONV_COST // 3,
    )(hidden, cot, dact, *clips)
    means = from_all(means + swap(means, "col", 1), "seq")
    rims = swap(rims, "col", 1)
    temporal_grad = call(
        functools.partial(temporal_grad_body, sizes, min(4, sizes.pairs)),
        struct((packed_rows(channels, sizes), 128), F32),
        [pltpu.VMEM((channels, 3 * sizes.edge), F32)],
        flops=CONV_COST // 3,
    )(tact, cot, before, after)

    devices = lax.axis_size("dp") * seqs * cols
    used = packed_rows(3 * channels, sizes) + packed_rows(channels, sizes)
    all_rows = -(-used // (16 * devices)) * 16 * devices
    half = all_rows // 2
    dtemp, dspat, keep, send = call(
        functools.partial(spatial_grad_body, sizes, clip_entries, seqs),
        [
            struct((sizes.pixels, width), BF16),
            struct((sizes.pixels, sizes.padded), BF16),
            struct((half, 128), F32),
            struct((half, 128), BF16),
        ],
        [
            padded_scratch,
            pltpu.VMEM((3 * channels, 3 * sizes.edge), F32),
            pltpu.VMEM((all_rows, 128), F32),
        ],
        flops=CONV_COST,
    )(hidden, cot, tgrad, rims, act, temporal_grad, *clips, *means)
    dnormed, mine = call(
        functools.partial(backward_body, sizes, frame_entries, min(4, sizes.pairs)),
        [struct((sizes.pixels, width), F32), frame_shape],
        [padded_scratch, pltpu.VMEM((2 * frames, 8, sizes.pair), F32)]
        + [pltpu.VMEM((sizes.edge, 3 * sizes.window), BF16)] * 2,
        flops=CONV_COST,
    )(x, sums, other, dspat, spatial_kernel)
    total = keep + swap(send, "col", 1).astype(F32)
    total, (dnormed, mine) = scattered(total, "dp", (dnormed, mine))
    total, _ = scattered(total, "seq")
    theirs = swap(mine, "col", 1)
    grad_latents = call(
        functools.partial(finish_body, sizes, frame_entries), struct((sizes.pixels, width), F32),
        flops=CONV_COST // 3,
    )(x, sums, other, cot, dtemp, dnormed, mine, theirs)
    parts = from_all(gathered(total.astype(BF16), "seq"), "dp")
    parts[1], grad_latents = lax.optimization_barrier((parts[1], grad_latents))
    others = [swap(part, "col", 1) for part in parts]
    spatial_grad, temporal_grad = call(
        functools.partial(unpack_body, sizes, grad_scale, len(parts)),
        [struct((9 * channels, channels), F32), struct((3 * channels, channels), F32)],
        [pltpu.VMEM((all_rows, 128), BF16)],
        flops=CONV_COST // 4,
    )(*parts, *others)

    return (
        grad_latents.reshape(latents.shape),
        spatial_grad.reshape(spatial_kernel.shape),
        temporal_grad.reshape(temporal_kernel.shape),
    )


def solution(mesh):
    in_specs = (P("dp", "seq", None, "col"), P(), P(), P("dp", "seq", None, "col"))
    out_specs = (P("dp", "seq", None, "col"), P(), P())
    return jax.shard_map(shards, mesh=mesh, in_specs=in_specs, out_specs=out_specs, check_vma=False)
```

```python
import functools
import math

import jax
import jax.numpy as jnp
from jax import lax
from jax.experimental import pallas as pl
from jax.experimental.pallas import tpu as pltpu
from jax.sharding import PartitionSpec as P

GROUPS = 32
EPSILON = 1e-05
F32 = jnp.float32
BF16 = jnp.bfloat16
VMEM_LIMIT = 20 * 1024 * 1024
CONV_COST = 12_000_000_000


def call(body, outs, scratch=(), flops=0, moved=0):
    return pl.pallas_call(
        body,
        out_shape=outs,
        out_specs=jax.tree.map(lambda _: pl.BlockSpec(memory_space=pltpu.VMEM), outs),
        scratch_shapes=list(scratch),
        compiler_params=pltpu.CompilerParams(vmem_limit_bytes=VMEM_LIMIT),
        cost_estimate=pl.CostEstimate(flops=flops, bytes_accessed=moved, transcendentals=0),
    )


def struct(shape, kind):
    return jax.ShapeDtypeStruct(shape, kind)


class Sizes:
    def __init__(self, frames, rows, columns, channels):
        self.frames = frames
        self.rows = rows
        self.columns = columns
        self.channels = channels
        self.pixels = frames * rows
        self.width = columns * channels
        self.pair = 2 * channels
        self.pairs = columns // 2
        self.edge = -(-channels // 128) * 128
        self.slack = self.edge - channels
        self.window = 3 * channels + self.slack
        self.padded = self.width + 2 * self.edge


def group_totals(sums, sizes):
    size = sizes.channels // GROUPS

    def member(shape, lane_dim):
        lane = lax.broadcasted_iota(jnp.int32, shape, lane_dim)
        group = lax.broadcasted_iota(jnp.int32, shape, 1 - lane_dim)
        channel = jnp.where(lane >= sizes.channels, lane - sizes.channels, lane)
        return ((channel >= group * size) & (channel < group * size + size)).astype(F32)

    high = lax.Precision.HIGHEST
    by_group = jnp.dot(sums, member((sizes.pair, 128), 0), precision=high, preferred_element_type=F32)
    return jnp.dot(by_group, member((128, sizes.pair), 1), precision=high, preferred_element_type=F32)


def moments(sums, half, entries, sizes):
    totals = group_totals(sums, sizes) * (1.0 / entries)
    mean = totals[0:half]
    rate = lax.rsqrt(totals[half : 2 * half] - mean * mean + EPSILON)
    return mean, rate


def fold(values):
    return jnp.sum(values.reshape(values.shape[0] // 8, 8, values.shape[1]), axis=0)


def pair_lanes(p, sizes):
    return pl.ds(pl.multiple_of(p * sizes.pair, 128), sizes.pair)


def join(even, odd, sizes):
    cut = sizes.edge - 128
    middle = even[:, cut:] + odd[:, :128]
    return jnp.concatenate([even[:, :cut], middle, odd[:, 128:]], axis=1)


def latent_sums_body(sizes, x_ref, sums_ref, edge_ref):
    def frame(f):
        rows = pl.ds(f * sizes.rows, sizes.rows)

        def step(p, carry):
            plain, square = carry
            v = x_ref[rows, pair_lanes(p, sizes)].astype(F32)
            return plain + fold(v), square + fold(v * v)

        zero = jnp.zeros((8, sizes.pair), F32)
        plain, square = lax.fori_loop(0, sizes.pairs, step, (zero, zero))
        return jnp.sum(plain, axis=0, keepdims=True), jnp.sum(square, axis=0, keepdims=True)

    found = [frame(f) for f in range(sizes.frames)]
    for f, (plain, square) in enumerate(found):
        sums_ref[f : f + 1, :] = plain
        sums_ref[sizes.frames + f : sizes.frames + f + 1, :] = square
    store_edge(sizes, x_ref, edge_ref)


def store_edge(sizes, source, target, at=0):
    left = lax.axis_index("col") == 0
    rows = pl.ds(at, sizes.pixels)

    @pl.when(left)
    def _():
        target[rows, :] = source[:, sizes.width - sizes.edge : sizes.width].astype(target.dtype)

    @pl.when(jnp.logical_not(left))
    def _():
        target[rows, :] = source[:, 0 : sizes.edge].astype(target.dtype)


def row_shifts(values, sizes):
    row = lax.broadcasted_iota(jnp.int32, values.shape, 0)
    down = jnp.where(row == 0, 0.0, pltpu.roll(values, 1, 0))
    up = jnp.where(row == sizes.rows - 1, 0.0, pltpu.roll(values, sizes.rows - 1, 0))
    return down, values, up


def put_shifts(values, frame, lanes, target, sizes):
    rows = pl.ds(frame * sizes.rows, sizes.rows)
    for i, moved in enumerate(row_shifts(values, sizes)):
        target[i, rows, lanes] = moved.astype(BF16)


def put_halo(of_frame, target, sizes):
    left = lax.axis_index("col") == 0
    for f in range(sizes.frames):
        rows = pl.ds(f * sizes.rows, sizes.rows)
        before, after = of_frame(rows, f, True), of_frame(rows, f, False)
        put_shifts(jnp.where(left, 0.0, before), f, pl.ds(0, sizes.edge), target, sizes)
        put_shifts(
            jnp.where(left, after, 0.0), f, pl.ds(sizes.edge + sizes.width, sizes.edge), target, sizes
        )


def forward_weights(kernel_ref, even_ref, odd_ref, sizes):
    channels, slack, window = sizes.channels, sizes.slack, sizes.window
    for weights in (even_ref, odd_ref):
        weights[...] = jnp.zeros(weights.shape, BF16)
    for i in range(3):
        for j in range(3):
            taps = kernel_ref[i, j]
            zeros = jnp.zeros((channels, slack), BF16)
            at = i * window + j * channels
            even_ref[at + slack : at + slack + channels, :] = jnp.concatenate([taps, zeros], axis=1)
            odd_ref[at : at + channels, :] = jnp.concatenate([zeros, taps], axis=1)


def backward_weights(kernel_ref, even_ref, odd_ref, sizes):
    channels, slack, window = sizes.channels, sizes.slack, sizes.window
    for weights in (even_ref, odd_ref):
        weights[...] = jnp.zeros(weights.shape, BF16)
    zeros = jnp.zeros((channels, slack), BF16)
    for i in range(3):
        taps = [kernel_ref[2 - i, 2 - j] for j in range(3)]
        lanes = slice(i * window, (i + 1) * window)
        even_ref[0:channels, lanes] = jnp.concatenate([zeros] + taps, axis=1)
        odd_ref[slack : slack + channels, lanes] = jnp.concatenate(taps + [zeros], axis=1)


def temporal_weights(kernel_ref, even_ref, odd_ref, sizes):
    channels, slack, edge = sizes.channels, sizes.slack, sizes.edge
    for weights in (even_ref, odd_ref):
        weights[...] = jnp.zeros(weights.shape, BF16)
    zeros = jnp.zeros((channels, slack), BF16)
    for i in range(3):
        lanes = slice(i * edge, (i + 1) * edge)
        even_ref[0:channels, lanes] = jnp.concatenate([kernel_ref[i], zeros], axis=1)
        odd_ref[slack : slack + channels, lanes] = jnp.concatenate([zeros, kernel_ref[i]], axis=1)


def windows(padded_ref, p, count, odd, sizes):
    found = []
    for q in range(count):
        start = pl.multiple_of((p + q) * sizes.pair, 128) + (sizes.edge if odd else 0)
        lanes = pl.ds(pl.multiple_of(start, 128), sizes.window)
        found.append(jnp.concatenate([padded_ref[i, :, lanes] for i in range(3)], axis=1))
    return jnp.concatenate(found, axis=0)


def silu_parts(v):
    s = 1.0 / (1.0 + jnp.exp(-v))
    return v * s, s


def forward_body(
    sizes, frame_entries, block, x_ref, sums_ref, other_ref, rim_ref, kernel_ref,
    hidden_ref, act_ref, clip_ref, padded, even_ref, odd_ref,
):
    forward_weights(kernel_ref, even_ref, odd_ref, sizes)
    mean, rate = moments(sums_ref[...] + other_ref[...], sizes.frames, frame_entries, sizes)

    def rim(rows, f, before):
        lanes = slice(sizes.pair - sizes.edge, sizes.pair) if before else slice(0, sizes.edge)
        v = rim_ref[rows, :].astype(F32)
        return silu_parts((v - mean[f : f + 1, lanes]) * rate[f : f + 1, lanes])[0]

    put_halo(rim, padded, sizes)

    def activate(p, _):
        for f in range(sizes.frames):
            v = x_ref[pl.ds(f * sizes.rows, sizes.rows), pair_lanes(p, sizes)].astype(F32)
            act = silu_parts((v - mean[f : f + 1]) * rate[f : f + 1])[0]
            lanes = pl.ds(pl.multiple_of(p * sizes.pair + sizes.edge, 128), sizes.pair)
            put_shifts(act, f, lanes, padded, sizes)
        return 0

    lax.fori_loop(0, sizes.pairs, activate, 0)
    act_ref[...] = padded[1]

    def step(b, carry):
        plain, square = carry
        p = b * block
        even = jnp.dot(windows(padded, p, block, False, sizes), even_ref[...], preferred_element_type=F32)
        odd = jnp.dot(windows(padded, p, block, True, sizes), odd_ref[...], preferred_element_type=F32)
        for q in range(block):
            rows = slice(q * sizes.pixels, (q + 1) * sizes.pixels)
            spatial = join(even[rows], odd[rows], sizes)
            lanes = pair_lanes(p + q, sizes)
            hidden = (x_ref[:, lanes].astype(F32) + spatial).astype(BF16)
            hidden_ref[:, lanes] = hidden
            wide = hidden.astype(F32)
            plain = plain + fold(wide)
            square = square + fold(wide * wide)
        return plain, square

    zero = jnp.zeros((8, sizes.pair), F32)
    plain, square = lax.fori_loop(0, sizes.pairs // block, step, (zero, zero))
    put_sums(clip_ref, plain, square)


def add_up(refs):
    total = refs[0][...]
    for ref in refs[1:]:
        total = total + ref[...]
    return total


def put_sums(target, plain, square):
    target[...] = jnp.zeros(target.shape, F32)
    target[0:1, :] = jnp.sum(plain, axis=0, keepdims=True)
    target[1:2, :] = jnp.sum(square, axis=0, keepdims=True)


def frame_taps(cot_ref, before_ref, after_ref, lanes, sizes):
    own = cot_ref[:, lanes]
    later = jnp.concatenate([own[sizes.rows :], after_ref[:, lanes]], axis=0)
    earlier = jnp.concatenate([before_ref[:, lanes], own[: sizes.pixels - sizes.rows]], axis=0)
    return later, own, earlier


def activation_grad_body(sizes, block, cot_ref, before_ref, after_ref, kernel_ref, dact_ref, even_ref, odd_ref):
    temporal_weights(kernel_ref, even_ref, odd_ref, sizes)

    def step(b, _):
        p = b * block
        found = []
        for odd, weights in ((False, even_ref), (True, odd_ref)):
            rows = []
            for q in range(block):
                start = (p + q) * sizes.pair + (sizes.pair - sizes.edge if odd else 0)
                lanes = pl.ds(pl.multiple_of(start, 128), sizes.edge)
                rows.append(
                    jnp.concatenate(frame_taps(cot_ref, before_ref, after_ref, lanes, sizes), axis=1)
                )
            found.append(
                lax.dot_general(
                    jnp.concatenate(rows, axis=0), weights[...], (((1,), (1,)), ((), ())),
                    preferred_element_type=F32,
                )
            )
        for q in range(block):
            rows = slice(q * sizes.pixels, (q + 1) * sizes.pixels)
            dact_ref[:, pair_lanes(p + q, sizes)] = join(found[0][rows], found[1][rows], sizes)
        return 0

    lax.fori_loop(0, sizes.pairs // block, step, 0)


def temporal_body(
    sizes, clip_entries, terms, hidden_ref, cot_ref, dact_ref, *refs
):
    clips, (act_ref, grad_ref, sums_ref, rim_ref, normed) = refs[:terms], refs[terms:]
    mean, rate = moments(add_up(clips), 1, clip_entries, sizes)

    def step(p, carry):
        plain, cross = carry
        lanes = pair_lanes(p, sizes)
        for f in range(sizes.frames):
            rows = pl.ds(f * sizes.rows, sizes.rows)
            tnormed = (hidden_ref[rows, lanes].astype(F32) - mean) * rate
            act, s = silu_parts(tnormed)
            act_ref[rows, lanes] = act.astype(BF16)
            normed[rows, lanes] = tnormed
            grad = dact_ref[rows, lanes] * (s * (1.0 + tnormed * (1.0 - s)))
            grad_ref[rows, lanes] = grad
            plain = plain + fold(grad)
            cross = cross + fold(grad * tnormed)
        return plain, cross

    zero = jnp.zeros((8, sizes.pair), F32)
    plain, cross = lax.fori_loop(0, sizes.pairs, step, (zero, zero))
    put_sums(sums_ref, plain, cross)
    for k, source in enumerate((grad_ref, normed, cot_ref)):
        store_edge(sizes, source, rim_ref, k * sizes.pixels)


def pack(total, target, at, sizes):
    rows, channels = total.shape[0], sizes.channels
    full = channels // 128
    count = 3 * rows
    for i in range(3):
        for k in range(full):
            lanes = slice(i * sizes.edge + k * 128, i * sizes.edge + (k + 1) * 128)
            target[at + k * count + i * rows : at + k * count + (i + 1) * rows, :] = total[:, lanes]
    ends = jnp.concatenate([total[:, i * sizes.edge + full * 128 : (i + 1) * sizes.edge] for i in range(3)], axis=0)
    half = count // 2
    target[at + full * count : at + full * count + half, :] = jnp.concatenate(
        [ends[:half, : 128 - sizes.slack], ends[half:, : 128 - sizes.slack]], axis=1
    )


def packed_rows(rows, sizes):
    return 3 * rows * sizes.channels // 128


def temporal_grad_body(sizes, block, act_ref, cot_ref, before_ref, after_ref, out_ref, total):
    total[...] = jnp.zeros(total.shape, F32)
    channels = sizes.channels
    zeros = jnp.zeros((sizes.pixels, sizes.slack), BF16)

    def step(b, _):
        acts, cots = [], []
        for q in range(block):
            lanes = pair_lanes(b * block + q, sizes)
            act = act_ref[:, lanes]
            acts += [act[:, :channels], act[:, channels:]]
            taps = frame_taps(cot_ref, before_ref, after_ref, lanes, sizes)
            for part in (slice(0, channels), slice(channels, 2 * channels)):
                cots.append(
                    jnp.concatenate([jnp.concatenate([t[:, part], zeros], axis=1) for t in taps], axis=1)
                )
        total[...] += lax.dot_general(
            jnp.concatenate(acts, axis=0), jnp.concatenate(cots, axis=0), (((0,), (0,)), ((), ())),
            preferred_element_type=F32,
        )
        return 0

    lax.fori_loop(0, sizes.pairs // block, step, 0)
    pack(total, out_ref, 0, sizes)


def spatial_grad_body(
    sizes, clip_entries, terms, hidden_ref, cot_ref, grad_ref, rim_ref, act_ref, time_ref, *refs
):
    clips, sums = refs[:terms], refs[terms : 2 * terms]
    dtemp_ref, dspat_ref = refs[2 * terms : 2 * terms + 2]
    chunks, (padded, total, packed) = refs[2 * terms + 2 : -3], refs[-3:]
    count = len(chunks) // 2
    mean, rate = moments(add_up(clips), 1, clip_entries, sizes)
    means = group_totals(add_up(sums), sizes) * (1.0 / clip_entries)
    plain, cross = means[0:1], means[1:2]

    def rim(rows, f, before):
        lanes = slice(sizes.pair - sizes.edge, sizes.pair) if before else slice(0, sizes.edge)
        at = [pl.ds(k * sizes.pixels + f * sizes.rows, sizes.rows) for k in range(3)]
        grad, tnormed, cot = (rim_ref[r, :] for r in at)
        dtemp = rate[:, lanes] * (grad - plain[:, lanes] - tnormed * cross[:, lanes])
        return (cot + dtemp.astype(BF16).astype(F32)).astype(BF16).astype(F32)

    put_halo(rim, padded, sizes)

    def combine(p, _):
        lanes = pair_lanes(p, sizes)
        for f in range(sizes.frames):
            rows = pl.ds(f * sizes.rows, sizes.rows)
            tnormed = (hidden_ref[rows, lanes].astype(F32) - mean) * rate
            dtemp = (rate * (grad_ref[rows, lanes] - plain - tnormed * cross)).astype(BF16)
            dtemp_ref[rows, lanes] = dtemp
            dspat = cot_ref[rows, lanes].astype(F32) + dtemp.astype(F32)
            put_shifts(
                dspat, f, pl.ds(pl.multiple_of(p * sizes.pair + sizes.edge, 128), sizes.pair), padded, sizes
            )
        return 0

    lax.fori_loop(0, sizes.pairs, combine, 0)
    dspat_ref[...] = padded[1]

    channels = sizes.channels
    zeros = jnp.zeros((sizes.pixels, sizes.slack), BF16)
    total[...] = jnp.zeros(total.shape, F32)

    block = min(4, sizes.pairs)

    def step(b, _):
        for odd in (False, True):
            left, right = [], []
            for q in range(block):
                p = block * b + q
                start = p * sizes.pair + (sizes.edge if odd else 0)
                left.append(act_ref[:, pl.ds(pl.multiple_of(start, 128), sizes.window)])
                both = pl.ds(pl.multiple_of(p * sizes.pair + sizes.edge, 128), sizes.pair)
                taps = []
                for i in range(3):
                    d = padded[2 - i, :, both]
                    d = d[:, channels:] if odd else d[:, :channels]
                    taps.append(jnp.concatenate([d, zeros], axis=1))
                right.append(jnp.concatenate(taps, axis=1))
            part = lax.dot_general(
                jnp.concatenate(left, axis=0), jnp.concatenate(right, axis=0), (((0,), (0,)), ((), ())),
                preferred_element_type=F32,
            )
            total[...] += part[: 3 * channels] if odd else part[sizes.slack :]
        return 0

    lax.fori_loop(0, sizes.pairs // block, step, 0)
    pack(total, packed, 0, sizes)
    own = packed_rows(3 * channels, sizes)
    packed[own : own + time_ref.shape[0], :] = time_ref[...]
    used = own + time_ref.shape[0]
    packed[used:, :] = jnp.zeros((packed.shape[0] - used, 128), F32)
    core = lax.axis_index("col")
    for n in range(count):
        keep_ref, send_ref = chunks[n], chunks[count + n]
        keep_ref[...] = packed[chunk_rows(core, n, packed.shape[0], count), :]
        send_ref[...] = packed[chunk_rows(1 - core, n, packed.shape[0], count), :].astype(BF16)


def backward_body(
    sizes, frame_entries, block, x_ref, sums_ref, other_ref, dspat_ref, kernel_ref,
    grad_ref, out_ref, padded, plains, even_ref, odd_ref,
):
    backward_weights(kernel_ref, even_ref, odd_ref, sizes)
    mean, rate = moments(sums_ref[...] + other_ref[...], sizes.frames, frame_entries, sizes)

    def spread(k, _):
        lanes = pl.ds(pl.multiple_of(k * 128, 128), 128)
        for f in range(sizes.frames):
            rows = pl.ds(f * sizes.rows, sizes.rows)
            put_shifts(dspat_ref[rows, lanes].astype(F32), f, lanes, padded, sizes)
        return 0

    lax.fori_loop(0, sizes.padded // 128, spread, 0)
    plains[...] = jnp.zeros(plains.shape, F32)
    contract = (((1,), (1,)), ((), ()))

    def step(b, _):
        p = b * block
        even = lax.dot_general(
            windows(padded, p, block, False, sizes), even_ref[...], contract, preferred_element_type=F32
        )
        odd = lax.dot_general(
            windows(padded, p, block, True, sizes), odd_ref[...], contract, preferred_element_type=F32
        )
        for q in range(block):
            base = q * sizes.pixels
            for f in range(sizes.frames):
                at = slice(base + f * sizes.rows, base + (f + 1) * sizes.rows)
                dact = join(even[at], odd[at], sizes)
                rows, lanes = pl.ds(f * sizes.rows, sizes.rows), pair_lanes(p + q, sizes)
                normed = (x_ref[rows, lanes].astype(F32) - mean[f : f + 1]) * rate[f : f + 1]
                _, s = silu_parts(normed)
                grad = dact * (s * (1.0 + normed * (1.0 - s)))
                grad_ref[rows, lanes] = grad
                plains[f] += fold(grad)
                plains[sizes.frames + f] += fold(grad * normed)
        return 0

    lax.fori_loop(0, sizes.pairs // block, step, 0)
    for k in range(2 * sizes.frames):
        out_ref[k : k + 1, :] = jnp.sum(plains[k], axis=0, keepdims=True)


def finish_body(
    sizes, frame_entries, x_ref, sums_ref, other_ref, cot_ref, dtemp_ref, grad_ref, mine_ref, theirs_ref, out_ref
):
    mean, rate = moments(sums_ref[...] + other_ref[...], sizes.frames, frame_entries, sizes)
    means = group_totals(mine_ref[...] + theirs_ref[...], sizes) * (1.0 / frame_entries)

    def step(p, _):
        lanes = pair_lanes(p, sizes)
        for f in range(sizes.frames):
            rows = pl.ds(f * sizes.rows, sizes.rows)
            normed = (x_ref[rows, lanes].astype(F32) - mean[f : f + 1]) * rate[f : f + 1]
            dhidden = cot_ref[rows, lanes].astype(F32) + dtemp_ref[rows, lanes].astype(F32)
            plain, cross = means[f : f + 1], means[sizes.frames + f : sizes.frames + f + 1]
            out_ref[rows, lanes] = dhidden + rate[f : f + 1] * (grad_ref[rows, lanes] - plain - normed * cross)
        return 0

    lax.fori_loop(0, sizes.pairs, step, 0)


PHASES = ("dp", "seq")


def crossed():
    return lax.axis_size("col") == 2 and lax.axis_size("dp") == lax.axis_size("seq")


def place_of(core, phase):
    place = lax.axis_index(PHASES[phase])
    if crossed():
        place = jnp.where(core == 0, place, lax.axis_index(PHASES[1 - phase]))
    return place


def exchange(values, phase, bits):
    names = ("dp", "seq", "col")
    dps, seqs, cols = (lax.axis_size(name) for name in names)
    pairs = []
    for i in range(dps * seqs * cols):
        place = [i // (seqs * cols), i // cols % seqs, i % cols]
        place[phase ^ place[2] if crossed() else phase] ^= bits
        pairs.append((i, (place[0] * seqs + place[1]) * cols + place[2]))
    return lax.ppermute(values, names, pairs)


def chunk_rows(core, bits, rows, count):
    chunk = rows // 2 // count
    start = core * (rows // 2) + (place_of(core, 0) ^ bits) * chunk
    return pl.ds(pl.multiple_of(start, 16), chunk)


def unpack_body(sizes, scale, parts, *refs):
    mine, theirs = refs[:parts], refs[parts : 2 * parts]
    spatial_ref, temporal_ref, packed = refs[2 * parts :]
    core = lax.axis_index("col")
    for n in range(parts):
        packed[chunk_rows(core, n, packed.shape[0], parts), :] = mine[n][...]
        packed[chunk_rows(1 - core, n, packed.shape[0], parts), :] = theirs[n][...]
    full = sizes.channels // 128
    at = 0
    for target in (spatial_ref, temporal_ref):
        count = target.shape[0]
        tile = math.gcd(count // 2, 240)

        def step(k, _, at=at, target=target, count=count, tile=tile):
            for second in range(2):
                row = pl.multiple_of(k * tile, 16) + second * (count // 2)
                found = [
                    packed[pl.ds(pl.multiple_of(at + b * count + row, 16), tile), :].astype(F32) for b in range(full)
                ]
                ends = packed[pl.ds(pl.multiple_of(at + full * count + k * tile, 16), tile), :].astype(F32)
                cut = 128 - sizes.slack
                found.append(ends[:, cut:] if second else ends[:, :cut])
                target[pl.ds(pl.multiple_of(row, 16), tile), :] = jnp.concatenate(found, axis=1) * scale
            return 0

        lax.fori_loop(0, count // 2 // tile, step, 0)
        at += count * sizes.channels // 128


def swap(values, axis, bit):
    count = lax.axis_size(axis)
    return lax.ppermute(values, axis, [(i, i ^ bit) for i in range(count)])


def from_all(values, axis):
    return [values] + [swap(values, axis, s) for s in range(1, lax.axis_size(axis))]


def added(terms):
    total = terms[0].astype(F32)
    for term in terms[1:]:
        total = total + term.astype(F32)
    return total


def scattered(total, phase):
    count = lax.axis_size(PHASES[phase])
    rows = total.shape[0] // count
    place = place_of(lax.axis_index("col"), phase)
    chunks = [lax.dynamic_slice_in_dim(total, (place ^ n) * rows, rows, 0) for n in range(count)]
    return added(chunks[:1] + [exchange(chunks[n].astype(BF16), phase, n) for n in range(1, count)])


def gathered(chunk, phase):
    count = lax.axis_size(PHASES[phase])
    parts = [chunk] + [exchange(chunk, phase, n) for n in range(1, count)]
    place = place_of(lax.axis_index("col"), phase)
    rows = chunk.shape[0]
    out = jnp.zeros((rows * count, chunk.shape[1]), chunk.dtype)
    for n, part in enumerate(parts):
        out = lax.dynamic_update_slice_in_dim(out, part, (place ^ n) * rows, 0)
    return out


def shards(latents, spatial_kernel, temporal_kernel, cotangent):
    _, frames, rows, width = latents.shape
    channels = spatial_kernel.shape[2]
    sizes = Sizes(frames, rows, width // channels, channels)
    cols, seqs = lax.axis_size("col"), lax.axis_size("seq")
    frame_entries = float(rows * sizes.columns * cols * (channels // GROUPS))
    clip_entries = frame_entries * frames * seqs
    pixels = lax.axis_size("dp") * seqs * cols * sizes.pixels * sizes.columns
    grad_scale = 1.0 / math.sqrt(pixels)

    x = latents.reshape(sizes.pixels, width)
    cot = cotangent.reshape(sizes.pixels, width)
    sum_shape = struct((8, sizes.pair), F32)
    frame_shape = struct((2 * frames, sizes.pair), F32)
    padded_scratch = pltpu.VMEM((3, sizes.pixels, sizes.padded), BF16)
    slack = sizes.slack

    forth = [(i, i + 1) for i in range(seqs - 1)]
    before = lax.ppermute(cot[sizes.pixels - rows :], "seq", forth)
    after = lax.ppermute(cot[:rows], "seq", [(j, i) for i, j in forth])

    sums, edge = call(
        functools.partial(latent_sums_body, sizes),
        [frame_shape, struct((sizes.pixels, sizes.edge), BF16)],
    )(x)
    other = swap(sums, "col", 1)
    rim = swap(edge, "col", 1)
    window_weights = [pltpu.VMEM((3 * sizes.window, sizes.edge), BF16)] * 2
    hidden, act, clip = call(
        functools.partial(forward_body, sizes, frame_entries, min(4, sizes.pairs)),
        [struct((sizes.pixels, width), BF16), struct((sizes.pixels, sizes.padded), BF16), sum_shape],
        [padded_scratch] + window_weights,
        flops=CONV_COST,
    )(x, sums, other, rim, spatial_kernel)
    clips = from_all(clip + swap(clip, "col", 1), "seq")
    dact = call(
        functools.partial(activation_grad_body, sizes, min(4, sizes.pairs)),
        struct((sizes.pixels, width), F32),
        [pltpu.VMEM((sizes.edge, 3 * sizes.edge), BF16)] * 2,
        flops=CONV_COST // 3,
    )(cot, before, after, temporal_kernel)
    tact, tgrad, means, rims = call(
        functools.partial(temporal_body, sizes, clip_entries, seqs),
        [
            struct((sizes.pixels, width), BF16),
            struct((sizes.pixels, width), F32),
            sum_shape,
            struct((3 * sizes.pixels, sizes.edge), F32),
        ],
        [pltpu.VMEM((sizes.pixels, width), F32)],
        flops=CONV_COST // 3,
    )(hidden, cot, dact, *clips)
    means = from_all(means + swap(means, "col", 1), "seq")
    rims = swap(rims, "col", 1)
    temporal_grad = call(
        functools.partial(temporal_grad_body, sizes, min(4, sizes.pairs)),
        struct((packed_rows(channels, sizes), 128), F32),
        [pltpu.VMEM((channels, 3 * sizes.edge), F32)],
        flops=CONV_COST // 3,
    )(tact, cot, before, after)

    devices = lax.axis_size("dp") * seqs * cols
    used = packed_rows(3 * channels, sizes) + packed_rows(channels, sizes)
    all_rows = -(-used // (16 * devices)) * 16 * devices
    count = lax.axis_size(PHASES[0])
    chunk = (all_rows // 2 // count, 128)
    dtemp, dspat, *chunks = call(
        functools.partial(spatial_grad_body, sizes, clip_entries, seqs),
        [
            struct((sizes.pixels, width), BF16),
            struct((sizes.pixels, sizes.padded), BF16),
        ]
        + [struct(chunk, F32)] * count
        + [struct(chunk, BF16)] * count,
        [
            padded_scratch,
            pltpu.VMEM((3 * channels, 3 * sizes.edge), F32),
            pltpu.VMEM((all_rows, 128), F32),
        ],
        flops=CONV_COST,
    )(hidden, cot, tgrad, rims, act, temporal_grad, *clips, *means)
    dnormed, mine = call(
        functools.partial(backward_body, sizes, frame_entries, min(4, sizes.pairs)),
        [struct((sizes.pixels, width), F32), frame_shape],
        [padded_scratch, pltpu.VMEM((2 * frames, 8, sizes.pair), F32)]
        + [pltpu.VMEM((sizes.edge, 3 * sizes.window), BF16)] * 2,
        flops=CONV_COST,
    )(x, sums, other, dspat, spatial_kernel)
    chunks = [chunks[n] + swap(chunks[count + n], "col", 1).astype(F32) for n in range(count)]
    found = [exchange(chunks[n].astype(BF16), 0, n) for n in range(1, count)]
    found, (dnormed, mine) = lax.optimization_barrier((found, (dnormed, mine)))
    total = scattered(added(chunks[:1] + found), 1)
    theirs = swap(mine, "col", 1)
    grad_latents = call(
        functools.partial(finish_body, sizes, frame_entries), struct((sizes.pixels, width), F32),
        flops=CONV_COST // 3,
    )(x, sums, other, cot, dtemp, dnormed, mine, theirs)
    part = gathered(total.astype(BF16), 1)
    parts = [part] + [exchange(part, 0, n) for n in range(1, count)]
    parts[1], grad_latents = lax.optimization_barrier((parts[1], grad_latents))
    others = [swap(part, "col", 1) for part in parts]
    spatial_grad, temporal_grad = call(
        functools.partial(unpack_body, sizes, grad_scale, len(parts)),
        [struct((9 * channels, channels), F32), struct((3 * channels, channels), F32)],
        [pltpu.VMEM((all_rows, 128), BF16)],
        flops=CONV_COST // 4,
    )(*parts, *others)

    return (
        grad_latents.reshape(latents.shape),
        spatial_grad.reshape(spatial_kernel.shape),
        temporal_grad.reshape(temporal_kernel.shape),
    )


def solution(mesh):
    in_specs = (P("dp", "seq", None, "col"), P(), P(), P("dp", "seq", None, "col"))
    out_specs = (P("dp", "seq", None, "col"), P(), P())
    return jax.shard_map(shards, mesh=mesh, in_specs=in_specs, out_specs=out_specs, check_vma=False)
```

```python
import functools
import math

import jax
import jax.numpy as jnp
from jax import lax
from jax.experimental import pallas as pl
from jax.experimental.pallas import tpu as pltpu
from jax.sharding import PartitionSpec as P

GROUPS = 32
EPSILON = 1e-05
F32 = jnp.float32
BF16 = jnp.bfloat16
VMEM_LIMIT = 20 * 1024 * 1024
SMALL_LIMIT = 4 * 1024 * 1024
CONV_COST = 12_000_000_000


def call(body, outs, scratch=(), flops=0, moved=0, limit=VMEM_LIMIT):
    return pl.pallas_call(
        body,
        out_shape=outs,
        out_specs=jax.tree.map(lambda _: pl.BlockSpec(memory_space=pltpu.VMEM), outs),
        scratch_shapes=list(scratch),
        compiler_params=pltpu.CompilerParams(vmem_limit_bytes=limit),
        cost_estimate=pl.CostEstimate(flops=flops, bytes_accessed=moved, transcendentals=0),
    )


def struct(shape, kind):
    return jax.ShapeDtypeStruct(shape, kind)


class Sizes:
    def __init__(self, frames, rows, columns, channels):
        self.frames = frames
        self.rows = rows
        self.columns = columns
        self.channels = channels
        self.pixels = frames * rows
        self.width = columns * channels
        self.pair = 2 * channels
        self.pairs = columns // 2
        self.edge = -(-channels // 128) * 128
        self.slack = self.edge - channels
        self.window = 3 * channels + self.slack
        self.padded = self.width + 2 * self.edge


def group_totals(sums, sizes):
    size = sizes.channels // GROUPS

    def member(shape, lane_dim):
        lane = lax.broadcasted_iota(jnp.int32, shape, lane_dim)
        group = lax.broadcasted_iota(jnp.int32, shape, 1 - lane_dim)
        channel = jnp.where(lane >= sizes.channels, lane - sizes.channels, lane)
        return ((channel >= group * size) & (channel < group * size + size)).astype(F32)

    high = lax.Precision.HIGHEST
    by_group = jnp.dot(sums, member((sizes.pair, 128), 0), precision=high, preferred_element_type=F32)
    return jnp.dot(by_group, member((128, sizes.pair), 1), precision=high, preferred_element_type=F32)


def moments(sums, half, entries, sizes):
    totals = group_totals(sums, sizes) * (1.0 / entries)
    mean = totals[0:half]
    rate = lax.rsqrt(totals[half : 2 * half] - mean * mean + EPSILON)
    return mean, rate


def fold(values):
    return jnp.sum(values.reshape(values.shape[0] // 8, 8, values.shape[1]), axis=0)


def pair_lanes(p, sizes):
    return pl.ds(pl.multiple_of(p * sizes.pair, 128), sizes.pair)


def join(even, odd, sizes):
    cut = sizes.edge - 128
    middle = even[:, cut:] + odd[:, :128]
    return jnp.concatenate([even[:, :cut], middle, odd[:, 128:]], axis=1)


def latent_sums_body(sizes, x_ref, sums_ref, edge_ref):
    def frame(f):
        rows = pl.ds(f * sizes.rows, sizes.rows)

        def step(p, carry):
            plain, square = carry
            v = x_ref[rows, pair_lanes(p, sizes)].astype(F32)
            return plain + fold(v), square + fold(v * v)

        zero = jnp.zeros((8, sizes.pair), F32)
        plain, square = lax.fori_loop(0, sizes.pairs, step, (zero, zero))
        return jnp.sum(plain, axis=0, keepdims=True), jnp.sum(square, axis=0, keepdims=True)

    found = [frame(f) for f in range(sizes.frames)]
    for f, (plain, square) in enumerate(found):
        sums_ref[f : f + 1, :] = plain
        sums_ref[sizes.frames + f : sizes.frames + f + 1, :] = square
    store_edge(sizes, x_ref, edge_ref)


def store_edge(sizes, source, target, at=0):
    left = lax.axis_index("col") == 0
    rows = pl.ds(at, sizes.pixels)

    @pl.when(left)
    def _():
        target[rows, :] = source[:, sizes.width - sizes.edge : sizes.width].astype(target.dtype)

    @pl.when(jnp.logical_not(left))
    def _():
        target[rows, :] = source[:, 0 : sizes.edge].astype(target.dtype)


def row_shifts(values, sizes):
    row = lax.broadcasted_iota(jnp.int32, values.shape, 0)
    down = jnp.where(row == 0, 0.0, pltpu.roll(values, 1, 0))
    up = jnp.where(row == sizes.rows - 1, 0.0, pltpu.roll(values, sizes.rows - 1, 0))
    return down, values, up


def put_shifts(values, frame, lanes, target, sizes):
    rows = pl.ds(frame * sizes.rows, sizes.rows)
    for i, moved in enumerate(row_shifts(values, sizes)):
        target[i, rows, lanes] = moved.astype(BF16)


def put_halo(of_frame, target, sizes):
    left = lax.axis_index("col") == 0
    for f in range(sizes.frames):
        rows = pl.ds(f * sizes.rows, sizes.rows)
        before, after = of_frame(rows, f, True), of_frame(rows, f, False)
        put_shifts(jnp.where(left, 0.0, before), f, pl.ds(0, sizes.edge), target, sizes)
        put_shifts(
            jnp.where(left, after, 0.0), f, pl.ds(sizes.edge + sizes.width, sizes.edge), target, sizes
        )


def forward_weights(kernel_ref, even_ref, odd_ref, sizes):
    channels, slack, window = sizes.channels, sizes.slack, sizes.window
    for weights in (even_ref, odd_ref):
        weights[...] = jnp.zeros(weights.shape, BF16)
    for i in range(3):
        for j in range(3):
            taps = kernel_ref[i, j]
            zeros = jnp.zeros((channels, slack), BF16)
            at = i * window + j * channels
            even_ref[at + slack : at + slack + channels, :] = jnp.concatenate([taps, zeros], axis=1)
            odd_ref[at : at + channels, :] = jnp.concatenate([zeros, taps], axis=1)


def backward_weights(kernel_ref, even_ref, odd_ref, sizes):
    channels, slack, window = sizes.channels, sizes.slack, sizes.window
    for weights in (even_ref, odd_ref):
        weights[...] = jnp.zeros(weights.shape, BF16)
    zeros = jnp.zeros((channels, slack), BF16)
    for i in range(3):
        taps = [kernel_ref[2 - i, 2 - j] for j in range(3)]
        lanes = slice(i * window, (i + 1) * window)
        even_ref[0:channels, lanes] = jnp.concatenate([zeros] + taps, axis=1)
        odd_ref[slack : slack + channels, lanes] = jnp.concatenate(taps + [zeros], axis=1)


def temporal_weights(kernel_ref, even_ref, odd_ref, sizes):
    channels, slack, edge = sizes.channels, sizes.slack, sizes.edge
    for weights in (even_ref, odd_ref):
        weights[...] = jnp.zeros(weights.shape, BF16)
    zeros = jnp.zeros((channels, slack), BF16)
    for i in range(3):
        lanes = slice(i * edge, (i + 1) * edge)
        even_ref[0:channels, lanes] = jnp.concatenate([kernel_ref[i], zeros], axis=1)
        odd_ref[slack : slack + channels, lanes] = jnp.concatenate([zeros, kernel_ref[i]], axis=1)


def windows(padded_ref, p, count, odd, sizes):
    found = []
    for q in range(count):
        start = pl.multiple_of((p + q) * sizes.pair, 128) + (sizes.edge if odd else 0)
        lanes = pl.ds(pl.multiple_of(start, 128), sizes.window)
        found.append(jnp.concatenate([padded_ref[i, :, lanes] for i in range(3)], axis=1))
    return jnp.concatenate(found, axis=0)


def silu_parts(v):
    s = 1.0 / (1.0 + jnp.exp(-v))
    return v * s, s


def forward_body(
    sizes, frame_entries, block, x_ref, sums_ref, other_ref, rim_ref, kernel_ref,
    hidden_ref, act_ref, clip_ref, padded, even_ref, odd_ref,
):
    forward_weights(kernel_ref, even_ref, odd_ref, sizes)
    mean, rate = moments(sums_ref[...] + other_ref[...], sizes.frames, frame_entries, sizes)

    def rim(rows, f, before):
        lanes = slice(sizes.pair - sizes.edge, sizes.pair) if before else slice(0, sizes.edge)
        v = rim_ref[rows, :].astype(F32)
        return silu_parts((v - mean[f : f + 1, lanes]) * rate[f : f + 1, lanes])[0]

    put_halo(rim, padded, sizes)

    def activate(p, _):
        for f in range(sizes.frames):
            v = x_ref[pl.ds(f * sizes.rows, sizes.rows), pair_lanes(p, sizes)].astype(F32)
            act = silu_parts((v - mean[f : f + 1]) * rate[f : f + 1])[0]
            lanes = pl.ds(pl.multiple_of(p * sizes.pair + sizes.edge, 128), sizes.pair)
            put_shifts(act, f, lanes, padded, sizes)
        return 0

    lax.fori_loop(0, sizes.pairs, activate, 0)
    act_ref[...] = padded[1]

    def step(b, carry):
        plain, square = carry
        p = b * block
        even = jnp.dot(windows(padded, p, block, False, sizes), even_ref[...], preferred_element_type=F32)
        odd = jnp.dot(windows(padded, p, block, True, sizes), odd_ref[...], preferred_element_type=F32)
        for q in range(block):
            rows = slice(q * sizes.pixels, (q + 1) * sizes.pixels)
            spatial = join(even[rows], odd[rows], sizes)
            lanes = pair_lanes(p + q, sizes)
            hidden = (x_ref[:, lanes].astype(F32) + spatial).astype(BF16)
            hidden_ref[:, lanes] = hidden
            wide = hidden.astype(F32)
            plain = plain + fold(wide)
            square = square + fold(wide * wide)
        return plain, square

    zero = jnp.zeros((8, sizes.pair), F32)
    plain, square = lax.fori_loop(0, sizes.pairs // block, step, (zero, zero))
    put_sums(clip_ref, plain, square)


def add_up(refs):
    total = refs[0][...]
    for ref in refs[1:]:
        total = total + ref[...]
    return total


def put_sums(target, plain, square):
    target[...] = jnp.zeros(target.shape, F32)
    target[0:1, :] = jnp.sum(plain, axis=0, keepdims=True)
    target[1:2, :] = jnp.sum(square, axis=0, keepdims=True)


def frame_taps(cot_ref, before_ref, after_ref, lanes, sizes):
    own = cot_ref[:, lanes]
    later = jnp.concatenate([own[sizes.rows :], after_ref[:, lanes]], axis=0)
    earlier = jnp.concatenate([before_ref[:, lanes], own[: sizes.pixels - sizes.rows]], axis=0)
    return later, own, earlier


def activation_grad_body(sizes, block, cot_ref, before_ref, after_ref, kernel_ref, dact_ref, even_ref, odd_ref):
    temporal_weights(kernel_ref, even_ref, odd_ref, sizes)

    def step(b, _):
        p = b * block
        found = []
        for odd, weights in ((False, even_ref), (True, odd_ref)):
            rows = []
            for q in range(block):
                start = (p + q) * sizes.pair + (sizes.pair - sizes.edge if odd else 0)
                lanes = pl.ds(pl.multiple_of(start, 128), sizes.edge)
                rows.append(
                    jnp.concatenate(frame_taps(cot_ref, before_ref, after_ref, lanes, sizes), axis=1)
                )
            found.append(
                lax.dot_general(
                    jnp.concatenate(rows, axis=0), weights[...], (((1,), (1,)), ((), ())),
                    preferred_element_type=F32,
                )
            )
        for q in range(block):
            rows = slice(q * sizes.pixels, (q + 1) * sizes.pixels)
            dact_ref[:, pair_lanes(p + q, sizes)] = join(found[0][rows], found[1][rows], sizes)
        return 0

    lax.fori_loop(0, sizes.pairs // block, step, 0)


def temporal_body(
    sizes, clip_entries, terms, hidden_ref, cot_ref, dact_ref, *refs
):
    clips, (act_ref, grad_ref, sums_ref, rim_ref, normed) = refs[:terms], refs[terms:]
    mean, rate = moments(add_up(clips), 1, clip_entries, sizes)

    def step(p, carry):
        plain, cross = carry
        lanes = pair_lanes(p, sizes)
        for f in range(sizes.frames):
            rows = pl.ds(f * sizes.rows, sizes.rows)
            tnormed = (hidden_ref[rows, lanes].astype(F32) - mean) * rate
            act, s = silu_parts(tnormed)
            act_ref[rows, lanes] = act.astype(BF16)
            normed[rows, lanes] = tnormed
            grad = dact_ref[rows, lanes] * (s * (1.0 + tnormed * (1.0 - s)))
            grad_ref[rows, lanes] = grad
            plain = plain + fold(grad)
            cross = cross + fold(grad * tnormed)
        return plain, cross

    zero = jnp.zeros((8, sizes.pair), F32)
    plain, cross = lax.fori_loop(0, sizes.pairs, step, (zero, zero))
    put_sums(sums_ref, plain, cross)
    for k, source in enumerate((grad_ref, normed, cot_ref)):
        store_edge(sizes, source, rim_ref, k * sizes.pixels)


def pack(total, target, at, sizes):
    rows, channels = total.shape[0], sizes.channels
    full = channels // 128
    count = 3 * rows
    for i in range(3):
        for k in range(full):
            lanes = slice(i * sizes.edge + k * 128, i * sizes.edge + (k + 1) * 128)
            target[at + k * count + i * rows : at + k * count + (i + 1) * rows, :] = total[:, lanes]
    ends = jnp.concatenate([total[:, i * sizes.edge + full * 128 : (i + 1) * sizes.edge] for i in range(3)], axis=0)
    half = count // 2
    target[at + full * count : at + full * count + half, :] = jnp.concatenate(
        [ends[:half, : 128 - sizes.slack], ends[half:, : 128 - sizes.slack]], axis=1
    )


def packed_rows(rows, sizes):
    return 3 * rows * sizes.channels // 128


def temporal_grad_body(sizes, block, act_ref, cot_ref, before_ref, after_ref, out_ref, total):
    total[...] = jnp.zeros(total.shape, F32)
    channels = sizes.channels
    zeros = jnp.zeros((sizes.pixels, sizes.slack), BF16)

    def step(b, _):
        acts, cots = [], []
        for q in range(block):
            lanes = pair_lanes(b * block + q, sizes)
            act = act_ref[:, lanes]
            acts += [act[:, :channels], act[:, channels:]]
            taps = frame_taps(cot_ref, before_ref, after_ref, lanes, sizes)
            for part in (slice(0, channels), slice(channels, 2 * channels)):
                cots.append(
                    jnp.concatenate([jnp.concatenate([t[:, part], zeros], axis=1) for t in taps], axis=1)
                )
        total[...] += lax.dot_general(
            jnp.concatenate(acts, axis=0), jnp.concatenate(cots, axis=0), (((0,), (0,)), ((), ())),
            preferred_element_type=F32,
        )
        return 0

    lax.fori_loop(0, sizes.pairs // block, step, 0)
    pack(total, out_ref, 0, sizes)


def spatial_grad_body(
    sizes, clip_entries, terms, hidden_ref, cot_ref, grad_ref, rim_ref, act_ref, time_ref, *refs
):
    clips, sums = refs[:terms], refs[terms : 2 * terms]
    dtemp_ref, dspat_ref = refs[2 * terms : 2 * terms + 2]
    chunks, (padded, total, packed) = refs[2 * terms + 2 : -3], refs[-3:]
    count = len(chunks) // 2
    mean, rate = moments(add_up(clips), 1, clip_entries, sizes)
    means = group_totals(add_up(sums), sizes) * (1.0 / clip_entries)
    plain, cross = means[0:1], means[1:2]

    def rim(rows, f, before):
        lanes = slice(sizes.pair - sizes.edge, sizes.pair) if before else slice(0, sizes.edge)
        at = [pl.ds(k * sizes.pixels + f * sizes.rows, sizes.rows) for k in range(3)]
        grad, tnormed, cot = (rim_ref[r, :] for r in at)
        dtemp = rate[:, lanes] * (grad - plain[:, lanes] - tnormed * cross[:, lanes])
        return (cot + dtemp.astype(BF16).astype(F32)).astype(BF16).astype(F32)

    put_halo(rim, padded, sizes)

    def combine(p, _):
        lanes = pair_lanes(p, sizes)
        for f in range(sizes.frames):
            rows = pl.ds(f * sizes.rows, sizes.rows)
            tnormed = (hidden_ref[rows, lanes].astype(F32) - mean) * rate
            dtemp = (rate * (grad_ref[rows, lanes] - plain - tnormed * cross)).astype(BF16)
            dtemp_ref[rows, lanes] = dtemp
            dspat = cot_ref[rows, lanes].astype(F32) + dtemp.astype(F32)
            put_shifts(
                dspat, f, pl.ds(pl.multiple_of(p * sizes.pair + sizes.edge, 128), sizes.pair), padded, sizes
            )
        return 0

    lax.fori_loop(0, sizes.pairs, combine, 0)
    dspat_ref[...] = padded[1]

    channels = sizes.channels
    zeros = jnp.zeros((sizes.pixels, sizes.slack), BF16)
    total[...] = jnp.zeros(total.shape, F32)

    block = min(4, sizes.pairs)

    def step(b, _):
        for odd in (False, True):
            left, right = [], []
            for q in range(block):
                p = block * b + q
                start = p * sizes.pair + (sizes.edge if odd else 0)
                left.append(act_ref[:, pl.ds(pl.multiple_of(start, 128), sizes.window)])
                both = pl.ds(pl.multiple_of(p * sizes.pair + sizes.edge, 128), sizes.pair)
                taps = []
                for i in range(3):
                    d = padded[2 - i, :, both]
                    d = d[:, channels:] if odd else d[:, :channels]
                    taps.append(jnp.concatenate([d, zeros], axis=1))
                right.append(jnp.concatenate(taps, axis=1))
            part = lax.dot_general(
                jnp.concatenate(left, axis=0), jnp.concatenate(right, axis=0), (((0,), (0,)), ((), ())),
                preferred_element_type=F32,
            )
            total[...] += part[: 3 * channels] if odd else part[sizes.slack :]
        return 0

    lax.fori_loop(0, sizes.pairs // block, step, 0)
    pack(total, packed, 0, sizes)
    own = packed_rows(3 * channels, sizes)
    packed[own : own + time_ref.shape[0], :] = time_ref[...]
    used = own + time_ref.shape[0]
    packed[used:, :] = jnp.zeros((packed.shape[0] - used, 128), F32)
    core = lax.axis_index("col")
    for n in range(count):
        keep_ref, send_ref = chunks[n], chunks[count + n]
        keep_ref[...] = packed[chunk_rows(core, n, packed.shape[0], count), :]
        send_ref[...] = packed[chunk_rows(1 - core, n, packed.shape[0], count), :].astype(BF16)


def backward_body(
    sizes, frame_entries, block, x_ref, sums_ref, other_ref, dspat_ref, kernel_ref,
    grad_ref, out_ref, padded, plains, even_ref, odd_ref,
):
    backward_weights(kernel_ref, even_ref, odd_ref, sizes)
    mean, rate = moments(sums_ref[...] + other_ref[...], sizes.frames, frame_entries, sizes)

    def spread(k, _):
        lanes = pl.ds(pl.multiple_of(k * 128, 128), 128)
        for f in range(sizes.frames):
            rows = pl.ds(f * sizes.rows, sizes.rows)
            put_shifts(dspat_ref[rows, lanes].astype(F32), f, lanes, padded, sizes)
        return 0

    lax.fori_loop(0, sizes.padded // 128, spread, 0)
    plains[...] = jnp.zeros(plains.shape, F32)
    contract = (((1,), (1,)), ((), ()))

    def step(b, _):
        p = b * block
        even = lax.dot_general(
            windows(padded, p, block, False, sizes), even_ref[...], contract, preferred_element_type=F32
        )
        odd = lax.dot_general(
            windows(padded, p, block, True, sizes), odd_ref[...], contract, preferred_element_type=F32
        )
        for q in range(block):
            base = q * sizes.pixels
            for f in range(sizes.frames):
                at = slice(base + f * sizes.rows, base + (f + 1) * sizes.rows)
                dact = join(even[at], odd[at], sizes)
                rows, lanes = pl.ds(f * sizes.rows, sizes.rows), pair_lanes(p + q, sizes)
                normed = (x_ref[rows, lanes].astype(F32) - mean[f : f + 1]) * rate[f : f + 1]
                _, s = silu_parts(normed)
                grad = dact * (s * (1.0 + normed * (1.0 - s)))
                grad_ref[rows, lanes] = grad
                plains[f] += fold(grad)
                plains[sizes.frames + f] += fold(grad * normed)
        return 0

    lax.fori_loop(0, sizes.pairs // block, step, 0)
    for k in range(2 * sizes.frames):
        out_ref[k : k + 1, :] = jnp.sum(plains[k], axis=0, keepdims=True)


def finish_body(
    sizes, frame_entries, x_ref, sums_ref, other_ref, cot_ref, dtemp_ref, grad_ref, mine_ref, theirs_ref, out_ref
):
    mean, rate = moments(sums_ref[...] + other_ref[...], sizes.frames, frame_entries, sizes)
    means = group_totals(mine_ref[...] + theirs_ref[...], sizes) * (1.0 / frame_entries)

    def step(p, _):
        lanes = pair_lanes(p, sizes)
        for f in range(sizes.frames):
            rows = pl.ds(f * sizes.rows, sizes.rows)
            normed = (x_ref[rows, lanes].astype(F32) - mean[f : f + 1]) * rate[f : f + 1]
            dhidden = cot_ref[rows, lanes].astype(F32) + dtemp_ref[rows, lanes].astype(F32)
            plain, cross = means[f : f + 1], means[sizes.frames + f : sizes.frames + f + 1]
            out_ref[rows, lanes] = dhidden + rate[f : f + 1] * (grad_ref[rows, lanes] - plain - normed * cross)
        return 0

    lax.fori_loop(0, sizes.pairs, step, 0)


PHASES = ("dp", "seq")


def crossed():
    return lax.axis_size("col") == 2 and lax.axis_size("dp") == lax.axis_size("seq")


def place_of(core, phase):
    place = lax.axis_index(PHASES[phase])
    if crossed():
        place = jnp.where(core == 0, place, lax.axis_index(PHASES[1 - phase]))
    return place


def exchange(values, phase, bits):
    names = ("dp", "seq", "col")
    dps, seqs, cols = (lax.axis_size(name) for name in names)
    pairs = []
    for i in range(dps * seqs * cols):
        place = [i // (seqs * cols), i // cols % seqs, i % cols]
        place[phase ^ place[2] if crossed() else phase] ^= bits
        pairs.append((i, (place[0] * seqs + place[1]) * cols + place[2]))
    return lax.ppermute(values, names, pairs)


def chunk_rows(core, bits, rows, count):
    chunk = rows // 2 // count
    start = core * (rows // 2) + (place_of(core, 0) ^ bits) * chunk
    return pl.ds(pl.multiple_of(start, 16), chunk)


def unpack_body(sizes, scale, parts, *refs):
    mine, theirs = refs[:parts], refs[parts : 2 * parts]
    spatial_ref, temporal_ref, packed = refs[2 * parts :]
    core = lax.axis_index("col")
    for n in range(parts):
        packed[chunk_rows(core, n, packed.shape[0], parts), :] = mine[n][...]
        packed[chunk_rows(1 - core, n, packed.shape[0], parts), :] = theirs[n][...]
    full = sizes.channels // 128
    at = 0
    for target in (spatial_ref, temporal_ref):
        count = target.shape[0]
        tile = math.gcd(count // 2, 240)

        def step(k, _, at=at, target=target, count=count, tile=tile):
            for second in range(2):
                row = pl.multiple_of(k * tile, 16) + second * (count // 2)
                found = [
                    packed[pl.ds(pl.multiple_of(at + b * count + row, 16), tile), :].astype(F32) for b in range(full)
                ]
                ends = packed[pl.ds(pl.multiple_of(at + full * count + k * tile, 16), tile), :].astype(F32)
                cut = 128 - sizes.slack
                found.append(ends[:, cut:] if second else ends[:, :cut])
                target[pl.ds(pl.multiple_of(row, 16), tile), :] = jnp.concatenate(found, axis=1) * scale
            return 0

        lax.fori_loop(0, count // 2 // tile, step, 0)
        at += count * sizes.channels // 128


def swap(values, axis, bit):
    count = lax.axis_size(axis)
    return lax.ppermute(values, axis, [(i, i ^ bit) for i in range(count)])


def from_all(values, axis):
    return [values] + [swap(values, axis, s) for s in range(1, lax.axis_size(axis))]


def added(terms):
    total = terms[0].astype(F32)
    for term in terms[1:]:
        total = total + term.astype(F32)
    return total


def place_rows(phase, bits, rows):
    place = place_of(lax.axis_index("col"), phase)
    return pl.ds(pl.multiple_of((place ^ bits) * rows, 16), rows)


def split_body(phase, terms, *refs):
    for bits, target in enumerate(refs[terms:]):
        rows = place_rows(phase, bits, target.shape[0])
        target[...] = added([ref[rows, :] for ref in refs[:terms]]).astype(target.dtype)


def scattered(terms, phase):
    count = lax.axis_size(PHASES[phase])
    chunk = (terms[0].shape[0] // count, terms[0].shape[1])
    own, *others = call(
        functools.partial(split_body, phase, len(terms)),
        [struct(chunk, F32)] + [struct(chunk, BF16)] * (count - 1),
        limit=SMALL_LIMIT,
    )(*terms)
    return [own] + [exchange(values, phase, n + 1) for n, values in enumerate(others)]


def gather_body(phase, *refs):
    for bits, part in enumerate(refs[:-1]):
        refs[-1][place_rows(phase, bits, part.shape[0]), :] = part[...]


def gathered(chunk, phase):
    count = lax.axis_size(PHASES[phase])
    parts = [chunk] + [exchange(chunk, phase, n) for n in range(1, count)]
    return call(
        functools.partial(gather_body, phase),
        struct((chunk.shape[0] * count, chunk.shape[1]), chunk.dtype),
        limit=SMALL_LIMIT,
    )(*parts)


def shards(latents, spatial_kernel, temporal_kernel, cotangent):
    _, frames, rows, width = latents.shape
    channels = spatial_kernel.shape[2]
    sizes = Sizes(frames, rows, width // channels, channels)
    cols, seqs = lax.axis_size("col"), lax.axis_size("seq")
    frame_entries = float(rows * sizes.columns * cols * (channels // GROUPS))
    clip_entries = frame_entries * frames * seqs
    pixels = lax.axis_size("dp") * seqs * cols * sizes.pixels * sizes.columns
    grad_scale = 1.0 / math.sqrt(pixels)

    x = latents.reshape(sizes.pixels, width)
    cot = cotangent.reshape(sizes.pixels, width)
    sum_shape = struct((8, sizes.pair), F32)
    frame_shape = struct((2 * frames, sizes.pair), F32)
    padded_scratch = pltpu.VMEM((3, sizes.pixels, sizes.padded), BF16)
    slack = sizes.slack

    forth = [(i, i + 1) for i in range(seqs - 1)]
    before = lax.ppermute(cot[sizes.pixels - rows :], "seq", forth)
    after = lax.ppermute(cot[:rows], "seq", [(j, i) for i, j in forth])

    sums, edge = call(
        functools.partial(latent_sums_body, sizes),
        [frame_shape, struct((sizes.pixels, sizes.edge), BF16)],
    )(x)
    other = swap(sums, "col", 1)
    rim = swap(edge, "col", 1)
    window_weights = [pltpu.VMEM((3 * sizes.window, sizes.edge), BF16)] * 2
    hidden, act, clip = call(
        functools.partial(forward_body, sizes, frame_entries, min(4, sizes.pairs)),
        [struct((sizes.pixels, width), BF16), struct((sizes.pixels, sizes.padded), BF16), sum_shape],
        [padded_scratch] + window_weights,
        flops=CONV_COST,
    )(x, sums, other, rim, spatial_kernel)
    clips = from_all(clip + swap(clip, "col", 1), "seq")
    dact = call(
        functools.partial(activation_grad_body, sizes, min(4, sizes.pairs)),
        struct((sizes.pixels, width), F32),
        [pltpu.VMEM((sizes.edge, 3 * sizes.edge), BF16)] * 2,
        flops=CONV_COST // 3,
    )(cot, before, after, temporal_kernel)
    tact, tgrad, means, rims = call(
        functools.partial(temporal_body, sizes, clip_entries, seqs),
        [
            struct((sizes.pixels, width), BF16),
            struct((sizes.pixels, width), F32),
            sum_shape,
            struct((3 * sizes.pixels, sizes.edge), F32),
        ],
        [pltpu.VMEM((sizes.pixels, width), F32)],
        flops=CONV_COST // 3,
    )(hidden, cot, dact, *clips)
    means = from_all(means + swap(means, "col", 1), "seq")
    rims = swap(rims, "col", 1)
    temporal_grad = call(
        functools.partial(temporal_grad_body, sizes, min(4, sizes.pairs)),
        struct((packed_rows(channels, sizes), 128), F32),
        [pltpu.VMEM((channels, 3 * sizes.edge), F32)],
        flops=CONV_COST // 3,
    )(tact, cot, before, after)

    devices = lax.axis_size("dp") * seqs * cols
    used = packed_rows(3 * channels, sizes) + packed_rows(channels, sizes)
    all_rows = -(-used // (16 * devices)) * 16 * devices
    count = lax.axis_size(PHASES[0])
    chunk = (all_rows // 2 // count, 128)
    dtemp, dspat, *chunks = call(
        functools.partial(spatial_grad_body, sizes, clip_entries, seqs),
        [
            struct((sizes.pixels, width), BF16),
            struct((sizes.pixels, sizes.padded), BF16),
        ]
        + [struct(chunk, F32)] * count
        + [struct(chunk, BF16)] * count,
        [
            padded_scratch,
            pltpu.VMEM((3 * channels, 3 * sizes.edge), F32),
            pltpu.VMEM((all_rows, 128), F32),
        ],
        flops=CONV_COST,
    )(hidden, cot, tgrad, rims, act, temporal_grad, *clips, *means)
    chunks = [chunks[n] + swap(chunks[count + n], "col", 1).astype(F32) for n in range(count)]
    sends = [values.astype(BF16) for values in chunks[1:]]
    sends, dspat = lax.optimization_barrier((sends, dspat))
    found = [exchange(values, 0, n + 1) for n, values in enumerate(sends)]
    dnormed, mine = call(
        functools.partial(backward_body, sizes, frame_entries, min(4, sizes.pairs)),
        [struct((sizes.pixels, width), F32), frame_shape],
        [padded_scratch, pltpu.VMEM((2 * frames, 8, sizes.pair), F32)]
        + [pltpu.VMEM((sizes.edge, 3 * sizes.window), BF16)] * 2,
        flops=CONV_COST,
    )(x, sums, other, dspat, spatial_kernel)
    found, (dnormed, mine) = lax.optimization_barrier((found, (dnormed, mine)))
    total = added(scattered(chunks[:1] + found, 1))
    theirs = swap(mine, "col", 1)
    grad_latents = call(
        functools.partial(finish_body, sizes, frame_entries), struct((sizes.pixels, width), F32),
        flops=CONV_COST // 3,
    )(x, sums, other, cot, dtemp, dnormed, mine, theirs)
    part = gathered(total.astype(BF16), 1)
    parts = [part] + [exchange(part, 0, n) for n in range(1, count)]
    parts[1], grad_latents = lax.optimization_barrier((parts[1], grad_latents))
    others = [swap(part, "col", 1) for part in parts]
    spatial_grad, temporal_grad = call(
        functools.partial(unpack_body, sizes, grad_scale, len(parts)),
        [struct((9 * channels, channels), F32), struct((3 * channels, channels), F32)],
        [pltpu.VMEM((all_rows, 128), BF16)],
        flops=CONV_COST // 4,
    )(*parts, *others)

    return (
        grad_latents.reshape(latents.shape),
        spatial_grad.reshape(spatial_kernel.shape),
        temporal_grad.reshape(temporal_kernel.shape),
    )


def solution(mesh):
    in_specs = (P("dp", "seq", None, "col"), P(), P(), P("dp", "seq", None, "col"))
    out_specs = (P("dp", "seq", None, "col"), P(), P())
    return jax.shard_map(shards, mesh=mesh, in_specs=in_specs, out_specs=out_specs, check_vma=False)
```

```python
import functools
import math

import jax
import jax.numpy as jnp
from jax import lax
from jax.experimental import pallas as pl
from jax.experimental.pallas import tpu as pltpu
from jax.sharding import PartitionSpec as P

GROUPS = 32
EPSILON = 1e-05
F32 = jnp.float32
BF16 = jnp.bfloat16
VMEM_LIMIT = 20 * 1024 * 1024
SMALL_LIMIT = 4 * 1024 * 1024
CONV_COST = 12_000_000_000


def call(body, outs, scratch=(), flops=0, moved=0, limit=VMEM_LIMIT, spaces=None, out_spaces=None):
    specs = {} if spaces is None else {"in_specs": [pl.BlockSpec(memory_space=space) for space in spaces]}
    return pl.pallas_call(
        body,
        out_shape=outs,
        **specs,
        out_specs=(
            jax.tree.map(lambda _: pl.BlockSpec(memory_space=pltpu.VMEM), outs)
            if out_spaces is None
            else [pl.BlockSpec(memory_space=space) for space in out_spaces]
        ),
        scratch_shapes=list(scratch),
        compiler_params=pltpu.CompilerParams(vmem_limit_bytes=limit),
        cost_estimate=pl.CostEstimate(flops=flops, bytes_accessed=moved, transcendentals=0),
    )


def struct(shape, kind):
    return jax.ShapeDtypeStruct(shape, kind)


class Sizes:
    def __init__(self, frames, rows, columns, channels):
        self.frames = frames
        self.rows = rows
        self.columns = columns
        self.channels = channels
        self.pixels = frames * rows
        self.width = columns * channels
        self.pair = 2 * channels
        self.pairs = columns // 2
        self.edge = -(-channels // 128) * 128
        self.slack = self.edge - channels
        self.window = 3 * channels + self.slack
        self.padded = self.width + 2 * self.edge


def group_totals(sums, sizes):
    size = sizes.channels // GROUPS

    def member(shape, lane_dim):
        lane = lax.broadcasted_iota(jnp.int32, shape, lane_dim)
        group = lax.broadcasted_iota(jnp.int32, shape, 1 - lane_dim)
        channel = jnp.where(lane >= sizes.channels, lane - sizes.channels, lane)
        return ((channel >= group * size) & (channel < group * size + size)).astype(F32)

    high = lax.Precision.HIGHEST
    by_group = jnp.dot(sums, member((sizes.pair, 128), 0), precision=high, preferred_element_type=F32)
    return jnp.dot(by_group, member((128, sizes.pair), 1), precision=high, preferred_element_type=F32)


def moments(sums, half, entries, sizes):
    totals = group_totals(sums, sizes) * (1.0 / entries)
    mean = totals[0:half]
    rate = lax.rsqrt(totals[half : 2 * half] - mean * mean + EPSILON)
    return mean, rate


def fold(values):
    return jnp.sum(values.reshape(values.shape[0] // 8, 8, values.shape[1]), axis=0)


def pair_lanes(p, sizes):
    return pl.ds(pl.multiple_of(p * sizes.pair, 128), sizes.pair)


def join(even, odd, sizes):
    cut = sizes.edge - 128
    middle = even[:, cut:] + odd[:, :128]
    return jnp.concatenate([even[:, :cut], middle, odd[:, 128:]], axis=1)


def latent_sums_body(sizes, x_ref, sums_ref, edge_ref):
    def frame(f):
        rows = pl.ds(f * sizes.rows, sizes.rows)

        def step(p, carry):
            plain, square = carry
            v = x_ref[rows, pair_lanes(p, sizes)].astype(F32)
            return plain + fold(v), square + fold(v * v)

        zero = jnp.zeros((8, sizes.pair), F32)
        plain, square = lax.fori_loop(0, sizes.pairs, step, (zero, zero))
        return jnp.sum(plain, axis=0, keepdims=True), jnp.sum(square, axis=0, keepdims=True)

    found = [frame(f) for f in range(sizes.frames)]
    for f, (plain, square) in enumerate(found):
        sums_ref[f : f + 1, :] = plain
        sums_ref[sizes.frames + f : sizes.frames + f + 1, :] = square
    store_edge(sizes, x_ref, edge_ref)


def store_edge(sizes, source, target, at=0):
    left = lax.axis_index("col") == 0
    rows = pl.ds(at, sizes.pixels)

    @pl.when(left)
    def _():
        target[rows, :] = source[:, sizes.width - sizes.edge : sizes.width].astype(target.dtype)

    @pl.when(jnp.logical_not(left))
    def _():
        target[rows, :] = source[:, 0 : sizes.edge].astype(target.dtype)


def row_shifts(values, sizes):
    row = lax.broadcasted_iota(jnp.int32, values.shape, 0)
    down = jnp.where(row == 0, 0.0, pltpu.roll(values, 1, 0))
    up = jnp.where(row == sizes.rows - 1, 0.0, pltpu.roll(values, sizes.rows - 1, 0))
    return down, values, up


def put_shifts(values, frame, lanes, target, sizes):
    rows = pl.ds(frame * sizes.rows, sizes.rows)
    for i, moved in enumerate(row_shifts(values, sizes)):
        target[i, rows, lanes] = moved.astype(BF16)


def put_halo(of_frame, target, sizes):
    left = lax.axis_index("col") == 0
    for f in range(sizes.frames):
        rows = pl.ds(f * sizes.rows, sizes.rows)
        before, after = of_frame(rows, f, True), of_frame(rows, f, False)
        put_shifts(jnp.where(left, 0.0, before), f, pl.ds(0, sizes.edge), target, sizes)
        put_shifts(
            jnp.where(left, after, 0.0), f, pl.ds(sizes.edge + sizes.width, sizes.edge), target, sizes
        )


def forward_weights(kernel_ref, even_ref, odd_ref, sizes):
    channels, slack, window = sizes.channels, sizes.slack, sizes.window
    for weights in (even_ref, odd_ref):
        weights[...] = jnp.zeros(weights.shape, BF16)
    for i in range(3):
        for j in range(3):
            taps = kernel_ref[i, j]
            zeros = jnp.zeros((channels, slack), BF16)
            at = i * window + j * channels
            even_ref[at + slack : at + slack + channels, :] = jnp.concatenate([taps, zeros], axis=1)
            odd_ref[at : at + channels, :] = jnp.concatenate([zeros, taps], axis=1)


def backward_weights(kernel_ref, even_ref, odd_ref, sizes):
    channels, slack, window = sizes.channels, sizes.slack, sizes.window
    for weights in (even_ref, odd_ref):
        weights[...] = jnp.zeros(weights.shape, BF16)
    zeros = jnp.zeros((channels, slack), BF16)
    for i in range(3):
        taps = [kernel_ref[2 - i, 2 - j] for j in range(3)]
        lanes = slice(i * window, (i + 1) * window)
        even_ref[0:channels, lanes] = jnp.concatenate([zeros] + taps, axis=1)
        odd_ref[slack : slack + channels, lanes] = jnp.concatenate(taps + [zeros], axis=1)


def temporal_weights(kernel_ref, even_ref, odd_ref, sizes):
    channels, slack, edge = sizes.channels, sizes.slack, sizes.edge
    for weights in (even_ref, odd_ref):
        weights[...] = jnp.zeros(weights.shape, BF16)
    zeros = jnp.zeros((channels, slack), BF16)
    for i in range(3):
        lanes = slice(i * edge, (i + 1) * edge)
        even_ref[0:channels, lanes] = jnp.concatenate([kernel_ref[i], zeros], axis=1)
        odd_ref[slack : slack + channels, lanes] = jnp.concatenate([zeros, kernel_ref[i]], axis=1)


def windows(padded_ref, p, count, odd, sizes):
    found = []
    for q in range(count):
        start = pl.multiple_of((p + q) * sizes.pair, 128) + (sizes.edge if odd else 0)
        lanes = pl.ds(pl.multiple_of(start, 128), sizes.window)
        found.append(jnp.concatenate([padded_ref[i, :, lanes] for i in range(3)], axis=1))
    return jnp.concatenate(found, axis=0)


def silu_parts(v):
    s = 0.5 * jnp.tanh(0.5 * v) + 0.5
    return v * s, s


def forward_body(
    sizes, frame_entries, block, x_ref, sums_ref, other_ref, rim_ref, kernel_ref,
    hidden_ref, act_ref, clip_ref, padded, even_ref, odd_ref,
):
    forward_weights(kernel_ref, even_ref, odd_ref, sizes)
    mean, rate = moments(sums_ref[...] + other_ref[...], sizes.frames, frame_entries, sizes)

    def rim(rows, f, before):
        lanes = slice(sizes.pair - sizes.edge, sizes.pair) if before else slice(0, sizes.edge)
        v = rim_ref[rows, :].astype(F32)
        return silu_parts((v - mean[f : f + 1, lanes]) * rate[f : f + 1, lanes])[0]

    put_halo(rim, padded, sizes)

    def activate(p, _):
        for f in range(sizes.frames):
            v = x_ref[pl.ds(f * sizes.rows, sizes.rows), pair_lanes(p, sizes)].astype(F32)
            act = silu_parts((v - mean[f : f + 1]) * rate[f : f + 1])[0]
            lanes = pl.ds(pl.multiple_of(p * sizes.pair + sizes.edge, 128), sizes.pair)
            put_shifts(act, f, lanes, padded, sizes)
        return 0

    lax.fori_loop(0, sizes.pairs, activate, 0)
    act_ref[...] = padded[1]

    def step(b, carry):
        plain, square = carry
        p = b * block
        even = jnp.dot(windows(padded, p, block, False, sizes), even_ref[...], preferred_element_type=F32)
        odd = jnp.dot(windows(padded, p, block, True, sizes), odd_ref[...], preferred_element_type=F32)
        for q in range(block):
            rows = slice(q * sizes.pixels, (q + 1) * sizes.pixels)
            spatial = join(even[rows], odd[rows], sizes)
            lanes = pair_lanes(p + q, sizes)
            hidden = (x_ref[:, lanes].astype(F32) + spatial).astype(BF16)
            hidden_ref[:, lanes] = hidden
            wide = hidden.astype(F32)
            plain = plain + fold(wide)
            square = square + fold(wide * wide)
        return plain, square

    zero = jnp.zeros((8, sizes.pair), F32)
    plain, square = lax.fori_loop(0, sizes.pairs // block, step, (zero, zero))
    put_sums(clip_ref, plain, square)


def add_up(refs):
    total = refs[0][...]
    for ref in refs[1:]:
        total = total + ref[...]
    return total


def put_sums(target, plain, square):
    target[...] = jnp.zeros(target.shape, F32)
    target[0:1, :] = jnp.sum(plain, axis=0, keepdims=True)
    target[1:2, :] = jnp.sum(square, axis=0, keepdims=True)


def end_frames_body(sizes, cot_hbm, first_ref, second_ref, sems):
    even = lax.axis_index("seq") % 2 == 0
    last = sizes.pixels - sizes.rows
    copies = []
    for k, target in enumerate((first_ref, second_ref)):
        start = jnp.where(even, last, 0) if k == 0 else jnp.where(even, 0, last)
        rows = pl.ds(pl.multiple_of(start, 16), sizes.rows)
        copies.append(pltpu.make_async_copy(cot_hbm.at[rows, :], target, sems.at[k]))
    for copy in copies:
        copy.start()
    for copy in copies:
        copy.wait()


def neighbour_frames(cot, sizes):
    seqs = lax.axis_size("seq")
    first, second = call(
        functools.partial(end_frames_body, sizes),
        [struct((sizes.rows, sizes.width), BF16)] * 2,
        [pltpu.SemaphoreType.DMA((2,))],
        limit=SMALL_LIMIT,
        spaces=[pltpu.HBM],
        flops=CONV_COST // 3,
    )(cot)
    found = []
    for low, values in ((0, first), (1, second)):
        pairs = []
        for i in range(low, seqs - 1, 2):
            pairs += [(i, i + 1), (i + 1, i)]
        found.append(lax.ppermute(values, "seq", pairs))
    return found


def frame_taps(cot_ref, first_ref, second_ref, lanes, sizes):
    even = lax.axis_index("seq") % 2 == 0
    own, first, second = cot_ref[:, lanes], first_ref[:, lanes], second_ref[:, lanes]
    later = jnp.concatenate([own[sizes.rows :], jnp.where(even, first, second)], axis=0)
    earlier = jnp.concatenate([jnp.where(even, second, first), own[: sizes.pixels - sizes.rows]], axis=0)
    return later, own, earlier


def activation_grad_body(sizes, block, cot_ref, before_ref, after_ref, kernel_ref, dact_ref, even_ref, odd_ref):
    temporal_weights(kernel_ref, even_ref, odd_ref, sizes)

    def step(b, _):
        p = b * block
        found = []
        for odd, weights in ((False, even_ref), (True, odd_ref)):
            rows = []
            for q in range(block):
                start = (p + q) * sizes.pair + (sizes.pair - sizes.edge if odd else 0)
                lanes = pl.ds(pl.multiple_of(start, 128), sizes.edge)
                rows.append(
                    jnp.concatenate(frame_taps(cot_ref, before_ref, after_ref, lanes, sizes), axis=1)
                )
            found.append(
                lax.dot_general(
                    jnp.concatenate(rows, axis=0), weights[...], (((1,), (1,)), ((), ())),
                    preferred_element_type=F32,
                )
            )
        for q in range(block):
            rows = slice(q * sizes.pixels, (q + 1) * sizes.pixels)
            dact_ref[:, pair_lanes(p + q, sizes)] = join(found[0][rows], found[1][rows], sizes)
        return 0

    lax.fori_loop(0, sizes.pairs // block, step, 0)


def temporal_body(
    sizes, clip_entries, terms, hidden_ref, cot_ref, dact_ref, *refs
):
    clips, (act_ref, grad_ref, sums_ref, rim_ref, normed) = refs[:terms], refs[terms:]
    mean, rate = moments(add_up(clips), 1, clip_entries, sizes)

    def step(p, carry):
        plain, cross = carry
        lanes = pair_lanes(p, sizes)
        for f in range(sizes.frames):
            rows = pl.ds(f * sizes.rows, sizes.rows)
            tnormed = (hidden_ref[rows, lanes].astype(F32) - mean) * rate
            act, s = silu_parts(tnormed)
            act_ref[rows, lanes] = act.astype(BF16)
            normed[rows, lanes] = tnormed
            grad = dact_ref[rows, lanes] * (s * (1.0 + tnormed * (1.0 - s)))
            grad_ref[rows, lanes] = grad
            plain = plain + fold(grad)
            cross = cross + fold(grad * tnormed)
        return plain, cross

    zero = jnp.zeros((8, sizes.pair), F32)
    plain, cross = lax.fori_loop(0, sizes.pairs, step, (zero, zero))
    put_sums(sums_ref, plain, cross)
    for k, source in enumerate((grad_ref, normed, cot_ref)):
        store_edge(sizes, source, rim_ref, k * sizes.pixels)


def pack(total, target, at, sizes):
    rows, width = total.shape
    full = width // 128
    for k in range(full):
        target[at + k * rows : at + (k + 1) * rows, :] = total[:, k * 128 : (k + 1) * 128]
    if width % 128:
        ends, half = total[:, full * 128 :], rows // 2
        target[at + full * rows : at + full * rows + half, :] = jnp.concatenate([ends[:half], ends[half:]], axis=1)


def packed_rows(rows, sizes):
    return 3 * rows * sizes.channels // 128


def temporal_grad_body(sizes, block, act_ref, cot_ref, before_ref, after_ref, out_ref, total):
    total[...] = jnp.zeros(total.shape, F32)
    channels = sizes.channels

    def step(b, _):
        acts, cots = [], []
        for q in range(block):
            lanes = pair_lanes(b * block + q, sizes)
            act = act_ref[:, lanes]
            acts += [act[:, :channels], act[:, channels:]]
            taps = frame_taps(cot_ref, before_ref, after_ref, lanes, sizes)
            for part in (slice(0, channels), slice(channels, 2 * channels)):
                cots.append(jnp.concatenate([t[:, part] for t in taps], axis=1))
        total[...] += lax.dot_general(
            jnp.concatenate(acts, axis=0), jnp.concatenate(cots, axis=0), (((0,), (0,)), ((), ())),
            preferred_element_type=F32,
        )
        return 0

    lax.fori_loop(0, sizes.pairs // block, step, 0)
    pack(total, out_ref, 0, sizes)


def spatial_grad_body(
    sizes, clip_entries, terms, hidden_ref, cot_ref, grad_ref, rim_ref, act_ref, time_ref, *refs
):
    clips, sums = refs[:terms], refs[terms : 2 * terms]
    dtemp_ref, dspat_ref = refs[2 * terms : 2 * terms + 2]
    chunks, (padded, total, packed) = refs[2 * terms + 2 : -3], refs[-3:]
    count = len(chunks) // 2
    mean, rate = moments(add_up(clips), 1, clip_entries, sizes)
    means = group_totals(add_up(sums), sizes) * (1.0 / clip_entries)
    plain, cross = means[0:1], means[1:2]

    def rim(rows, f, before):
        lanes = slice(sizes.pair - sizes.edge, sizes.pair) if before else slice(0, sizes.edge)
        at = [pl.ds(k * sizes.pixels + f * sizes.rows, sizes.rows) for k in range(3)]
        grad, tnormed, cot = (rim_ref[r, :] for r in at)
        dtemp = rate[:, lanes] * (grad - plain[:, lanes] - tnormed * cross[:, lanes])
        return (cot + dtemp.astype(BF16).astype(F32)).astype(BF16).astype(F32)

    put_halo(rim, padded, sizes)

    def combine(p, _):
        lanes = pair_lanes(p, sizes)
        for f in range(sizes.frames):
            rows = pl.ds(f * sizes.rows, sizes.rows)
            tnormed = (hidden_ref[rows, lanes].astype(F32) - mean) * rate
            dtemp = (rate * (grad_ref[rows, lanes] - plain - tnormed * cross)).astype(BF16)
            dtemp_ref[rows, lanes] = dtemp
            dspat = cot_ref[rows, lanes].astype(F32) + dtemp.astype(F32)
            put_shifts(
                dspat, f, pl.ds(pl.multiple_of(p * sizes.pair + sizes.edge, 128), sizes.pair), padded, sizes
            )
        return 0

    lax.fori_loop(0, sizes.pairs, combine, 0)
    dspat_ref[...] = padded[1]

    channels = sizes.channels
    total[...] = jnp.zeros(total.shape, F32)

    block = min(4, sizes.pairs)

    def step(b, _):
        for odd in (False, True):
            left, right = [], []
            for q in range(block):
                p = block * b + q
                start = p * sizes.pair + (sizes.edge if odd else 0)
                left.append(act_ref[:, pl.ds(pl.multiple_of(start, 128), sizes.window)])
                both = pl.ds(pl.multiple_of(p * sizes.pair + sizes.edge, 128), sizes.pair)
                taps = []
                for i in range(3):
                    d = padded[2 - i, :, both]
                    d = d[:, channels:] if odd else d[:, :channels]
                    taps.append(d)
                right.append(jnp.concatenate(taps, axis=1))
            part = lax.dot_general(
                jnp.concatenate(left, axis=0), jnp.concatenate(right, axis=0), (((0,), (0,)), ((), ())),
                preferred_element_type=F32,
            )
            total[...] += part[: 3 * channels] if odd else part[sizes.slack :]
        return 0

    lax.fori_loop(0, sizes.pairs // block, step, 0)
    pack(total, packed, 0, sizes)
    own = packed_rows(3 * channels, sizes)
    packed[own : own + time_ref.shape[0], :] = time_ref[...]
    used = own + time_ref.shape[0]
    packed[used:, :] = jnp.zeros((packed.shape[0] - used, 128), F32)
    core = lax.axis_index("col")
    for n in range(count):
        keep_ref, send_ref = chunks[n], chunks[count + n]
        keep_ref[...] = packed[chunk_rows(core, n, packed.shape[0], count), :]
        send_ref[...] = packed[chunk_rows(1 - core, n, packed.shape[0], count), :].astype(BF16)


def backward_body(
    sizes, frame_entries, block, x_ref, sums_ref, other_ref, dspat_ref, kernel_ref,
    grad_ref, out_ref, padded, plains, even_ref, odd_ref,
):
    backward_weights(kernel_ref, even_ref, odd_ref, sizes)
    mean, rate = moments(sums_ref[...] + other_ref[...], sizes.frames, frame_entries, sizes)

    def spread(k, _):
        lanes = pl.ds(pl.multiple_of(k * 128, 128), 128)
        for f in range(sizes.frames):
            rows = pl.ds(f * sizes.rows, sizes.rows)
            put_shifts(dspat_ref[rows, lanes].astype(F32), f, lanes, padded, sizes)
        return 0

    lax.fori_loop(0, sizes.padded // 128, spread, 0)
    plains[...] = jnp.zeros(plains.shape, F32)
    contract = (((1,), (1,)), ((), ()))

    def step(b, _):
        p = b * block
        even = lax.dot_general(
            windows(padded, p, block, False, sizes), even_ref[...], contract, preferred_element_type=F32
        )
        odd = lax.dot_general(
            windows(padded, p, block, True, sizes), odd_ref[...], contract, preferred_element_type=F32
        )
        for q in range(block):
            base = q * sizes.pixels
            for f in range(sizes.frames):
                at = slice(base + f * sizes.rows, base + (f + 1) * sizes.rows)
                dact = join(even[at], odd[at], sizes)
                rows, lanes = pl.ds(f * sizes.rows, sizes.rows), pair_lanes(p + q, sizes)
                normed = (x_ref[rows, lanes].astype(F32) - mean[f : f + 1]) * rate[f : f + 1]
                _, s = silu_parts(normed)
                grad = dact * (s * (1.0 + normed * (1.0 - s)))
                grad_ref[rows, lanes] = grad
                plains[f] += fold(grad)
                plains[sizes.frames + f] += fold(grad * normed)
        return 0

    lax.fori_loop(0, sizes.pairs // block, step, 0)
    for k in range(2 * sizes.frames):
        out_ref[k : k + 1, :] = jnp.sum(plains[k], axis=0, keepdims=True)


def finish_body(
    sizes, frame_entries, x_ref, sums_ref, other_ref, cot_ref, dtemp_ref, grad_ref, mine_ref, theirs_ref, out_ref
):
    mean, rate = moments(sums_ref[...] + other_ref[...], sizes.frames, frame_entries, sizes)
    means = group_totals(mine_ref[...] + theirs_ref[...], sizes) * (1.0 / frame_entries)

    def step(p, _):
        lanes = pair_lanes(p, sizes)
        for f in range(sizes.frames):
            rows = pl.ds(f * sizes.rows, sizes.rows)
            normed = (x_ref[rows, lanes].astype(F32) - mean[f : f + 1]) * rate[f : f + 1]
            dhidden = cot_ref[rows, lanes].astype(F32) + dtemp_ref[rows, lanes].astype(F32)
            plain, cross = means[f : f + 1], means[sizes.frames + f : sizes.frames + f + 1]
            out_ref[rows, lanes] = dhidden + rate[f : f + 1] * (grad_ref[rows, lanes] - plain - normed * cross)
        return 0

    lax.fori_loop(0, sizes.pairs, step, 0)


PHASES = ("dp", "seq")


def crossed():
    return lax.axis_size("col") == 2 and lax.axis_size("dp") == lax.axis_size("seq")


def place_of(core, phase):
    place = lax.axis_index(PHASES[phase])
    if crossed():
        place = jnp.where(core == 0, place, lax.axis_index(PHASES[1 - phase]))
    return place


def exchange(values, phase, bits):
    names = ("dp", "seq", "col")
    dps, seqs, cols = (lax.axis_size(name) for name in names)
    pairs = []
    for i in range(dps * seqs * cols):
        place = [i // (seqs * cols), i // cols % seqs, i % cols]
        place[phase ^ place[2] if crossed() else phase] ^= bits
        pairs.append((i, (place[0] * seqs + place[1]) * cols + place[2]))
    return lax.ppermute(values, names, pairs)


def chunk_rows(core, bits, rows, count):
    chunk = rows // 2 // count
    start = core * (rows // 2) + (place_of(core, 0) ^ bits) * chunk
    return pl.ds(pl.multiple_of(start, 16), chunk)


def unpack_body(sizes, scale, parts, *refs):
    mine, theirs = refs[:parts], refs[parts : 2 * parts]
    spatial_hbm, temporal_hbm, packed, spatial_ref, temporal_ref, sems = refs[2 * parts :]
    core = lax.axis_index("col")
    for n in range(parts):
        packed[chunk_rows(core, n, packed.shape[0], parts), :] = mine[n][...]
        packed[chunk_rows(1 - core, n, packed.shape[0], parts), :] = theirs[n][...]
    width = 3 * sizes.channels
    full, left = width // 128, width % 128
    at = 0
    copies = []
    for target, hbm in ((spatial_ref, spatial_hbm), (temporal_ref, temporal_hbm)):
        count = target.shape[0] // 3
        tile = math.gcd(count // 2, 80)
        block = math.gcd(count // 2, 240)
        for first in range(0, count // 2, block):

            def step(k, _, at=at, target=target, count=count, first=first, tile=tile):
                line = first + k * tile
                ends = packed[pl.ds(pl.multiple_of(at + full * count + line, 16), tile), :].astype(F32)
                for second in range(2):
                    row = line + second * (count // 2)
                    found = [
                        packed[pl.ds(pl.multiple_of(at + b * count + row, 16), tile), :].astype(F32) for b in range(full)
                    ]
                    found.append(ends[:, left:] if second else ends[:, :left])
                    wide = jnp.concatenate(found, axis=1) * scale
                    for i in range(3):
                        rows = pl.ds(pl.multiple_of(i * count + row, 16), tile)
                        target[rows, :] = wide[:, i * sizes.channels : (i + 1) * sizes.channels]
                return 0

            lax.fori_loop(0, block // tile, step, 0)
            for start in range(first, 3 * count, count // 2):
                rows = pl.ds(start, block)
                copies.append(pltpu.make_async_copy(target.at[rows, :], hbm.at[rows, :], sems.at[len(copies)]))
                copies[-1].start()
        at += count * width // 128
    for copy in copies:
        copy.wait()


def swap(values, axis, bit):
    count = lax.axis_size(axis)
    return lax.ppermute(values, axis, [(i, i ^ bit) for i in range(count)])


def from_all(values, axis):
    return [values] + [swap(values, axis, s) for s in range(1, lax.axis_size(axis))]


def added(terms):
    total = terms[0].astype(F32)
    for term in terms[1:]:
        total = total + term.astype(F32)
    return total


def place_rows(phase, bits, rows):
    place = place_of(lax.axis_index("col"), phase)
    return pl.ds(pl.multiple_of((place ^ bits) * rows, 16), rows)


def split_body(phase, terms, *refs):
    for bits, target in enumerate(refs[terms:]):
        rows = place_rows(phase, bits, target.shape[0])
        target[...] = added([ref[rows, :] for ref in refs[:terms]]).astype(target.dtype)


def scattered(terms, phase):
    count = lax.axis_size(PHASES[phase])
    chunk = (terms[0].shape[0] // count, terms[0].shape[1])
    own, *others = call(
        functools.partial(split_body, phase, len(terms)),
        [struct(chunk, F32)] + [struct(chunk, BF16)] * (count - 1),
        limit=SMALL_LIMIT,
    )(*terms)
    return [own] + [exchange(values, phase, n + 1) for n, values in enumerate(others)]


def gather_body(phase, *refs):
    for bits, part in enumerate(refs[:-1]):
        refs[-1][place_rows(phase, bits, part.shape[0]), :] = part[...]


def gathered(chunk, phase):
    count = lax.axis_size(PHASES[phase])
    parts = [chunk] + [exchange(chunk, phase, n) for n in range(1, count)]
    return call(
        functools.partial(gather_body, phase),
        struct((chunk.shape[0] * count, chunk.shape[1]), chunk.dtype),
        limit=SMALL_LIMIT,
    )(*parts)


def shards(latents, spatial_kernel, temporal_kernel, cotangent):
    _, frames, rows, width = latents.shape
    channels = spatial_kernel.shape[2]
    sizes = Sizes(frames, rows, width // channels, channels)
    cols, seqs = lax.axis_size("col"), lax.axis_size("seq")
    frame_entries = float(rows * sizes.columns * cols * (channels // GROUPS))
    clip_entries = frame_entries * frames * seqs
    pixels = lax.axis_size("dp") * seqs * cols * sizes.pixels * sizes.columns
    grad_scale = 1.0 / math.sqrt(pixels)

    x = latents.reshape(sizes.pixels, width)
    cot = cotangent.reshape(sizes.pixels, width)
    sum_shape = struct((8, sizes.pair), F32)
    frame_shape = struct((2 * frames, sizes.pair), F32)
    padded_scratch = pltpu.VMEM((3, sizes.pixels, sizes.padded), BF16)
    slack = sizes.slack

    before, after = neighbour_frames(cot, sizes)

    sums, edge = call(
        functools.partial(latent_sums_body, sizes),
        [frame_shape, struct((sizes.pixels, sizes.edge), BF16)],
        flops=CONV_COST // 3,
    )(x)
    other = swap(sums, "col", 1)
    rim = swap(edge, "col", 1)
    hidden, act, clip = call(
        functools.partial(forward_body, sizes, frame_entries, min(4, sizes.pairs)),
        [struct((sizes.pixels, width), BF16), struct((sizes.pixels, sizes.padded), BF16), sum_shape],
        [padded_scratch] + [pltpu.VMEM((3 * sizes.window, sizes.edge), BF16)] * 2,
        flops=CONV_COST,
    )(x, sums, other, rim, spatial_kernel)
    clips = from_all(clip + swap(clip, "col", 1), "seq")
    dact = call(
        functools.partial(activation_grad_body, sizes, min(4, sizes.pairs)),
        struct((sizes.pixels, width), F32),
        [pltpu.VMEM((sizes.edge, 3 * sizes.edge), BF16)] * 2,
        flops=CONV_COST // 3,
    )(cot, before, after, temporal_kernel)
    tact, tgrad, means, rims = call(
        functools.partial(temporal_body, sizes, clip_entries, seqs),
        [
            struct((sizes.pixels, width), BF16),
            struct((sizes.pixels, width), F32),
            sum_shape,
            struct((3 * sizes.pixels, sizes.edge), F32),
        ],
        [pltpu.VMEM((sizes.pixels, width), F32)],
        flops=CONV_COST // 3,
    )(hidden, cot, dact, *clips)
    means = from_all(means + swap(means, "col", 1), "seq")
    rims = swap(rims, "col", 1)
    temporal_grad = call(
        functools.partial(temporal_grad_body, sizes, min(4, sizes.pairs)),
        struct((packed_rows(channels, sizes), 128), F32),
        [pltpu.VMEM((channels, 3 * channels), F32)],
        flops=CONV_COST // 3,
    )(tact, cot, before, after)

    devices = lax.axis_size("dp") * seqs * cols
    used = packed_rows(3 * channels, sizes) + packed_rows(channels, sizes)
    all_rows = -(-used // (16 * devices)) * 16 * devices
    count = lax.axis_size(PHASES[0])
    chunk = (all_rows // 2 // count, 128)
    dtemp, dspat, *chunks = call(
        functools.partial(spatial_grad_body, sizes, clip_entries, seqs),
        [
            struct((sizes.pixels, width), BF16),
            struct((sizes.pixels, sizes.padded), BF16),
        ]
        + [struct(chunk, F32)] * count
        + [struct(chunk, BF16)] * count,
        [
            padded_scratch,
            pltpu.VMEM((3 * channels, 3 * channels), F32),
            pltpu.VMEM((all_rows, 128), F32),
        ],
        flops=CONV_COST,
    )(hidden, cot, tgrad, rims, act, temporal_grad, *clips, *means)
    chunks = [chunks[n] + swap(chunks[count + n], "col", 1).astype(F32) for n in range(count)]
    sends = [values.astype(BF16) for values in chunks[1:]]
    sends, dspat = lax.optimization_barrier((sends, dspat))
    found = [exchange(values, 0, n + 1) for n, values in enumerate(sends)]
    dnormed, mine = call(
        functools.partial(backward_body, sizes, frame_entries, min(4, sizes.pairs)),
        [struct((sizes.pixels, width), F32), frame_shape],
        [padded_scratch, pltpu.VMEM((2 * frames, 8, sizes.pair), F32)]
        + [pltpu.VMEM((sizes.edge, 3 * sizes.window), BF16)] * 2,
        flops=CONV_COST,
    )(x, sums, other, dspat, spatial_kernel)
    found, (dnormed, mine) = lax.optimization_barrier((found, (dnormed, mine)))
    total = added(scattered(chunks[:1] + found, 1))
    theirs = swap(mine, "col", 1)
    grad_latents = call(
        functools.partial(finish_body, sizes, frame_entries), struct((sizes.pixels, width), F32),
        flops=CONV_COST // 3,
    )(x, sums, other, cot, dtemp, dnormed, mine, theirs)
    part = gathered(total.astype(BF16), 1)
    parts = [part] + [exchange(part, 0, n) for n in range(1, count)]
    parts[1], grad_latents = lax.optimization_barrier((parts[1], grad_latents))
    others = [swap(part, "col", 1) for part in parts]
    spatial_grad, temporal_grad = call(
        functools.partial(unpack_body, sizes, grad_scale, len(parts)),
        [struct((9 * channels, channels), F32), struct((3 * channels, channels), F32)],
        [
            pltpu.VMEM((all_rows, 128), BF16),
            pltpu.VMEM((9 * channels, channels), F32),
            pltpu.VMEM((3 * channels, channels), F32),
            pltpu.SemaphoreType.DMA((64,)),
        ],
        flops=CONV_COST // 4,
        out_spaces=[pltpu.HBM] * 2,
    )(*parts, *others)

    return (
        grad_latents.reshape(latents.shape),
        spatial_grad.reshape(spatial_kernel.shape),
        temporal_grad.reshape(temporal_kernel.shape),
    )


def solution(mesh):
    in_specs = (P("dp", "seq", None, "col"), P(), P(), P("dp", "seq", None, "col"))
    out_specs = (P("dp", "seq", None, "col"), P(), P())
    return jax.shard_map(shards, mesh=mesh, in_specs=in_specs, out_specs=out_specs, check_vma=False)
```

```python
import functools
import math

import jax
import jax.numpy as jnp
from jax import lax
from jax.experimental import pallas as pl
from jax.experimental.pallas import tpu as pltpu
from jax.sharding import PartitionSpec as P

GROUPS = 32
EPSILON = 1e-05
F32 = jnp.float32
BF16 = jnp.bfloat16
VMEM_LIMIT = 20 * 1024 * 1024
SMALL_LIMIT = 4 * 1024 * 1024
CONV_COST = 12_000_000_000


def call(body, outs, scratch=(), flops=0, moved=0, limit=VMEM_LIMIT, spaces=None, out_spaces=None, aliases=None):
    specs = {} if spaces is None else {"in_specs": [pl.BlockSpec(memory_space=space) for space in spaces]}
    return pl.pallas_call(
        body,
        out_shape=outs,
        **specs,
        out_specs=(
            jax.tree.map(lambda _: pl.BlockSpec(memory_space=pltpu.VMEM), outs)
            if out_spaces is None
            else [pl.BlockSpec(memory_space=space) for space in out_spaces]
        ),
        scratch_shapes=list(scratch),
        input_output_aliases=aliases or {},
        compiler_params=pltpu.CompilerParams(vmem_limit_bytes=limit),
        cost_estimate=pl.CostEstimate(flops=flops, bytes_accessed=moved, transcendentals=0),
    )


def struct(shape, kind):
    return jax.ShapeDtypeStruct(shape, kind)


class Sizes:
    def __init__(self, frames, rows, columns, channels):
        self.frames = frames
        self.rows = rows
        self.columns = columns
        self.channels = channels
        self.pixels = frames * rows
        self.width = columns * channels
        self.pair = 2 * channels
        self.pairs = columns // 2
        self.edge = -(-channels // 128) * 128
        self.slack = self.edge - channels
        self.window = 3 * channels + self.slack
        self.padded = self.width + 2 * self.edge


def group_totals(sums, sizes):
    size = sizes.channels // GROUPS

    def member(shape, lane_dim):
        lane = lax.broadcasted_iota(jnp.int32, shape, lane_dim)
        group = lax.broadcasted_iota(jnp.int32, shape, 1 - lane_dim)
        channel = jnp.where(lane >= sizes.channels, lane - sizes.channels, lane)
        return ((channel >= group * size) & (channel < group * size + size)).astype(F32)

    high = lax.Precision.HIGHEST
    by_group = jnp.dot(sums, member((sizes.pair, 128), 0), precision=high, preferred_element_type=F32)
    return jnp.dot(by_group, member((128, sizes.pair), 1), precision=high, preferred_element_type=F32)


def moments(sums, half, entries, sizes):
    totals = group_totals(sums, sizes) * (1.0 / entries)
    mean = totals[0:half]
    rate = lax.rsqrt(totals[half : 2 * half] - mean * mean + EPSILON)
    return mean, rate


def fold(values):
    return jnp.sum(values.reshape(values.shape[0] // 8, 8, values.shape[1]), axis=0)


def pair_lanes(p, sizes):
    return pl.ds(pl.multiple_of(p * sizes.pair, 128), sizes.pair)


def join(even, odd, sizes):
    cut = sizes.edge - 128
    middle = even[:, cut:] + odd[:, :128]
    return jnp.concatenate([even[:, :cut], middle, odd[:, 128:]], axis=1)


def latent_sums_body(sizes, x_ref, sums_ref, edge_ref):
    def frame(f):
        rows = pl.ds(f * sizes.rows, sizes.rows)

        def step(p, carry):
            plain, square = carry
            v = x_ref[rows, pair_lanes(p, sizes)].astype(F32)
            return plain + fold(v), square + fold(v * v)

        zero = jnp.zeros((8, sizes.pair), F32)
        plain, square = lax.fori_loop(0, sizes.pairs, step, (zero, zero))
        return jnp.sum(plain, axis=0, keepdims=True), jnp.sum(square, axis=0, keepdims=True)

    found = [frame(f) for f in range(sizes.frames)]
    for f, (plain, square) in enumerate(found):
        sums_ref[f : f + 1, :] = plain
        sums_ref[sizes.frames + f : sizes.frames + f + 1, :] = square
    store_edge(sizes, x_ref, edge_ref)


def store_edge(sizes, source, target, at=0):
    left = lax.axis_index("col") == 0
    rows = pl.ds(at, sizes.pixels)

    @pl.when(left)
    def _():
        target[rows, :] = source[:, sizes.width - sizes.edge : sizes.width].astype(target.dtype)

    @pl.when(jnp.logical_not(left))
    def _():
        target[rows, :] = source[:, 0 : sizes.edge].astype(target.dtype)


def row_shifts(values, sizes):
    row = lax.broadcasted_iota(jnp.int32, values.shape, 0)
    down = jnp.where(row == 0, 0.0, pltpu.roll(values, 1, 0))
    up = jnp.where(row == sizes.rows - 1, 0.0, pltpu.roll(values, sizes.rows - 1, 0))
    return down, values, up


def put_shifts(values, frame, lanes, target, sizes):
    rows = pl.ds(frame * sizes.rows, sizes.rows)
    for i, moved in enumerate(row_shifts(values, sizes)):
        target[i, rows, lanes] = moved.astype(BF16)


def put_halo(of_frame, target, sizes):
    left = lax.axis_index("col") == 0
    for f in range(sizes.frames):
        rows = pl.ds(f * sizes.rows, sizes.rows)
        before, after = of_frame(rows, f, True), of_frame(rows, f, False)
        put_shifts(jnp.where(left, 0.0, before), f, pl.ds(0, sizes.edge), target, sizes)
        put_shifts(
            jnp.where(left, after, 0.0), f, pl.ds(sizes.edge + sizes.width, sizes.edge), target, sizes
        )


def forward_weights(kernel_ref, even_ref, odd_ref, sizes):
    channels, slack, window = sizes.channels, sizes.slack, sizes.window
    for weights in (even_ref, odd_ref):
        weights[...] = jnp.zeros(weights.shape, BF16)
    for i in range(3):
        for j in range(3):
            taps = kernel_ref[i, j]
            zeros = jnp.zeros((channels, slack), BF16)
            at = i * window + j * channels
            even_ref[at + slack : at + slack + channels, :] = jnp.concatenate([taps, zeros], axis=1)
            odd_ref[at : at + channels, :] = jnp.concatenate([zeros, taps], axis=1)


def backward_weights(kernel_ref, even_ref, odd_ref, sizes):
    channels, slack, window = sizes.channels, sizes.slack, sizes.window
    for weights in (even_ref, odd_ref):
        weights[...] = jnp.zeros(weights.shape, BF16)
    zeros = jnp.zeros((channels, slack), BF16)
    for i in range(3):
        taps = [kernel_ref[2 - i, 2 - j] for j in range(3)]
        lanes = slice(i * window, (i + 1) * window)
        even_ref[0:channels, lanes] = jnp.concatenate([zeros] + taps, axis=1)
        odd_ref[slack : slack + channels, lanes] = jnp.concatenate(taps + [zeros], axis=1)


def temporal_weights(kernel_ref, even_ref, odd_ref, sizes):
    channels, slack, edge = sizes.channels, sizes.slack, sizes.edge
    for weights in (even_ref, odd_ref):
        weights[...] = jnp.zeros(weights.shape, BF16)
    zeros = jnp.zeros((channels, slack), BF16)
    for i in range(3):
        lanes = slice(i * edge, (i + 1) * edge)
        even_ref[0:channels, lanes] = jnp.concatenate([kernel_ref[i], zeros], axis=1)
        odd_ref[slack : slack + channels, lanes] = jnp.concatenate([zeros, kernel_ref[i]], axis=1)


def windows(padded_ref, p, count, odd, sizes):
    found = []
    for q in range(count):
        start = pl.multiple_of((p + q) * sizes.pair, 128) + (sizes.edge if odd else 0)
        lanes = pl.ds(pl.multiple_of(start, 128), sizes.window)
        found.append(jnp.concatenate([padded_ref[i, :, lanes] for i in range(3)], axis=1))
    return jnp.concatenate(found, axis=0)


def silu_parts(v):
    s = 0.5 * jnp.tanh(0.5 * v) + 0.5
    return v * s, s


def forward_body(
    sizes, frame_entries, block, x_ref, sums_ref, other_ref, rim_ref, kernel_ref,
    hidden_ref, act_ref, clip_ref, padded, even_ref, odd_ref,
):
    forward_weights(kernel_ref, even_ref, odd_ref, sizes)
    mean, rate = moments(sums_ref[...] + other_ref[...], sizes.frames, frame_entries, sizes)

    def rim(rows, f, before):
        lanes = slice(sizes.pair - sizes.edge, sizes.pair) if before else slice(0, sizes.edge)
        v = rim_ref[rows, :].astype(F32)
        return silu_parts((v - mean[f : f + 1, lanes]) * rate[f : f + 1, lanes])[0]

    put_halo(rim, padded, sizes)

    def activate(p, _):
        for f in range(sizes.frames):
            v = x_ref[pl.ds(f * sizes.rows, sizes.rows), pair_lanes(p, sizes)].astype(F32)
            act = silu_parts((v - mean[f : f + 1]) * rate[f : f + 1])[0]
            lanes = pl.ds(pl.multiple_of(p * sizes.pair + sizes.edge, 128), sizes.pair)
            put_shifts(act, f, lanes, padded, sizes)
        return 0

    lax.fori_loop(0, sizes.pairs, activate, 0)
    act_ref[...] = padded[1]

    def step(b, carry):
        plain, square = carry
        p = b * block
        even = jnp.dot(windows(padded, p, block, False, sizes), even_ref[...], preferred_element_type=F32)
        odd = jnp.dot(windows(padded, p, block, True, sizes), odd_ref[...], preferred_element_type=F32)
        for q in range(block):
            rows = slice(q * sizes.pixels, (q + 1) * sizes.pixels)
            spatial = join(even[rows], odd[rows], sizes)
            lanes = pair_lanes(p + q, sizes)
            hidden = (x_ref[:, lanes].astype(F32) + spatial).astype(BF16)
            hidden_ref[:, lanes] = hidden
            wide = hidden.astype(F32)
            plain = plain + fold(wide)
            square = square + fold(wide * wide)
        return plain, square

    zero = jnp.zeros((8, sizes.pair), F32)
    plain, square = lax.fori_loop(0, sizes.pairs // block, step, (zero, zero))
    put_sums(clip_ref, plain, square)


def add_up(refs):
    total = refs[0][...]
    for ref in refs[1:]:
        total = total + ref[...]
    return total


def put_sums(target, plain, square):
    target[...] = jnp.zeros(target.shape, F32)
    target[0:1, :] = jnp.sum(plain, axis=0, keepdims=True)
    target[1:2, :] = jnp.sum(square, axis=0, keepdims=True)


def end_frames_body(sizes, cot_hbm, first_ref, second_ref, sems):
    even = lax.axis_index("seq") % 2 == 0
    last = sizes.pixels - sizes.rows
    copies = []
    for k, target in enumerate((first_ref, second_ref)):
        start = jnp.where(even, last, 0) if k == 0 else jnp.where(even, 0, last)
        rows = pl.ds(pl.multiple_of(start, 16), sizes.rows)
        copies.append(pltpu.make_async_copy(cot_hbm.at[rows, :], target, sems.at[k]))
    for copy in copies:
        copy.start()
    for copy in copies:
        copy.wait()


def neighbour_frames(cot, sizes):
    seqs = lax.axis_size("seq")
    first, second = call(
        functools.partial(end_frames_body, sizes),
        [struct((sizes.rows, sizes.width), BF16)] * 2,
        [pltpu.SemaphoreType.DMA((2,))],
        limit=SMALL_LIMIT,
        spaces=[pltpu.HBM],
        flops=CONV_COST // 3,
    )(cot)
    found = []
    for low, values in ((0, first), (1, second)):
        pairs = []
        for i in range(low, seqs - 1, 2):
            pairs += [(i, i + 1), (i + 1, i)]
        found.append(lax.ppermute(values, "seq", pairs))
    return found


def frame_taps(cot_ref, first_ref, second_ref, lanes, sizes):
    even = lax.axis_index("seq") % 2 == 0
    own, first, second = cot_ref[:, lanes], first_ref[:, lanes], second_ref[:, lanes]
    later = jnp.concatenate([own[sizes.rows :], jnp.where(even, first, second)], axis=0)
    earlier = jnp.concatenate([jnp.where(even, second, first), own[: sizes.pixels - sizes.rows]], axis=0)
    return later, own, earlier


def activation_grad_body(sizes, block, cot_ref, before_ref, after_ref, kernel_ref, dact_ref, even_ref, odd_ref):
    temporal_weights(kernel_ref, even_ref, odd_ref, sizes)

    def step(b, _):
        p = b * block
        found = []
        for odd, weights in ((False, even_ref), (True, odd_ref)):
            rows = []
            for q in range(block):
                start = (p + q) * sizes.pair + (sizes.pair - sizes.edge if odd else 0)
                lanes = pl.ds(pl.multiple_of(start, 128), sizes.edge)
                rows.append(
                    jnp.concatenate(frame_taps(cot_ref, before_ref, after_ref, lanes, sizes), axis=1)
                )
            found.append(
                lax.dot_general(
                    jnp.concatenate(rows, axis=0), weights[...], (((1,), (1,)), ((), ())),
                    preferred_element_type=F32,
                )
            )
        for q in range(block):
            rows = slice(q * sizes.pixels, (q + 1) * sizes.pixels)
            dact_ref[:, pair_lanes(p + q, sizes)] = join(found[0][rows], found[1][rows], sizes)
        return 0

    lax.fori_loop(0, sizes.pairs // block, step, 0)


def temporal_body(
    sizes, clip_entries, terms, hidden_ref, cot_ref, dact_ref, *refs
):
    clips, (act_ref, grad_ref, sums_ref, rim_ref, normed) = refs[:terms], refs[terms:]
    mean, rate = moments(add_up(clips), 1, clip_entries, sizes)

    def step(p, carry):
        plain, cross = carry
        lanes = pair_lanes(p, sizes)
        for f in range(sizes.frames):
            rows = pl.ds(f * sizes.rows, sizes.rows)
            tnormed = (hidden_ref[rows, lanes].astype(F32) - mean) * rate
            act, s = silu_parts(tnormed)
            act_ref[rows, lanes] = act.astype(BF16)
            normed[rows, lanes] = tnormed
            grad = dact_ref[rows, lanes] * (s * (1.0 + tnormed * (1.0 - s)))
            grad_ref[rows, lanes] = grad
            plain = plain + fold(grad)
            cross = cross + fold(grad * tnormed)
        return plain, cross

    zero = jnp.zeros((8, sizes.pair), F32)
    plain, cross = lax.fori_loop(0, sizes.pairs, step, (zero, zero))
    put_sums(sums_ref, plain, cross)
    for k, source in enumerate((grad_ref, normed, cot_ref)):
        store_edge(sizes, source, rim_ref, k * sizes.pixels)


def pack(total, start, rows, target):
    width = total.shape[1]
    full, used, half = width // 128, rows * width // 128, rows // 2
    lines = pl.ds(pl.multiple_of(start, 16), rows)
    for k in range(full):
        target[k * rows : (k + 1) * rows, :] = total[lines, k * 128 : (k + 1) * 128].astype(target.dtype)
    if width % 128:
        ends = total[lines, full * 128 :].astype(target.dtype)
        target[full * rows : used, :] = jnp.concatenate([ends[:half], ends[half:]], axis=1)
    target[used:, :] = jnp.zeros((target.shape[0] - used, 128), target.dtype)


def temporal_grad_body(sizes, block, act_ref, cot_ref, before_ref, after_ref, total):
    total[...] = jnp.zeros(total.shape, F32)
    channels = sizes.channels

    def step(b, _):
        acts, cots = [], []
        for q in range(block):
            lanes = pair_lanes(b * block + q, sizes)
            act = act_ref[:, lanes]
            acts += [act[:, :channels], act[:, channels:]]
            taps = frame_taps(cot_ref, before_ref, after_ref, lanes, sizes)
            for part in (slice(0, channels), slice(channels, 2 * channels)):
                cots.append(jnp.concatenate([t[:, part] for t in taps], axis=1))
        total[...] += lax.dot_general(
            jnp.concatenate(acts, axis=0), jnp.concatenate(cots, axis=0), (((0,), (0,)), ((), ())),
            preferred_element_type=F32,
        )
        return 0

    lax.fori_loop(0, sizes.pairs // block, step, 0)


def spatial_grad_body(
    sizes, clip_entries, terms, hidden_ref, cot_ref, grad_ref, rim_ref, act_ref, time_ref, *refs
):
    clips, sums = refs[:terms], refs[terms : 2 * terms]
    dtemp_ref, dspat_ref = refs[2 * terms : 2 * terms + 2]
    chunks, (padded, total) = refs[2 * terms + 2 : -2], refs[-2:]
    count = len(chunks) // 2
    mean, rate = moments(add_up(clips), 1, clip_entries, sizes)
    means = group_totals(add_up(sums), sizes) * (1.0 / clip_entries)
    plain, cross = means[0:1], means[1:2]

    def rim(rows, f, before):
        lanes = slice(sizes.pair - sizes.edge, sizes.pair) if before else slice(0, sizes.edge)
        at = [pl.ds(k * sizes.pixels + f * sizes.rows, sizes.rows) for k in range(3)]
        grad, tnormed, cot = (rim_ref[r, :] for r in at)
        dtemp = rate[:, lanes] * (grad - plain[:, lanes] - tnormed * cross[:, lanes])
        return (cot + dtemp.astype(BF16).astype(F32)).astype(BF16).astype(F32)

    put_halo(rim, padded, sizes)

    def combine(p, _):
        lanes = pair_lanes(p, sizes)
        for f in range(sizes.frames):
            rows = pl.ds(f * sizes.rows, sizes.rows)
            tnormed = (hidden_ref[rows, lanes].astype(F32) - mean) * rate
            dtemp = (rate * (grad_ref[rows, lanes] - plain - tnormed * cross)).astype(BF16)
            dtemp_ref[rows, lanes] = dtemp
            dspat = cot_ref[rows, lanes].astype(F32) + dtemp.astype(F32)
            put_shifts(
                dspat, f, pl.ds(pl.multiple_of(p * sizes.pair + sizes.edge, 128), sizes.pair), padded, sizes
            )
        return 0

    lax.fori_loop(0, sizes.pairs, combine, 0)
    dspat_ref[...] = padded[1]

    channels = sizes.channels
    own = 3 * channels
    total[:own, :] = jnp.zeros((own, own), F32)
    total[own:, :] = time_ref[...]
    block = min(4, sizes.pairs)

    def step(b, _):
        for odd in (False, True):
            left, right = [], []
            for q in range(block):
                p = block * b + q
                start = p * sizes.pair + (sizes.edge if odd else 0)
                left.append(act_ref[:, pl.ds(pl.multiple_of(start, 128), sizes.window)])
                both = pl.ds(pl.multiple_of(p * sizes.pair + sizes.edge, 128), sizes.pair)
                taps = []
                for i in range(3):
                    d = padded[2 - i, :, both]
                    d = d[:, channels:] if odd else d[:, :channels]
                    taps.append(d)
                right.append(jnp.concatenate(taps, axis=1))
            part = lax.dot_general(
                jnp.concatenate(left, axis=0), jnp.concatenate(right, axis=0), (((0,), (0,)), ((), ())),
                preferred_element_type=F32,
            )
            total[:own, :] += part[:own] if odd else part[sizes.slack :]
        return 0

    lax.fori_loop(0, sizes.pairs // block, step, 0)
    core = lax.axis_index("col")
    rows = total.shape[0] // 2 // count
    for n in range(count):
        pack(total, chunk_place(core, n, count) * rows, rows, chunks[n])
        pack(total, chunk_place(1 - core, n, count) * rows, rows, chunks[count + n])


def backward_body(
    sizes, frame_entries, block, x_ref, sums_ref, other_ref, dspat_ref, kernel_ref,
    grad_ref, out_ref, padded, plains, even_ref, odd_ref,
):
    backward_weights(kernel_ref, even_ref, odd_ref, sizes)
    mean, rate = moments(sums_ref[...] + other_ref[...], sizes.frames, frame_entries, sizes)

    def spread(k, _):
        lanes = pl.ds(pl.multiple_of(k * 128, 128), 128)
        for f in range(sizes.frames):
            rows = pl.ds(f * sizes.rows, sizes.rows)
            put_shifts(dspat_ref[rows, lanes].astype(F32), f, lanes, padded, sizes)
        return 0

    lax.fori_loop(0, sizes.padded // 128, spread, 0)
    plains[...] = jnp.zeros(plains.shape, F32)
    contract = (((1,), (1,)), ((), ()))

    def step(b, _):
        p = b * block
        even = lax.dot_general(
            windows(padded, p, block, False, sizes), even_ref[...], contract, preferred_element_type=F32
        )
        odd = lax.dot_general(
            windows(padded, p, block, True, sizes), odd_ref[...], contract, preferred_element_type=F32
        )
        for q in range(block):
            base = q * sizes.pixels
            for f in range(sizes.frames):
                at = slice(base + f * sizes.rows, base + (f + 1) * sizes.rows)
                dact = join(even[at], odd[at], sizes)
                rows, lanes = pl.ds(f * sizes.rows, sizes.rows), pair_lanes(p + q, sizes)
                normed = (x_ref[rows, lanes].astype(F32) - mean[f : f + 1]) * rate[f : f + 1]
                _, s = silu_parts(normed)
                grad = dact * (s * (1.0 + normed * (1.0 - s)))
                grad_ref[rows, lanes] = grad
                plains[f] += fold(grad)
                plains[sizes.frames + f] += fold(grad * normed)
        return 0

    lax.fori_loop(0, sizes.pairs // block, step, 0)
    for k in range(2 * sizes.frames):
        out_ref[k : k + 1, :] = jnp.sum(plains[k], axis=0, keepdims=True)


def finish_body(
    sizes, frame_entries, x_ref, sums_ref, other_ref, cot_ref, dtemp_ref, grad_ref, mine_ref, theirs_ref, out_ref
):
    mean, rate = moments(sums_ref[...] + other_ref[...], sizes.frames, frame_entries, sizes)
    means = group_totals(mine_ref[...] + theirs_ref[...], sizes) * (1.0 / frame_entries)

    def step(p, _):
        lanes = pair_lanes(p, sizes)
        for f in range(sizes.frames):
            rows = pl.ds(f * sizes.rows, sizes.rows)
            normed = (x_ref[rows, lanes].astype(F32) - mean[f : f + 1]) * rate[f : f + 1]
            dhidden = cot_ref[rows, lanes].astype(F32) + dtemp_ref[rows, lanes].astype(F32)
            plain, cross = means[f : f + 1], means[sizes.frames + f : sizes.frames + f + 1]
            out_ref[rows, lanes] = dhidden + rate[f : f + 1] * (grad_ref[rows, lanes] - plain - normed * cross)
        return 0

    lax.fori_loop(0, sizes.pairs, step, 0)


PHASES = ("dp", "seq")


def crossed():
    return lax.axis_size("col") == 2 and lax.axis_size("dp") == lax.axis_size("seq")


def place_of(core, phase):
    place = lax.axis_index(PHASES[phase])
    if crossed():
        place = jnp.where(core == 0, place, lax.axis_index(PHASES[1 - phase]))
    return place


def exchange(values, phase, bits):
    names = ("dp", "seq", "col")
    dps, seqs, cols = (lax.axis_size(name) for name in names)
    pairs = []
    for i in range(dps * seqs * cols):
        place = [i // (seqs * cols), i // cols % seqs, i % cols]
        place[phase ^ place[2] if crossed() else phase] ^= bits
        pairs.append((i, (place[0] * seqs + place[1]) * cols + place[2]))
    return lax.ppermute(values, names, pairs)


def chunk_place(core, bits, count):
    return core * count + (place_of(core, 0) ^ bits)


def unpack_body(sizes, scale, count, chunks, *refs):
    found, (spatial_hbm, temporal_hbm, staged, sems) = refs[: len(chunks)], refs[-4:]
    core = lax.axis_index("col")
    width = 3 * sizes.channels
    full, left = width // 128, width % 128
    rows = (width + sizes.channels) // 2 // count
    half = rows // 2

    def each(k, act):
        mine, bits = chunks[k]
        place = chunk_place(core if mine else 1 - core, bits, count)
        spatial = place < width // rows
        for inside, target, at in (
            (spatial, spatial_hbm, place), (jnp.logical_not(spatial), temporal_hbm, place - width // rows)
        ):

            @pl.when(inside)
            def _(target=target, at=at):
                lines = pl.ds(pl.multiple_of(at * rows, 16), rows)
                for i in range(3):
                    act(pltpu.make_async_copy(staged.at[k, i], target.at[i, lines, :], sems.at[3 * k + i]))

    for k, chunk in enumerate(found):
        ends = chunk[full * rows : full * rows + half, :].astype(F32)
        for second in range(2):
            at = second * half
            taken = [chunk[b * rows + at : b * rows + at + half, :].astype(F32) for b in range(full)]
            taken.append(ends[:, left:] if second else ends[:, :left])
            wide = jnp.concatenate(taken, axis=1) * scale
            for i in range(3):
                staged[k, i, at : at + half, :] = wide[:, i * sizes.channels : (i + 1) * sizes.channels]
        each(k, lambda copy: copy.start())
    for k in range(len(found)):
        each(k, lambda copy: copy.wait())


def unpack(sizes, scale, count, found, before=None):
    channels = sizes.channels
    outs = [struct((3, 3 * channels, channels), F32), struct((3, channels, channels), F32)]
    rows = 2 * channels // count
    carried = [] if before is None else list(before)
    return call(
        functools.partial(unpack_body, sizes, scale, count, tuple(found)),
        outs,
        [pltpu.VMEM((len(found), 3, rows, channels), F32), pltpu.SemaphoreType.DMA((3 * len(found),))],
        flops=1000,
        moved=1000,
        spaces=[pltpu.VMEM] * len(found) + [pltpu.HBM] * len(carried),
        out_spaces=[pltpu.HBM] * 2,
        aliases={len(found) + k: k for k in range(len(carried))},
    )(*found.values(), *carried)


def swap(values, axis, bit):
    count = lax.axis_size(axis)
    return lax.ppermute(values, axis, [(i, i ^ bit) for i in range(count)])


def from_all(values, axis):
    return [values] + [swap(values, axis, s) for s in range(1, lax.axis_size(axis))]


def added(terms):
    total = terms[0].astype(F32)
    for term in terms[1:]:
        total = total + term.astype(F32)
    return total


def place_rows(phase, bits, rows):
    place = place_of(lax.axis_index("col"), phase)
    return pl.ds(pl.multiple_of((place ^ bits) * rows, 16), rows)


def split_body(phase, terms, *refs):
    for bits, target in enumerate(refs[terms:]):
        rows = place_rows(phase, bits, target.shape[0])
        target[...] = added([ref[rows, :] for ref in refs[:terms]]).astype(target.dtype)


def scattered(terms, phase):
    count = lax.axis_size(PHASES[phase])
    chunk = (terms[0].shape[0] // count, terms[0].shape[1])
    own, *others = call(
        functools.partial(split_body, phase, len(terms)),
        [struct(chunk, F32)] + [struct(chunk, BF16)] * (count - 1),
        limit=SMALL_LIMIT,
    )(*terms)
    return [own] + [exchange(values, phase, n + 1) for n, values in enumerate(others)]


def gather_body(phase, *refs):
    for bits, part in enumerate(refs[:-1]):
        refs[-1][place_rows(phase, bits, part.shape[0]), :] = part[...]


def gathered(chunk, phase):
    count = lax.axis_size(PHASES[phase])
    parts = [chunk] + [exchange(chunk, phase, n) for n in range(1, count)]
    return call(
        functools.partial(gather_body, phase),
        struct((chunk.shape[0] * count, chunk.shape[1]), chunk.dtype),
        limit=SMALL_LIMIT,
    )(*parts)


def shards(latents, spatial_kernel, temporal_kernel, cotangent):
    _, frames, rows, width = latents.shape
    channels = spatial_kernel.shape[2]
    sizes = Sizes(frames, rows, width // channels, channels)
    cols, seqs = lax.axis_size("col"), lax.axis_size("seq")
    frame_entries = float(rows * sizes.columns * cols * (channels // GROUPS))
    clip_entries = frame_entries * frames * seqs
    pixels = lax.axis_size("dp") * seqs * cols * sizes.pixels * sizes.columns
    grad_scale = 1.0 / math.sqrt(pixels)

    x = latents.reshape(sizes.pixels, width)
    cot = cotangent.reshape(sizes.pixels, width)
    sum_shape = struct((8, sizes.pair), F32)
    frame_shape = struct((2 * frames, sizes.pair), F32)
    padded_scratch = pltpu.VMEM((3, sizes.pixels, sizes.padded), BF16)
    slack = sizes.slack

    before, after = neighbour_frames(cot, sizes)

    sums, edge = call(
        functools.partial(latent_sums_body, sizes),
        [frame_shape, struct((sizes.pixels, sizes.edge), BF16)],
        flops=CONV_COST // 3,
    )(x)
    other = swap(sums, "col", 1)
    rim = swap(edge, "col", 1)
    hidden, act, clip = call(
        functools.partial(forward_body, sizes, frame_entries, min(4, sizes.pairs)),
        [struct((sizes.pixels, width), BF16), struct((sizes.pixels, sizes.padded), BF16), sum_shape],
        [padded_scratch] + [pltpu.VMEM((3 * sizes.window, sizes.edge), BF16)] * 2,
        flops=CONV_COST,
    )(x, sums, other, rim, spatial_kernel)
    clips = from_all(clip + swap(clip, "col", 1), "seq")
    dact = call(
        functools.partial(activation_grad_body, sizes, min(4, sizes.pairs)),
        struct((sizes.pixels, width), F32),
        [pltpu.VMEM((sizes.edge, 3 * sizes.edge), BF16)] * 2,
        flops=CONV_COST // 3,
    )(cot, before, after, temporal_kernel)
    tact, tgrad, means, rims = call(
        functools.partial(temporal_body, sizes, clip_entries, seqs),
        [
            struct((sizes.pixels, width), BF16),
            struct((sizes.pixels, width), F32),
            sum_shape,
            struct((3 * sizes.pixels, sizes.edge), F32),
        ],
        [pltpu.VMEM((sizes.pixels, width), F32)],
        flops=CONV_COST // 3,
    )(hidden, cot, dact, *clips)
    means = from_all(means + swap(means, "col", 1), "seq")
    rims = swap(rims, "col", 1)
    temporal_grad = call(
        functools.partial(temporal_grad_body, sizes, min(4, sizes.pairs)),
        struct((channels, 3 * channels), F32),
        flops=CONV_COST // 3,
    )(tact, cot, before, after)

    count, after_count = (lax.axis_size(name) for name in PHASES)
    chunk_rows = 4 * channels // (2 * count) * 3 * channels // 128
    chunk = (-(-chunk_rows // (16 * after_count)) * 16 * after_count, 128)
    dtemp, dspat, *chunks = call(
        functools.partial(spatial_grad_body, sizes, clip_entries, seqs),
        [
            struct((sizes.pixels, width), BF16),
            struct((sizes.pixels, sizes.padded), BF16),
        ]
        + [struct(chunk, F32)] * count
        + [struct(chunk, BF16)] * count,
        [
            padded_scratch,
            pltpu.VMEM((4 * channels, 3 * channels), F32),
        ],
        flops=CONV_COST,
    )(hidden, cot, tgrad, rims, act, temporal_grad, *clips, *means)
    chunks = [chunks[n] + swap(chunks[count + n], "col", 1).astype(F32) for n in range(count)]
    sends = [values.astype(BF16) for values in chunks[1:]]
    sends, dspat = lax.optimization_barrier((sends, dspat))
    found = [exchange(values, 0, n + 1) for n, values in enumerate(sends)]
    dnormed, mine = call(
        functools.partial(backward_body, sizes, frame_entries, min(4, sizes.pairs)),
        [struct((sizes.pixels, width), F32), frame_shape],
        [padded_scratch, pltpu.VMEM((2 * frames, 8, sizes.pair), F32)]
        + [pltpu.VMEM((sizes.edge, 3 * sizes.window), BF16)] * 2,
        flops=CONV_COST,
    )(x, sums, other, dspat, spatial_kernel)
    found, (dnormed, mine) = lax.optimization_barrier((found, (dnormed, mine)))
    theirs = swap(mine, "col", 1)
    terms, theirs = lax.optimization_barrier((scattered(chunks[:1] + found, 1), theirs))
    total = added(terms)
    grad_latents = call(
        functools.partial(finish_body, sizes, frame_entries), struct((sizes.pixels, width), F32),
        flops=CONV_COST // 3,
    )(x, sums, other, cot, dtemp, dnormed, mine, theirs)
    part = gathered(total.astype(BF16), 1)
    near = [exchange(part, 0, 1 << k) for k in range(count.bit_length() - 1)]
    part, near, grad_latents = lax.optimization_barrier((part, near, grad_latents))
    parts = [part] + [None] * (count - 1)
    for n in range(1, count):
        parts[n] = exchange(parts[n & (n - 1)], 0, n & -n) if n & (n - 1) else near[n.bit_length() - 1]
    found = {}
    for n, part in enumerate(parts[:-1]):
        found[True, n], found[False, n] = part, swap(part, "col", 1)
    grads = unpack(sizes, grad_scale, count, found)
    part, grads = lax.optimization_barrier((parts[-1], grads))
    last = {(True, count - 1): part, (False, count - 1): swap(part, "col", 1)}
    spatial_grad, temporal_grad = unpack(sizes, grad_scale, count, last, grads)
    return (
        grad_latents.reshape(latents.shape),
        spatial_grad.reshape(spatial_kernel.shape),
        temporal_grad.reshape(temporal_kernel.shape),
    )


def solution(mesh):
    in_specs = (P("dp", "seq", None, "col"), P(), P(), P("dp", "seq", None, "col"))
    out_specs = (P("dp", "seq", None, "col"), P(), P())
    return jax.shard_map(shards, mesh=mesh, in_specs=in_specs, out_specs=out_specs, check_vma=False)
```

```python
import functools
import math

import jax
import jax.numpy as jnp
from jax import lax
from jax.experimental import pallas as pl
from jax.experimental.pallas import tpu as pltpu
from jax.sharding import PartitionSpec as P

GROUPS = 32
EPSILON = 1e-05
F32 = jnp.float32
BF16 = jnp.bfloat16
VMEM_LIMIT = 20 * 1024 * 1024
CONV_LIMIT = 28 * 1024 * 1024
SMALL_LIMIT = 4 * 1024 * 1024
CONV_COST = 12_000_000_000


def call(body, outs, scratch=(), flops=0, moved=0, limit=VMEM_LIMIT, spaces=None, out_spaces=None, aliases=None):
    specs = {} if spaces is None else {"in_specs": [pl.BlockSpec(memory_space=space) for space in spaces]}
    return pl.pallas_call(
        body,
        out_shape=outs,
        **specs,
        out_specs=(
            jax.tree.map(lambda _: pl.BlockSpec(memory_space=pltpu.VMEM), outs)
            if out_spaces is None
            else [pl.BlockSpec(memory_space=space) for space in out_spaces]
        ),
        scratch_shapes=list(scratch),
        input_output_aliases=aliases or {},
        compiler_params=pltpu.CompilerParams(vmem_limit_bytes=limit),
        cost_estimate=pl.CostEstimate(flops=flops, bytes_accessed=moved, transcendentals=0),
    )


def struct(shape, kind):
    return jax.ShapeDtypeStruct(shape, kind)


class Sizes:
    def __init__(self, frames, rows, columns, channels):
        self.frames = frames
        self.rows = rows
        self.columns = columns
        self.channels = channels
        self.pixels = frames * rows
        self.width = columns * channels
        self.pair = 2 * channels
        self.pairs = columns // 2
        self.edge = -(-channels // 128) * 128
        self.slack = self.edge - channels
        self.window = 3 * channels + self.slack
        self.padded = self.width + 2 * self.edge


def group_totals(sums, sizes):
    size = sizes.channels // GROUPS

    def member(shape, lane_dim):
        lane = lax.broadcasted_iota(jnp.int32, shape, lane_dim)
        group = lax.broadcasted_iota(jnp.int32, shape, 1 - lane_dim)
        channel = jnp.where(lane >= sizes.channels, lane - sizes.channels, lane)
        return ((channel >= group * size) & (channel < group * size + size)).astype(F32)

    high = lax.Precision.HIGHEST
    by_group = jnp.dot(sums, member((sizes.pair, 128), 0), precision=high, preferred_element_type=F32)
    return jnp.dot(by_group, member((128, sizes.pair), 1), precision=high, preferred_element_type=F32)


def moments(sums, half, entries, sizes):
    totals = group_totals(sums, sizes) * (1.0 / entries)
    mean = totals[0:half]
    rate = lax.rsqrt(totals[half : 2 * half] - mean * mean + EPSILON)
    return mean, rate


def fold(values):
    return jnp.sum(values.reshape(values.shape[0] // 8, 8, values.shape[1]), axis=0)


def pair_lanes(p, sizes):
    return pl.ds(pl.multiple_of(p * sizes.pair, 128), sizes.pair)


def join(even, odd, sizes):
    cut = sizes.edge - 128
    middle = even[:, cut:] + odd[:, :128]
    return jnp.concatenate([even[:, :cut], middle, odd[:, 128:]], axis=1)


def latent_sums_body(sizes, x_ref, sums_ref, edge_ref):
    def frame(f):
        rows = pl.ds(f * sizes.rows, sizes.rows)

        def step(p, carry):
            plain, square = carry
            v = x_ref[rows, pair_lanes(p, sizes)].astype(F32)
            return plain + fold(v), square + fold(v * v)

        zero = jnp.zeros((8, sizes.pair), F32)
        plain, square = lax.fori_loop(0, sizes.pairs, step, (zero, zero))
        return jnp.sum(plain, axis=0, keepdims=True), jnp.sum(square, axis=0, keepdims=True)

    found = [frame(f) for f in range(sizes.frames)]
    for f, (plain, square) in enumerate(found):
        sums_ref[f : f + 1, :] = plain
        sums_ref[sizes.frames + f : sizes.frames + f + 1, :] = square
    store_edge(sizes, x_ref, edge_ref)


def store_edge(sizes, source, target, at=0):
    left = lax.axis_index("col") == 0
    rows = pl.ds(at, sizes.pixels)

    @pl.when(left)
    def _():
        target[rows, :] = source[:, sizes.width - sizes.edge : sizes.width].astype(target.dtype)

    @pl.when(jnp.logical_not(left))
    def _():
        target[rows, :] = source[:, 0 : sizes.edge].astype(target.dtype)


def row_shifts(values, sizes):
    row = lax.broadcasted_iota(jnp.int32, values.shape, 0)
    down = jnp.where(row == 0, 0.0, pltpu.roll(values, 1, 0))
    up = jnp.where(row == sizes.rows - 1, 0.0, pltpu.roll(values, sizes.rows - 1, 0))
    return down, values, up


def put_shifts(values, frame, lanes, target, sizes):
    rows = pl.ds(frame * sizes.rows, sizes.rows)
    for i, moved in enumerate(row_shifts(values, sizes)):
        target[i, rows, lanes] = moved.astype(BF16)


def put_halo(of_frame, target, sizes):
    left = lax.axis_index("col") == 0
    for f in range(sizes.frames):
        rows = pl.ds(f * sizes.rows, sizes.rows)
        before, after = of_frame(rows, f, True), of_frame(rows, f, False)
        put_shifts(jnp.where(left, 0.0, before), f, pl.ds(0, sizes.edge), target, sizes)
        put_shifts(
            jnp.where(left, after, 0.0), f, pl.ds(sizes.edge + sizes.width, sizes.edge), target, sizes
        )


class Tile:
    def __init__(self, t, sizes):
        channels = sizes.channels
        low, high = 256 * t // channels, (256 * t + 255) // channels
        self.lanes = slice(256 * t, 256 * t + 256)
        self.columns = []
        for column in range(low, high + 1):
            first = max(256 * t, column * channels)
            last = min(256 * t + 256, (column + 1) * channels)
            self.columns.append((column, first - column * channels, last - column * channels, first - 256 * t))
        self.taken = range(low - 1, high + 2)
        begin = sizes.edge + (low - 1) * channels
        end = sizes.edge + (high + 2) * channels
        self.start = begin // 128 * 128
        self.head = begin - self.start
        self.size = -(-(end - self.start) // 128) * 128
        self.tail = self.size - self.head - len(self.taken) * channels


def tiles_of(sizes):
    return [Tile(t, sizes) for t in range(4 * sizes.channels // 256)]


def tile_scratch(sizes):
    return [pltpu.VMEM((3 * tile.size, 256), BF16) for tile in tiles_of(sizes)]


def tile_scratch_back(sizes):
    return [pltpu.VMEM((256, 3 * tile.size), BF16) for tile in tiles_of(sizes)]


def forward_weights(kernel_ref, tiles, targets, sizes):
    channels = sizes.channels
    for tile, target in zip(tiles, targets):
        for i in range(3):
            at = i * tile.size
            if tile.head:
                target[at : at + tile.head, :] = jnp.zeros((tile.head, 256), BF16)
            at += tile.head
            for taken in tile.taken:
                parts = []
                for column, first, last, _ in tile.columns:
                    j = taken - column + 1
                    inside = 0 <= j <= 2
                    parts.append(kernel_ref[i, j][:, first:last] if inside else jnp.zeros((channels, last - first), BF16))
                target[at : at + channels, :] = jnp.concatenate(parts, axis=1) if len(parts) > 1 else parts[0]
                at += channels
            if tile.tail:
                target[at : at + tile.tail, :] = jnp.zeros((tile.tail, 256), BF16)


def backward_weights(kernel_ref, tiles, targets, sizes):
    channels = sizes.channels
    for tile, target in zip(tiles, targets):
        for i in range(3):
            lanes = slice(i * tile.size, (i + 1) * tile.size)
            for column, first, last, at in tile.columns:
                count = last - first
                parts = [jnp.zeros((count, tile.head), BF16)] if tile.head else []
                for taken in tile.taken:
                    j = taken - column + 1
                    inside = 0 <= j <= 2
                    parts.append(kernel_ref[2 - i, 2 - j][first:last, :] if inside else jnp.zeros((count, channels), BF16))
                if tile.tail:
                    parts.append(jnp.zeros((count, tile.tail), BF16))
                target[at : at + count, lanes] = jnp.concatenate(parts, axis=1)


def temporal_weights(kernel_ref, even_ref, odd_ref, sizes):
    channels, slack, edge = sizes.channels, sizes.slack, sizes.edge
    for weights in (even_ref, odd_ref):
        weights[...] = jnp.zeros(weights.shape, BF16)
    zeros = jnp.zeros((channels, slack), BF16)
    for i in range(3):
        lanes = slice(i * edge, (i + 1) * edge)
        even_ref[0:channels, lanes] = jnp.concatenate([kernel_ref[i], zeros], axis=1)
        odd_ref[slack : slack + channels, lanes] = jnp.concatenate([zeros, kernel_ref[i]], axis=1)


def windows(padded_ref, tile, sizes):
    found = []
    for start in range(tile.start, tile.start + sizes.width, 2 * sizes.pair):
        lanes = slice(start, start + tile.size)
        found.append(jnp.concatenate([padded_ref[i, :, lanes] for i in range(3)], axis=1))
    return jnp.concatenate(found, axis=0)


def silu_parts(v):
    s = 0.5 * jnp.tanh(0.5 * v) + 0.5
    return v * s, s


def forward_body(
    sizes, frame_entries, x_ref, sums_ref, other_ref, rim_ref, kernel_ref,
    hidden_ref, act_ref, clip_ref, padded, plain, square, *weights
):
    tiles = tiles_of(sizes)
    forward_weights(kernel_ref, tiles, weights, sizes)
    mean, rate = moments(sums_ref[...] + other_ref[...], sizes.frames, frame_entries, sizes)

    def rim(rows, f, before):
        lanes = slice(sizes.pair - sizes.edge, sizes.pair) if before else slice(0, sizes.edge)
        v = rim_ref[rows, :].astype(F32)
        return silu_parts((v - mean[f : f + 1, lanes]) * rate[f : f + 1, lanes])[0]

    put_halo(rim, padded, sizes)

    def activate(p, _):
        for f in range(sizes.frames):
            v = x_ref[pl.ds(f * sizes.rows, sizes.rows), pair_lanes(p, sizes)].astype(F32)
            act = silu_parts((v - mean[f : f + 1]) * rate[f : f + 1])[0]
            lanes = pl.ds(pl.multiple_of(p * sizes.pair + sizes.edge, 128), sizes.pair)
            put_shifts(act, f, lanes, padded, sizes)
        return 0

    lax.fori_loop(0, sizes.pairs, activate, 0)
    act_ref[...] = padded[1]

    for tile, weight in zip(tiles, weights):
        spatial = jnp.dot(windows(padded, tile, sizes), weight[...], preferred_element_type=F32)
        sums = [jnp.zeros((8, 256), F32)] * 2
        for q in range(sizes.pairs // 2):
            lanes = slice(q * 2 * sizes.pair + tile.lanes.start, q * 2 * sizes.pair + tile.lanes.stop)
            hidden = x_ref[:, lanes].astype(F32) + spatial[q * sizes.pixels : (q + 1) * sizes.pixels]
            hidden = hidden.astype(BF16)
            hidden_ref[:, lanes] = hidden
            wide = hidden.astype(F32)
            sums = [sums[0] + fold(wide), sums[1] + fold(wide * wide)]
        plain[:, tile.lanes], square[:, tile.lanes] = sums
    put_sums(clip_ref, *(both[:, : sizes.pair] + both[:, sizes.pair :] for both in (plain, square)))


def add_up(refs):
    total = refs[0][...]
    for ref in refs[1:]:
        total = total + ref[...]
    return total


def put_sums(target, plain, square):
    target[...] = jnp.zeros(target.shape, F32)
    target[0:1, :] = jnp.sum(plain, axis=0, keepdims=True)
    target[1:2, :] = jnp.sum(square, axis=0, keepdims=True)


def end_frames_body(sizes, cot_hbm, first_ref, second_ref, sems):
    even = lax.axis_index("seq") % 2 == 0
    last = sizes.pixels - sizes.rows
    copies = []
    for k, target in enumerate((first_ref, second_ref)):
        start = jnp.where(even, last, 0) if k == 0 else jnp.where(even, 0, last)
        rows = pl.ds(pl.multiple_of(start, 16), sizes.rows)
        copies.append(pltpu.make_async_copy(cot_hbm.at[rows, :], target, sems.at[k]))
    for copy in copies:
        copy.start()
    for copy in copies:
        copy.wait()


def neighbour_frames(cot, sizes):
    seqs = lax.axis_size("seq")
    first, second = call(
        functools.partial(end_frames_body, sizes),
        [struct((sizes.rows, sizes.width), BF16)] * 2,
        [pltpu.SemaphoreType.DMA((2,))],
        limit=SMALL_LIMIT,
        spaces=[pltpu.HBM],
        flops=CONV_COST // 3,
    )(cot)
    found = []
    for low, values in ((0, first), (1, second)):
        pairs = []
        for i in range(low, seqs - 1, 2):
            pairs += [(i, i + 1), (i + 1, i)]
        found.append(lax.ppermute(values, "seq", pairs))
    return found


def frame_taps(cot_ref, first_ref, second_ref, lanes, sizes):
    even = lax.axis_index("seq") % 2 == 0
    own, first, second = cot_ref[:, lanes], first_ref[:, lanes], second_ref[:, lanes]
    later = jnp.concatenate([own[sizes.rows :], jnp.where(even, first, second)], axis=0)
    earlier = jnp.concatenate([jnp.where(even, second, first), own[: sizes.pixels - sizes.rows]], axis=0)
    return later, own, earlier


def activation_grad_body(sizes, block, cot_ref, before_ref, after_ref, kernel_ref, dact_ref, even_ref, odd_ref):
    temporal_weights(kernel_ref, even_ref, odd_ref, sizes)

    def step(b, _):
        p = b * block
        found = []
        for odd, weights in ((False, even_ref), (True, odd_ref)):
            rows = []
            for q in range(block):
                start = (p + q) * sizes.pair + (sizes.pair - sizes.edge if odd else 0)
                lanes = pl.ds(pl.multiple_of(start, 128), sizes.edge)
                rows.append(
                    jnp.concatenate(frame_taps(cot_ref, before_ref, after_ref, lanes, sizes), axis=1)
                )
            found.append(
                lax.dot_general(
                    jnp.concatenate(rows, axis=0), weights[...], (((1,), (1,)), ((), ())),
                    preferred_element_type=F32,
                )
            )
        for q in range(block):
            rows = slice(q * sizes.pixels, (q + 1) * sizes.pixels)
            dact_ref[:, pair_lanes(p + q, sizes)] = join(found[0][rows], found[1][rows], sizes)
        return 0

    lax.fori_loop(0, sizes.pairs // block, step, 0)


def temporal_body(
    sizes, clip_entries, terms, hidden_ref, cot_ref, dact_ref, *refs
):
    clips, (act_ref, grad_ref, sums_ref, rim_ref, normed) = refs[:terms], refs[terms:]
    mean, rate = moments(add_up(clips), 1, clip_entries, sizes)

    def step(p, carry):
        plain, cross = carry
        lanes = pair_lanes(p, sizes)
        for f in range(sizes.frames):
            rows = pl.ds(f * sizes.rows, sizes.rows)
            tnormed = (hidden_ref[rows, lanes].astype(F32) - mean) * rate
            act, s = silu_parts(tnormed)
            act_ref[rows, lanes] = act.astype(BF16)
            normed[rows, lanes] = tnormed
            grad = dact_ref[rows, lanes] * (s * (1.0 + tnormed * (1.0 - s)))
            grad_ref[rows, lanes] = grad
            plain = plain + fold(grad)
            cross = cross + fold(grad * tnormed)
        return plain, cross

    zero = jnp.zeros((8, sizes.pair), F32)
    plain, cross = lax.fori_loop(0, sizes.pairs, step, (zero, zero))
    put_sums(sums_ref, plain, cross)
    for k, source in enumerate((grad_ref, normed, cot_ref)):
        store_edge(sizes, source, rim_ref, k * sizes.pixels)


def pack(total, start, rows, target):
    width = total.shape[1]
    full, used, half = width // 128, rows * width // 128, rows // 2
    lines = pl.ds(pl.multiple_of(start, 16), rows)
    for k in range(full):
        target[k * rows : (k + 1) * rows, :] = total[lines, k * 128 : (k + 1) * 128].astype(target.dtype)
    if width % 128:
        ends = total[lines, full * 128 :].astype(target.dtype)
        target[full * rows : used, :] = jnp.concatenate([ends[:half], ends[half:]], axis=1)
    target[used:, :] = jnp.zeros((target.shape[0] - used, 128), target.dtype)


def temporal_grad_body(sizes, block, act_ref, cot_ref, before_ref, after_ref, total):
    total[...] = jnp.zeros(total.shape, F32)
    channels = sizes.channels

    def step(b, _):
        acts, cots = [], []
        for q in range(block):
            lanes = pair_lanes(b * block + q, sizes)
            act = act_ref[:, lanes]
            acts += [act[:, :channels], act[:, channels:]]
            taps = frame_taps(cot_ref, before_ref, after_ref, lanes, sizes)
            for part in (slice(0, channels), slice(channels, 2 * channels)):
                cots.append(jnp.concatenate([t[:, part] for t in taps], axis=1))
        total[...] += lax.dot_general(
            jnp.concatenate(acts, axis=0), jnp.concatenate(cots, axis=0), (((0,), (0,)), ((), ())),
            preferred_element_type=F32,
        )
        return 0

    lax.fori_loop(0, sizes.pairs // block, step, 0)


def spatial_grad_body(
    sizes, clip_entries, terms, hidden_ref, cot_ref, grad_ref, rim_ref, act_ref, time_ref, *refs
):
    clips, sums = refs[:terms], refs[terms : 2 * terms]
    dtemp_ref, dspat_ref = refs[2 * terms : 2 * terms + 2]
    chunks, (padded, total) = refs[2 * terms + 2 : -2], refs[-2:]
    count = len(chunks) // 2
    mean, rate = moments(add_up(clips), 1, clip_entries, sizes)
    means = group_totals(add_up(sums), sizes) * (1.0 / clip_entries)
    plain, cross = means[0:1], means[1:2]

    def rim(rows, f, before):
        lanes = slice(sizes.pair - sizes.edge, sizes.pair) if before else slice(0, sizes.edge)
        at = [pl.ds(k * sizes.pixels + f * sizes.rows, sizes.rows) for k in range(3)]
        grad, tnormed, cot = (rim_ref[r, :] for r in at)
        dtemp = rate[:, lanes] * (grad - plain[:, lanes] - tnormed * cross[:, lanes])
        return (cot + dtemp.astype(BF16).astype(F32)).astype(BF16).astype(F32)

    put_halo(rim, padded, sizes)

    def combine(p, _):
        lanes = pair_lanes(p, sizes)
        for f in range(sizes.frames):
            rows = pl.ds(f * sizes.rows, sizes.rows)
            tnormed = (hidden_ref[rows, lanes].astype(F32) - mean) * rate
            dtemp = (rate * (grad_ref[rows, lanes] - plain - tnormed * cross)).astype(BF16)
            dtemp_ref[rows, lanes] = dtemp
            dspat = cot_ref[rows, lanes].astype(F32) + dtemp.astype(F32)
            put_shifts(
                dspat, f, pl.ds(pl.multiple_of(p * sizes.pair + sizes.edge, 128), sizes.pair), padded, sizes
            )
        return 0

    lax.fori_loop(0, sizes.pairs, combine, 0)
    dspat_ref[...] = padded[1]

    channels = sizes.channels
    own = 3 * channels
    total[:own, :] = jnp.zeros((own, own), F32)
    total[own:, :] = time_ref[...]
    block = min(4, sizes.pairs)

    def step(b, _):
        for odd in (False, True):
            left, right = [], []
            for q in range(block):
                p = block * b + q
                start = p * sizes.pair + (sizes.edge if odd else 0)
                left.append(act_ref[:, pl.ds(pl.multiple_of(start, 128), sizes.window)])
                both = pl.ds(pl.multiple_of(p * sizes.pair + sizes.edge, 128), sizes.pair)
                taps = []
                for i in range(3):
                    d = padded[2 - i, :, both]
                    d = d[:, channels:] if odd else d[:, :channels]
                    taps.append(d)
                right.append(jnp.concatenate(taps, axis=1))
            part = lax.dot_general(
                jnp.concatenate(left, axis=0), jnp.concatenate(right, axis=0), (((0,), (0,)), ((), ())),
                preferred_element_type=F32,
            )
            total[:own, :] += part[:own] if odd else part[sizes.slack :]
        return 0

    lax.fori_loop(0, sizes.pairs // block, step, 0)
    core = lax.axis_index("col")
    rows = total.shape[0] // 2 // count
    for n in range(count):
        pack(total, chunk_place(core, n, count) * rows, rows, chunks[n])
        pack(total, chunk_place(1 - core, n, count) * rows, rows, chunks[count + n])


def backward_body(
    sizes, frame_entries, x_ref, sums_ref, other_ref, dspat_ref, kernel_ref,
    grad_ref, out_ref, padded, plains, *weights
):
    tiles = tiles_of(sizes)
    backward_weights(kernel_ref, tiles, weights, sizes)
    mean, rate = moments(sums_ref[...] + other_ref[...], sizes.frames, frame_entries, sizes)

    def spread(k, _):
        lanes = pl.ds(pl.multiple_of(k * 128, 128), 128)
        for f in range(sizes.frames):
            rows = pl.ds(f * sizes.rows, sizes.rows)
            put_shifts(dspat_ref[rows, lanes].astype(F32), f, lanes, padded, sizes)
        return 0

    lax.fori_loop(0, sizes.padded // 128, spread, 0)
    mean, rate = (jnp.concatenate([values, values], axis=1) for values in (mean, rate))
    for tile, weight in zip(tiles, weights):
        dact = lax.dot_general(
            windows(padded, tile, sizes), weight[...], (((1,), (1,)), ((), ())), preferred_element_type=F32
        )
        for f in range(sizes.frames):
            rows = pl.ds(f * sizes.rows, sizes.rows)
            sums = [jnp.zeros((8, 256), F32)] * 2
            for q in range(sizes.pairs // 2):
                lanes = slice(q * 2 * sizes.pair + tile.lanes.start, q * 2 * sizes.pair + tile.lanes.stop)
                normed = (x_ref[rows, lanes].astype(F32) - mean[f : f + 1, tile.lanes]) * rate[f : f + 1, tile.lanes]
                _, s = silu_parts(normed)
                at = q * sizes.pixels + f * sizes.rows
                grad = dact[at : at + sizes.rows] * (s * (1.0 + normed * (1.0 - s)))
                grad_ref[rows, lanes] = grad
                sums = [sums[0] + fold(grad), sums[1] + fold(grad * normed)]
            plains[f, :, tile.lanes], plains[sizes.frames + f, :, tile.lanes] = sums
    for k in range(2 * sizes.frames):
        both = jnp.sum(plains[k], axis=0, keepdims=True)
        out_ref[k : k + 1, :] = both[:, : sizes.pair] + both[:, sizes.pair :]


def finish_body(
    sizes, frame_entries, x_ref, sums_ref, other_ref, cot_ref, dtemp_ref, grad_ref, mine_ref, theirs_ref, out_ref
):
    mean, rate = moments(sums_ref[...] + other_ref[...], sizes.frames, frame_entries, sizes)
    means = group_totals(mine_ref[...] + theirs_ref[...], sizes) * (1.0 / frame_entries)

    def step(p, _):
        lanes = pair_lanes(p, sizes)
        for f in range(sizes.frames):
            rows = pl.ds(f * sizes.rows, sizes.rows)
            normed = (x_ref[rows, lanes].astype(F32) - mean[f : f + 1]) * rate[f : f + 1]
            dhidden = cot_ref[rows, lanes].astype(F32) + dtemp_ref[rows, lanes].astype(F32)
            plain, cross = means[f : f + 1], means[sizes.frames + f : sizes.frames + f + 1]
            out_ref[rows, lanes] = dhidden + rate[f : f + 1] * (grad_ref[rows, lanes] - plain - normed * cross)
        return 0

    lax.fori_loop(0, sizes.pairs, step, 0)


PHASES = ("dp", "seq")


def crossed():
    return lax.axis_size("col") == 2 and lax.axis_size("dp") == lax.axis_size("seq")


def place_of(core, phase):
    place = lax.axis_index(PHASES[phase])
    if crossed():
        place = jnp.where(core == 0, place, lax.axis_index(PHASES[1 - phase]))
    return place


def exchange(values, phase, bits):
    names = ("dp", "seq", "col")
    dps, seqs, cols = (lax.axis_size(name) for name in names)
    pairs = []
    for i in range(dps * seqs * cols):
        place = [i // (seqs * cols), i // cols % seqs, i % cols]
        place[phase ^ place[2] if crossed() else phase] ^= bits
        pairs.append((i, (place[0] * seqs + place[1]) * cols + place[2]))
    return lax.ppermute(values, names, pairs)


def chunk_place(core, bits, count):
    return core * count + (place_of(core, 0) ^ bits)


def unpack_body(sizes, scale, count, chunks, *refs):
    found, (spatial_hbm, temporal_hbm, staged, sems) = refs[: len(chunks)], refs[-4:]
    core = lax.axis_index("col")
    width = 3 * sizes.channels
    full, left = width // 128, width % 128
    rows = (width + sizes.channels) // 2 // count
    half = rows // 2

    def each(k, act):
        mine, bits = chunks[k]
        place = chunk_place(core if mine else 1 - core, bits, count)
        spatial = place < width // rows
        for inside, target, at in (
            (spatial, spatial_hbm, place), (jnp.logical_not(spatial), temporal_hbm, place - width // rows)
        ):

            @pl.when(inside)
            def _(target=target, at=at):
                lines = pl.ds(pl.multiple_of(at * rows, 16), rows)
                for i in range(3):
                    act(pltpu.make_async_copy(staged.at[k, i], target.at[i, lines, :], sems.at[3 * k + i]))

    for k, chunk in enumerate(found):
        ends = chunk[full * rows : full * rows + half, :].astype(F32)
        for second in range(2):
            at = second * half
            taken = [chunk[b * rows + at : b * rows + at + half, :].astype(F32) for b in range(full)]
            taken.append(ends[:, left:] if second else ends[:, :left])
            wide = jnp.concatenate(taken, axis=1) * scale
            for i in range(3):
                staged[k, i, at : at + half, :] = wide[:, i * sizes.channels : (i + 1) * sizes.channels]
        each(k, lambda copy: copy.start())
    for k in range(len(found)):
        each(k, lambda copy: copy.wait())


def unpack(sizes, scale, count, found, before=None):
    channels = sizes.channels
    outs = [struct((3, 3 * channels, channels), F32), struct((3, channels, channels), F32)]
    rows = 2 * channels // count
    carried = [] if before is None else list(before)
    return call(
        functools.partial(unpack_body, sizes, scale, count, tuple(found)),
        outs,
        [pltpu.VMEM((len(found), 3, rows, channels), F32), pltpu.SemaphoreType.DMA((3 * len(found),))],
        flops=1000,
        moved=1000,
        spaces=[pltpu.VMEM] * len(found) + [pltpu.HBM] * len(carried),
        out_spaces=[pltpu.HBM] * 2,
        aliases={len(found) + k: k for k in range(len(carried))},
    )(*found.values(), *carried)


def swap(values, axis, bit):
    count = lax.axis_size(axis)
    return lax.ppermute(values, axis, [(i, i ^ bit) for i in range(count)])


def from_all(values, axis):
    return [values] + [swap(values, axis, s) for s in range(1, lax.axis_size(axis))]


def added(terms):
    total = terms[0].astype(F32)
    for term in terms[1:]:
        total = total + term.astype(F32)
    return total


def place_rows(phase, bits, rows):
    place = place_of(lax.axis_index("col"), phase)
    return pl.ds(pl.multiple_of((place ^ bits) * rows, 16), rows)


def split_body(phase, terms, *refs):
    for bits, target in enumerate(refs[terms:]):
        rows = place_rows(phase, bits, target.shape[0])
        target[...] = added([ref[rows, :] for ref in refs[:terms]]).astype(target.dtype)


def scattered(terms, phase):
    count = lax.axis_size(PHASES[phase])
    chunk = (terms[0].shape[0] // count, terms[0].shape[1])
    own, *others = call(
        functools.partial(split_body, phase, len(terms)),
        [struct(chunk, F32)] + [struct(chunk, BF16)] * (count - 1),
        limit=SMALL_LIMIT,
    )(*terms)
    return [own] + [exchange(values, phase, n + 1) for n, values in enumerate(others)]


def gather_body(phase, *refs):
    for bits, part in enumerate(refs[:-1]):
        refs[-1][place_rows(phase, bits, part.shape[0]), :] = part[...]


def gathered(chunk, phase):
    count = lax.axis_size(PHASES[phase])
    parts = [chunk] + [exchange(chunk, phase, n) for n in range(1, count)]
    return call(
        functools.partial(gather_body, phase),
        struct((chunk.shape[0] * count, chunk.shape[1]), chunk.dtype),
        limit=SMALL_LIMIT,
    )(*parts)


def shards(latents, spatial_kernel, temporal_kernel, cotangent):
    _, frames, rows, width = latents.shape
    channels = spatial_kernel.shape[2]
    sizes = Sizes(frames, rows, width // channels, channels)
    cols, seqs = lax.axis_size("col"), lax.axis_size("seq")
    frame_entries = float(rows * sizes.columns * cols * (channels // GROUPS))
    clip_entries = frame_entries * frames * seqs
    pixels = lax.axis_size("dp") * seqs * cols * sizes.pixels * sizes.columns
    grad_scale = 1.0 / math.sqrt(pixels)

    x = latents.reshape(sizes.pixels, width)
    cot = cotangent.reshape(sizes.pixels, width)
    sum_shape = struct((8, sizes.pair), F32)
    frame_shape = struct((2 * frames, sizes.pair), F32)
    padded_scratch = pltpu.VMEM((3, sizes.pixels, sizes.padded), BF16)
    slack = sizes.slack

    before, after = neighbour_frames(cot, sizes)

    sums, edge = call(
        functools.partial(latent_sums_body, sizes),
        [frame_shape, struct((sizes.pixels, sizes.edge), BF16)],
        flops=CONV_COST // 3,
    )(x)
    other = swap(sums, "col", 1)
    rim = swap(edge, "col", 1)
    hidden, act, clip = call(
        functools.partial(forward_body, sizes, frame_entries),
        [struct((sizes.pixels, width), BF16), struct((sizes.pixels, sizes.padded), BF16), sum_shape],
        [padded_scratch] + [pltpu.VMEM((8, 2 * sizes.pair), F32)] * 2 + tile_scratch(sizes),
        flops=CONV_COST,
        limit=CONV_LIMIT,
    )(x, sums, other, rim, spatial_kernel)
    clips = from_all(clip + swap(clip, "col", 1), "seq")
    dact = call(
        functools.partial(activation_grad_body, sizes, min(4, sizes.pairs)),
        struct((sizes.pixels, width), F32),
        [pltpu.VMEM((sizes.edge, 3 * sizes.edge), BF16)] * 2,
        flops=CONV_COST // 3,
    )(cot, before, after, temporal_kernel)
    tact, tgrad, means, rims = call(
        functools.partial(temporal_body, sizes, clip_entries, seqs),
        [
            struct((sizes.pixels, width), BF16),
            struct((sizes.pixels, width), F32),
            sum_shape,
            struct((3 * sizes.pixels, sizes.edge), F32),
        ],
        [pltpu.VMEM((sizes.pixels, width), F32)],
        flops=CONV_COST // 3,
    )(hidden, cot, dact, *clips)
    means = from_all(means + swap(means, "col", 1), "seq")
    rims = swap(rims, "col", 1)
    temporal_grad = call(
        functools.partial(temporal_grad_body, sizes, min(4, sizes.pairs)),
        struct((channels, 3 * channels), F32),
        flops=CONV_COST // 3,
    )(tact, cot, before, after)

    count, after_count = (lax.axis_size(name) for name in PHASES)
    chunk_rows = 4 * channels // (2 * count) * 3 * channels // 128
    chunk = (-(-chunk_rows // (16 * after_count)) * 16 * after_count, 128)
    dtemp, dspat, *chunks = call(
        functools.partial(spatial_grad_body, sizes, clip_entries, seqs),
        [
            struct((sizes.pixels, width), BF16),
            struct((sizes.pixels, sizes.padded), BF16),
        ]
        + [struct(chunk, F32)] * count
        + [struct(chunk, BF16)] * count,
        [
            padded_scratch,
            pltpu.VMEM((4 * channels, 3 * channels), F32),
        ],
        flops=CONV_COST,
    )(hidden, cot, tgrad, rims, act, temporal_grad, *clips, *means)
    chunks = [chunks[n] + swap(chunks[count + n], "col", 1).astype(F32) for n in range(count)]
    sends = [values.astype(BF16) for values in chunks[1:]]
    sends, dspat = lax.optimization_barrier((sends, dspat))
    found = [exchange(values, 0, n + 1) for n, values in enumerate(sends)]
    dnormed, mine = call(
        functools.partial(backward_body, sizes, frame_entries),
        [struct((sizes.pixels, width), F32), frame_shape],
        [padded_scratch, pltpu.VMEM((2 * frames, 8, 2 * sizes.pair), F32)] + tile_scratch_back(sizes),
        flops=CONV_COST,
        limit=CONV_LIMIT,
    )(x, sums, other, dspat, spatial_kernel)
    found, (dnormed, mine) = lax.optimization_barrier((found, (dnormed, mine)))
    theirs = swap(mine, "col", 1)
    terms, theirs = lax.optimization_barrier((scattered(chunks[:1] + found, 1), theirs))
    total = added(terms)
    grad_latents = call(
        functools.partial(finish_body, sizes, frame_entries), struct((sizes.pixels, width), F32),
        flops=CONV_COST // 3,
    )(x, sums, other, cot, dtemp, dnormed, mine, theirs)
    part = gathered(total.astype(BF16), 1)
    near = [exchange(part, 0, 1 << k) for k in range(count.bit_length() - 1)]
    part, near, grad_latents = lax.optimization_barrier((part, near, grad_latents))
    parts = [part] + [None] * (count - 1)
    for n in range(1, count):
        parts[n] = exchange(parts[n & (n - 1)], 0, n & -n) if n & (n - 1) else near[n.bit_length() - 1]
    found = {}
    for n, part in enumerate(parts[:-1]):
        found[True, n], found[False, n] = part, swap(part, "col", 1)
    grads = unpack(sizes, grad_scale, count, found)
    part, grads = lax.optimization_barrier((parts[-1], grads))
    last = {(True, count - 1): part, (False, count - 1): swap(part, "col", 1)}
    spatial_grad, temporal_grad = unpack(sizes, grad_scale, count, last, grads)
    return (
        grad_latents.reshape(latents.shape),
        spatial_grad.reshape(spatial_kernel.shape),
        temporal_grad.reshape(temporal_kernel.shape),
    )


def solution(mesh):
    in_specs = (P("dp", "seq", None, "col"), P(), P(), P("dp", "seq", None, "col"))
    out_specs = (P("dp", "seq", None, "col"), P(), P())
    return jax.shard_map(shards, mesh=mesh, in_specs=in_specs, out_specs=out_specs, check_vma=False)
```
